128 devices in a mesh: rep: 4 (over x), fsdp: 32 (over z, y, core).
Axes of the slice: x: 4, y: 4, z: 4, core: 2. Of those that a mesh axis runs over, the one named last changes fastest.
Arguments:
- grads: bfloat16 [4, 256, 512, 512], P('rep', None, 'fsdp'), may hold values from -2 to 2
- owner_table: int32 [256, 1], replicated, may hold values from 0 to 31; in each aligned block of 64 rows (0 to 63, 64 to 127, ...) at most 3 rows name the same one
- left_stats: float32 [4, 32, 3, 512, 512], P('rep', 'fsdp'), may hold values from -1 to 100, as said below
- right_stats: float32 [4, 32, 3, 512, 512], P('rep', 'fsdp'), may hold values from -1 to 100, as said below
- left_roots: bfloat16 [4, 32, 3, 512, 512], P('rep', 'fsdp'), may hold values from -1 to 6, as said below
- right_roots: bfloat16 [4, 32, 3, 512, 512], P('rep', 'fsdp'), may hold values from -1 to 6, as said below
Outputs:
- preconditioned: bfloat16 [256, 512, 512], P('rep', 'fsdp')
- left_updated: float32 [4, 32, 3, 512, 512], P('rep', 'fsdp')
- right_updated: float32 [4, 32, 3, 512, 512], P('rep', 'fsdp')
- left_root_new: bfloat16 [4, 32, 512, 512], P('rep', 'fsdp')
- right_root_new: bfloat16 [4, 32, 512, 512], P('rep', 'fsdp')
The draws below stay inside these ranges and needn't reach their ends.
Inputs may be any that keep to these rules, and one draw needn't show every extreme that they name: `owner_table`: block b belongs to replica group b // 64. Among the 64 blocks of one group no owner is named more than 3 times, and in some group one owner is named exactly 3 times. `left_stats`: each matrix is symmetric positive definite. `right_stats`: each matrix is symmetric positive definite. `left_roots`: each matrix is symmetric positive definite. `right_roots`: each matrix is symmetric positive definite.
All inputs are finite; a program needn't handle non-finite values.
Results may differ from the reference program's by a relative error of at most 0.015.
Values may be sent and summed in bfloat16 or wider, within the bound.
No kernel may reach another device: no remote copies, remote signals or barrier semaphores. Data moves between devices by JAX's collectives and lax.ppermute only.
A program may use at most 128 MiB of HBM per device.

```python
import math
import jax
import jax.numpy as jnp
import numpy as np
from jax import lax

BLK = 512
ITERS = 2
MOST = 3
QB = 64
NBLK = 256
N_REP = 4
N_FSDP = 32


def dominant_field(key, diag_level, spread_top, full_shape):
    first_key, second_key, third_key = jax.random.split(key, 3)
    side_count = full_shape[-1]
    uneven = jax.random.uniform(first_key, full_shape, jnp.float32, -1.0, 1.0)
    offdiag = uneven
    offdiag = 0.5 * (offdiag + jnp.swapaxes(offdiag, -1, -2))
    diagonal = jax.random.uniform(second_key, full_shape[:-1], jnp.float32, 1.0, 2.0) * side_count
    rows_ids = jnp.arange(side_count)[:, None]
    cols_ids = jnp.arange(side_count)[None, :]
    identity_mat = (rows_ids == cols_ids).astype(jnp.float32)
    core = (offdiag * (1.0 - identity_mat) + identity_mat * diagonal[..., None]) * (diag_level / side_count)
    row_scale = jnp.exp(jax.random.uniform(third_key, full_shape[:-1], jnp.float32, 0.0, math.log(spread_top)))
    return core * row_scale[..., :, None] * row_scale[..., None, :]


def draw_left_stats(key, part):
    key = jax.random.fold_in(key, 11)
    full_shape = (N_REP, N_FSDP, MOST, BLK, BLK)
    return dominant_field(key, 3.0, 3.2, full_shape)


def draw_right_stats(key, part):
    key = jax.random.fold_in(key, 23)
    full_shape = (N_REP, N_FSDP, MOST, BLK, BLK)
    return dominant_field(key, 3.0, 3.2, full_shape)


def draw_left_roots(key, part):
    key = jax.random.fold_in(key, 37)
    full_shape = (N_REP, N_FSDP, MOST, BLK, BLK)
    return dominant_field(key, 0.7, 1.5, full_shape).astype(jnp.bfloat16)


def draw_right_roots(key, part):
    key = jax.random.fold_in(key, 41)
    full_shape = (N_REP, N_FSDP, MOST, BLK, BLK)
    return dominant_field(key, 0.7, 1.5, full_shape).astype(jnp.bfloat16)


def block_levels(own_key, extent, cuts, least, top_value):
    factor_of, own = 1.0, jax.random.fold_in(own_key, 6)
    for dim, shards_of in cuts:
        draws = jnp.exp(jax.random.uniform(jax.random.fold_in(own, dim), (shards_of,), jnp.float32, least / len(cuts), top_value / len(cuts)))
        factor_of = factor_of * jnp.repeat(draws, extent[dim] // shards_of).reshape([-1 if axis == dim else 1 for axis in range(len(extent))])
    return factor_of


def routed_block(own_key, own, number, rows, count, top, reach, lean):
    ranking = jax.random.permutation(own_key, count)
    crowded, usual = load_shares(count, rows * top, reach, lean, True), load_shares(count, rows * top, reach, lean, False)
    places = jnp.arange(count)

    def named(tallies, turn):
        used = int((tallies > 0).sum())
        fixed = max(1, used // 4)
        moved = fixed + (places - fixed + turn * (used - fixed)) % max(1, count - fixed)
        return jnp.zeros((count,), jnp.int32).at[ranking[jnp.where(places < fixed, places, moved)]].set(jnp.asarray(tallies, jnp.int32))

    tallies = jnp.where(number % 4 == 0, named(crowded, number // 4), named(usual, number - number // 4 - 1))
    mixed = jax.random.permutation(jax.random.fold_in(own, 3), count)
    donor, taker = mixed[0:count // 2 * 2:2], mixed[1:count // 2 * 2:2]
    margin = jnp.minimum(tallies[donor] - 1, reach - tallies[taker]) // 2
    margin = jnp.where((donor == ranking[0]) | (taker == ranking[0]) | (tallies[taker] == 0), 0, jnp.maximum(margin, 0))
    moved = jax.random.randint(jax.random.fold_in(own, 4), (count // 2,), 0, 1 << 20) % (margin + 1)
    tallies = tallies.at[donor].add(-moved).at[taker].add(moved)
    members = jnp.searchsorted(jnp.cumsum(tallies), jnp.arange(rows * top), side="right").astype(jnp.int32)
    table = members.reshape(top, rows).T
    table = table[jax.random.permutation(jax.random.fold_in(own, 1), rows)]
    turn = jax.random.randint(jax.random.fold_in(own, 2), (rows, 1), 0, top)
    return jnp.take_along_axis(table, (jnp.arange(top)[None, :] + turn) % top, axis=1)


def load_shares(count, total, most, slope, full):
    loads = [(1 << 20) // math.isqrt(rank ** slope) + 1 for rank in range(1, count + 1)]
    largest = most if full else min(most, max(-(-total // count), total * loads[0] // sum(loads)))
    least = 1 if total - largest >= count - 1 else 0
    given, surplus = [largest] + [least] * (count - 1), total - largest - least * (count - 1)
    while surplus > 0:
        free = [i for i in range(1, count) if given[i] < largest] or [i for i in range(1, count) if given[i] < most]
        pool, remaining = sum([loads[i] for i in free]), surplus
        for i in free:
            addition = min(most - given[i], max(1, remaining * loads[i] // pool), surplus)
            given[i] = given[i] + addition
            surplus = surplus - addition
    return np.array(given)


def centred(rng, extent, deviation, reach, cuts=(), held_as=jnp.bfloat16):
    array = jax.random.normal(rng, extent, jnp.float32) * deviation
    if len(cuts) > 0:
        array = block_levels(rng, extent, cuts, -0.22, 0.18) * array
    return jnp.clip(array, min=-reach, max=reach).astype(held_as)


def setup_inputs(seed: int = 0) -> dict:
    streams_of = jax.random.split(jax.random.key(seed), 7)
    grads = centred(streams_of[0], (N_REP, NBLK, BLK, BLK), 0.125, 2.0, ((0, 4), (2, 32)))
    owner_table_keys = jax.random.split(jax.random.fold_in(streams_of[1], 1), NBLK // QB)
    owner_table_turns = jax.random.permutation(jax.random.fold_in(streams_of[1], 3), NBLK // QB)
    owner_table = jax.vmap(lambda own, number: routed_block(jax.random.fold_in(streams_of[1], 2), own, number, QB, N_FSDP, 1, MOST, 2))(owner_table_keys, owner_table_turns).reshape((NBLK, 1))
    left_stats = draw_left_stats(jax.random.fold_in(streams_of[6], 71), 0)
    right_stats = draw_right_stats(jax.random.fold_in(streams_of[6], 71), 0)
    left_roots = draw_left_roots(jax.random.fold_in(streams_of[6], 71), 0)
    right_roots = draw_right_roots(jax.random.fold_in(streams_of[6], 71), 0)
    return {"grads": grads, "owner_table": owner_table, "left_stats": left_stats, "right_stats": right_stats, "left_roots": left_roots, "right_roots": right_roots}


DECAY_RATE = 0.9
ROOT_RIDGE = 1e-06
GRAFT_EPS = 1e-12
NORM_EPS = 1e-12

def slot_positions(owner_row, most_slots):
    count_rows = owner_row.shape[0]
    order_ids = jnp.arange(count_rows, dtype=jnp.int32)
    same_owner = owner_row[:, None] == owner_row[None, :]
    earlier = order_ids[None, :] < order_ids[:, None]
    slot_rank = lax.optimization_barrier(jnp.sum((same_owner & earlier).astype(jnp.int32), axis=1)).astype(jnp.int32)
    return (owner_row * most_slots + slot_rank).astype(jnp.int32)

def slot_blocks(position, total_slots):
    count_rows = position.shape[0]
    order_ids = jnp.arange(count_rows, dtype=jnp.int32)
    matches = position[None, :] == jnp.arange(total_slots, dtype=jnp.int32)[:, None]
    block_index = lax.optimization_barrier(jnp.sum(jnp.where(matches, order_ids[None, :], 0), axis=1)).astype(jnp.int32)
    occupied = jnp.any(matches, axis=1)
    return (block_index, occupied)

def batch_mul(left_mat, right_mat):
    return jnp.einsum('bij,bjk->bik', left_mat, right_mat, precision=lax.Precision.HIGHEST)

def fourth_root(stacked):
    side_count = stacked.shape[-1]
    identity_mat = jnp.eye(side_count, dtype=jnp.float32)
    frob_norm = side_count * jnp.sqrt(lax.optimization_barrier(jnp.mean(stacked * stacked, axis=(1, 2))) + NORM_EPS)
    scaled = stacked * (2.5 / frob_norm)[:, None, None]
    root_est = jnp.broadcast_to(identity_mat, stacked.shape).astype(jnp.float32)
    for newton_turn in range(ITERS):
        factor = (5.0 * identity_mat - scaled) * 0.25
        square = batch_mul(factor, factor)
        fourth = batch_mul(square, square)
        root_est = batch_mul(root_est, factor)
        scaled = batch_mul(fourth, scaled)
    return root_est

def refresh(blocks, live_slots, left_prev, right_prev, left_given, right_given):
    wide_blocks = blocks.astype(jnp.float32)
    gram_left = jnp.einsum('sij,skj->sik', wide_blocks, wide_blocks, precision=lax.Precision.HIGHEST)
    gram_right = jnp.einsum('sji,sjk->sik', wide_blocks, wide_blocks, precision=lax.Precision.HIGHEST)
    keep_mask = live_slots[:, None, None]
    new_left = jnp.where(keep_mask, DECAY_RATE * left_prev + (1.0 - DECAY_RATE) * gram_left, left_prev)
    new_right = jnp.where(keep_mask, DECAY_RATE * right_prev + (1.0 - DECAY_RATE) * gram_right, right_prev)
    side_count = blocks.shape[-1]
    identity_mat = jnp.eye(side_count, dtype=jnp.float32)
    roots = fourth_root(jnp.stack([new_left[0], new_right[0]]) + ROOT_RIDGE * identity_mat)
    root_pair = roots.astype(jnp.bfloat16)
    left_use = jnp.concatenate([root_pair[0:1], left_given[1:]], axis=0)
    right_use = jnp.concatenate([root_pair[1:2], right_given[1:]], axis=0)
    right_applied = jnp.einsum('sij,sjk->sik', wide_blocks, right_use.astype(jnp.float32), precision=lax.Precision.HIGHEST).astype(jnp.bfloat16)
    raw_out = jnp.einsum('sij,sjk->sik', left_use.astype(jnp.float32), right_applied.astype(jnp.float32), precision=lax.Precision.HIGHEST)
    grad_power = lax.optimization_barrier(jnp.mean(wide_blocks * wide_blocks, axis=(1, 2)))
    out_power = lax.optimization_barrier(jnp.mean(raw_out * raw_out, axis=(1, 2)))
    graft_scale = jnp.sqrt(grad_power) / jnp.sqrt(out_power + GRAFT_EPS)
    slot_out = (raw_out * graft_scale[:, None, None]).astype(jnp.bfloat16)
    return (slot_out, new_left, new_right, root_pair[0], root_pair[1])

def reference(grads, owner_table, left_stats, right_stats, left_roots, right_roots):
    gradient = lax.optimization_barrier(jnp.sum(grads.astype(jnp.float32), axis=0)).astype(jnp.bfloat16)
    quarters = gradient.reshape(N_REP, QB, BLK, BLK)
    owner_rows = owner_table[:, 0].astype(jnp.int32).reshape(N_REP, QB)
    positions = jax.vmap(lambda row_ids: slot_positions(row_ids, MOST))(owner_rows)
    block_index, occupied = jax.vmap(lambda place_ids: slot_blocks(place_ids, N_FSDP * MOST))(positions)
    block_index = block_index.reshape(N_REP, N_FSDP, MOST)
    occupied = occupied.reshape(N_REP, N_FSDP, MOST)

    def per_owner(flat_id):
        group_id = flat_id // N_FSDP
        owner_id = flat_id % N_FSDP
        chosen = block_index[group_id, owner_id]
        live_slots = occupied[group_id, owner_id]
        picked = jnp.take(quarters[group_id], chosen, axis=0)
        blocks = jnp.where(live_slots[:, None, None], picked, jnp.zeros_like(picked))
        return refresh(blocks, live_slots, left_stats[group_id, owner_id], right_stats[group_id, owner_id], left_roots[group_id, owner_id], right_roots[group_id, owner_id])
    slot_out, new_left, new_right, left_new, right_new = lax.map(per_owner, jnp.arange(N_REP * N_FSDP, dtype=jnp.int32))
    slot_out = slot_out.reshape(N_REP, N_FSDP * MOST, BLK, BLK)
    gathered_out = jax.vmap(lambda group_out, place_ids: jnp.take(group_out, place_ids, axis=0))(slot_out, positions)
    preconditioned = gathered_out.reshape(NBLK, BLK, BLK)
    return (preconditioned, new_left.reshape(N_REP, N_FSDP, MOST, BLK, BLK), new_right.reshape(N_REP, N_FSDP, MOST, BLK, BLK), left_new.reshape(N_REP, N_FSDP, BLK, BLK), right_new.reshape(N_REP, N_FSDP, BLK, BLK))
```

```python
import functools

import jax
import jax.numpy as jnp
from jax import lax
from jax.experimental import pallas as pl
from jax.experimental.pallas import tpu as pltpu
from jax.sharding import PartitionSpec as P

DECAY_RATE = 0.9
ROOT_RIDGE = 1e-06
GRAFT_EPS = 1e-12
NORM_EPS = 1e-12
MOST = 3

ROOT_POLY = (
    25.0 / 16.0,
    -5.0 / 16.0 - 3125.0 / 4096.0,
    3125.0 / 4096.0,
    -1250.0 / 4096.0,
    250.0 / 4096.0,
    -25.0 / 4096.0,
    1.0 / 4096.0,
)

VMEM_LIMIT = 40 * 1024 * 1024
VMEM_MOST = 48 * 1024 * 1024
VMEM = pltpu.VMEM
HBM = pltpu.HBM
SMEM = pltpu.SMEM


def mul(left, right, dims=((1,), (0,))):
    return lax.dot_general(left, right, (dims, ((), ())), preferred_element_type=jnp.float32)


def blend(live, prev, gram):
    return jnp.where(live, DECAY_RATE * prev + (1.0 - DECAY_RATE) * gram, prev)


ROWS = 64
COLS = 128


def tiles(side):
    return [
        (slice(row, row + ROWS), slice(col, col + COLS))
        for row in range(0, side, ROWS)
        for col in range(0, side, COLS)
    ]


def plus_diag(tile, rows, cols, value):
    if rows.start // COLS != cols.start // COLS:
        return tile
    row_ids = lax.broadcasted_iota(jnp.int32, tile.shape, 0) + rows.start
    col_ids = lax.broadcasted_iota(jnp.int32, tile.shape, 1) + cols.start
    return tile + jnp.where(row_ids == col_ids, value, 0.0).astype(tile.dtype)


def total(parts):
    return jnp.sum(functools.reduce(lambda x, y: x + y, parts), keepdims=True)


def cost(matmuls, side, nbytes):
    return pl.CostEstimate(flops=matmuls * 2 * side**3, bytes_accessed=nbytes, transcendentals=0)


def place_kernel(place_ref, empty_ref, front_ref, up_ref, back_ref, down_ref, out_ref, sums, zeros, sem):
    half = front_ref.shape[0]
    zeros[...] = jnp.zeros_like(zeros)

    def blank(place, carry):
        @pl.when(empty_ref[place] > 0)
        def _():
            pltpu.make_async_copy(zeros, out_ref.at[place], sem).start()

        return carry

    def put(block):
        pltpu.make_async_copy(sums.at[block], out_ref.at[place_ref[block]], sem).start()

    def add(j, carry):
        sums[j] = (front_ref[j] + up_ref[j].astype(jnp.float32)).astype(jnp.bfloat16)
        put(j)
        sums[half + j] = (back_ref[j] + down_ref[j].astype(jnp.float32)).astype(jnp.bfloat16)
        put(half + j)
        return carry

    lax.fori_loop(0, half, add, 0, unroll=4)
    lax.fori_loop(0, out_ref.shape[0], blank, 0, unroll=4)
    pltpu.make_async_copy(out_ref, out_ref, sem).wait()


def place_blocks(place, empty, front, up, back, down):
    half, rows, cols = front.shape
    scalars = pl.BlockSpec(memory_space=SMEM)
    return pl.pallas_call(
        place_kernel,
        out_shape=jax.ShapeDtypeStruct((empty.shape[0], rows, cols), jnp.bfloat16),
        in_specs=[scalars] * 2 + [pl.BlockSpec(memory_space=VMEM)] * 4,
        out_specs=pl.BlockSpec(memory_space=HBM),
        scratch_shapes=[
            VMEM((2 * half, rows, cols), jnp.bfloat16),
            VMEM((rows, cols), jnp.bfloat16),
            pltpu.SemaphoreType.DMA(()),
        ],
        compiler_params=pltpu.CompilerParams(vmem_limit_bytes=VMEM_LIMIT),
        cost_estimate=cost(0, 0, 8 * half * rows * cols * 2),
        name="place_blocks",
    )(place, empty, front, up, back, down)


def precondition_kernel(
    live_ref, arrived, left_stats, right_stats, left_roots, right_roots, _, out, left_new, right_new,
    done_ref, stats, roots, results, wide, prod, raws, low, square, term, in_sems, out_sems,
):
    side = stats.shape[-1]
    entries = side * side
    f32, bf16 = jnp.float32, jnp.bfloat16
    c0, c1, c2, c3, c4, c5, c6 = ROOT_POLY
    grid = tiles(side)
    fetch = {}

    def get(name, source, target):
        fetch[name] = pltpu.make_async_copy(source, target, in_sems.at[len(fetch)])
        fetch[name].start()

    for slot in range(1, MOST):
        get("r%d" % slot, right_roots.at[0, 0, slot], roots.at[2 * slot - 1])
        get("l%d" % slot, left_roots.at[0, 0, slot], roots.at[2 * slot - 2])
    get("left", left_stats.at[0, 0, 0], stats.at[0])
    get("right", right_stats.at[0, 0, 0], stats.at[1])

    def block_of(slot):
        return arrived[:, slot].reshape(side, side)

    def give(number, target):
        copy = pltpu.make_async_copy(results.at[number], target, out_sems.at[number])
        copy.start()
        return copy

    def put(number, rows, cols, tile):
        slabs = slice(rows.start // 16, rows.stop // 16)
        results[number, slabs, :, cols] = tile.reshape(ROWS // 16, 16, COLS)

    def power(tile_of):
        return total([jnp.square(tile_of(rows, cols)) for rows, cols in grid]) * (1.0 / entries)

    def graft(slot, block, raw):
        grad_power = power(lambda rows, cols: block[rows, cols].astype(f32))
        scale = jnp.sqrt(grad_power) / jnp.sqrt(power(lambda rows, cols: raw[rows, cols]) + GRAFT_EPS)
        for rows, cols in grid:
            put(slot, rows, cols, (raw[rows, cols] * scale).astype(bf16))

    block = block_of(0)
    others = [block_of(slot) for slot in range(1, MOST)]
    wide[0] = mul(block, block, ((1,), (1,)))
    wide[1] = mul(block, block, ((0,), (0,)))
    for i in range(MOST - 1):
        fetch["r%d" % (i + 1)].wait()
        raws[i] = mul(others[i], roots[2 * i + 1])
    for i in range(MOST - 1):
        for rows, cols in grid:
            square[i, rows, cols] = raws[i, rows, cols].astype(bf16)
        fetch["l%d" % (i + 1)].wait()
        raws[i] = mul(roots[2 * i], square[i])
    sent = []
    live = live_ref[0] > 0
    keep = jnp.where(live, DECAY_RATE, 1.0)
    take = jnp.where(live, 1.0 - DECAY_RATE, 0.0)
    scales = []
    for i, name in enumerate(("left", "right")):
        fetch[name].wait()
        squares = []
        for rows, cols in grid:
            tile = keep * stats[i, rows, cols] + take * wide[i, rows, cols]
            tile = plus_diag(tile, rows, cols, ROOT_RIDGE)
            low[i, rows, cols] = tile.astype(bf16)
            squares.append(tile * tile)
        frob = side * jnp.sqrt(total(squares) * (1.0 / entries) + NORM_EPS)
        scales.append(2.5 / frob)
        prod[i] = mul(low[i], low[i])
        graft(i + 1, others[i], raws.at[i])
        sent.append(give(i + 1, out.at[:, i + 1]))
    for i in range(2):
        one, two = scales[i], scales[i] * scales[i]
        for rows, cols in grid:
            tile = prod[i, rows, cols].astype(bf16)
            square[i, rows, cols] = tile
            tile = (c5 * one).astype(bf16) * low[i, rows, cols] + (c6 * two).astype(bf16) * tile
            term[i, rows, cols] = plus_diag(tile, rows, cols, c4)
        prod[i] = mul(square[i], term[i])
    for i in range(2):
        one, two = scales[i], scales[i] * scales[i]
        for rows, cols in grid:
            tile = (two * prod[i, rows, cols]).astype(bf16) + (c3 * one).astype(bf16) * low[i, rows, cols]
            term[i, rows, cols] = plus_diag(tile, rows, cols, c2)
        prod[i] = mul(square[i], term[i])
    for i in (1, 0):
        one, two = scales[i], scales[i] * scales[i]
        for rows, cols in grid:
            tile = two * prod[i, rows, cols] + (c1 * one) * low[i, rows, cols].astype(f32)
            tile = plus_diag(tile, rows, cols, c0).astype(bf16)
            term[i, rows, cols] = tile
            put(MOST + i, rows, cols, tile)
    sent += [give(MOST, left_new), give(MOST + 1, right_new)]
    prod[0] = mul(block, term[1])
    for rows, cols in grid:
        low[0, rows, cols] = prod[0, rows, cols].astype(bf16)
    prod[1] = mul(term[0], low[0])
    graft(0, block, prod.at[1])
    sent.append(give(0, out.at[:, 0]))
    for copy in sent:
        copy.wait()
    done_ref[0] = 0


def precondition(live, arrived, left_stats, right_stats, left_roots, right_roots, spent):
    owners, _, rows, side = arrived.shape
    root = jax.ShapeDtypeStruct((owners, rows, side), jnp.bfloat16)
    far = pl.BlockSpec(memory_space=HBM)
    return pl.pallas_call(
        precondition_kernel,
        out_shape=[
            jax.ShapeDtypeStruct((owners, MOST, rows, side), jnp.bfloat16), root, root, token_shape(),
        ],
        in_specs=[pl.BlockSpec(memory_space=SMEM), pl.BlockSpec(memory_space=VMEM)] + [far] * 5,
        out_specs=[far] * 3 + [pl.BlockSpec(memory_space=SMEM)],
        scratch_shapes=[
            VMEM((2, side, side), jnp.float32),
            VMEM((2 * MOST - 2, side, side), jnp.bfloat16),
            VMEM((MOST + 2, owners, rows, side), jnp.bfloat16),
            VMEM((2, side, side), jnp.float32),
            VMEM((2, side, side), jnp.float32),
            VMEM((2, side, side), jnp.float32),
            VMEM((2, side, side), jnp.bfloat16),
            VMEM((2, side, side), jnp.bfloat16),
            VMEM((2, side, side), jnp.bfloat16),
            pltpu.SemaphoreType.DMA((2 * MOST,)),
            pltpu.SemaphoreType.DMA((MOST + 2,)),
        ],
        compiler_params=pltpu.CompilerParams(vmem_limit_bytes=VMEM_MOST),
        cost_estimate=cost(14, side, 9 * side * side * 4),
        input_output_aliases={6: 0},
        name="precondition",
    )(live, arrived, left_stats, right_stats, left_roots, right_roots, spent)


def stats_kernel(live_ref, block_ref, lprev_ref, rprev_ref, _, left_ref, right_ref):
    side = lprev_ref.shape[-1]
    block = block_ref[:, 0].reshape(side, side)
    live = live_ref[pl.program_id(0)] > 0
    left_ref[0, 0, 0] = blend(live, lprev_ref[0, 0, 0], mul(block, block, ((1,), (1,))))
    right_ref[0, 0, 0] = blend(live, rprev_ref[0, 0, 0], mul(block, block, ((0,), (0,))))


def update_stats(live, arrived, left_stats, right_stats, tied):
    owners, _, rows, side = arrived.shape
    at_slot = pl.BlockSpec((1, 1, 1, side, side), lambda s: (0, 0, s, 0, 0))
    shape = jax.ShapeDtypeStruct(left_stats.shape, jnp.float32)
    return pl.pallas_call(
        stats_kernel,
        grid=(MOST,),
        out_shape=[shape, shape],
        in_specs=[pl.BlockSpec(memory_space=SMEM)]
        + [pl.BlockSpec((owners, 1, rows, side), lambda s: (0, s, 0, 0))]
        + [at_slot, at_slot, pl.BlockSpec(memory_space=SMEM)],
        out_specs=[at_slot, at_slot],
        compiler_params=pltpu.CompilerParams(vmem_limit_bytes=VMEM_MOST),
        cost_estimate=cost(2 * MOST, side, 13 * side * side * 4),
        name="update_stats",
    )(live, arrived, left_stats, right_stats, tied)


def assemble_kernel(slot_ref, owner_ref, back_ref, out_ref, sem):
    count = out_ref.shape[0]

    def start(b, carry):
        pltpu.make_async_copy(back_ref.at[owner_ref[b], slot_ref[b]], out_ref.at[b], sem).start()
        return carry

    lax.fori_loop(0, count, start, 0, unroll=8)
    pltpu.make_async_copy(out_ref, out_ref, sem).wait()


def assemble(slot_of, owner_of, back):
    count = slot_of.shape[0]
    rows, cols = back.shape[2:]
    return pl.pallas_call(
        assemble_kernel,
        out_shape=jax.ShapeDtypeStruct((count, rows, cols), jnp.bfloat16),
        in_specs=[pl.BlockSpec(memory_space=SMEM)] * 2 + [pl.BlockSpec(memory_space=pl.ANY)],
        out_specs=pl.BlockSpec(memory_space=HBM),
        scratch_shapes=[pltpu.SemaphoreType.DMA(())],
        compiler_params=pltpu.CompilerParams(vmem_limit_bytes=VMEM_LIMIT),
        cost_estimate=cost(0, 0, 2 * count * rows * cols * 2),
        name="assemble",
    )(slot_of, owner_of, back)


def token_shape():
    return jax.ShapeDtypeStruct((1,), jnp.int32)


def routing(owner, owners):
    ids = jnp.arange(owner.shape[0], dtype=jnp.int32)
    same = owner[:, None] == owner[None, :]
    slot = jnp.sum((same & (ids[None, :] < ids[:, None])).astype(jnp.int32), axis=1)
    place = owner * MOST + slot
    taken = place[None, :] == jnp.arange(owners * MOST, dtype=jnp.int32)[:, None]
    return slot, place, 1 - jnp.sum(taken.astype(jnp.int32), axis=1)


def on_device(grads, owner_table, left_stats, right_stats, left_roots, right_roots):
    groups = lax.axis_size("rep")
    owners = lax.axis_size("fsdp")
    group_id = lax.axis_index("rep")
    owner_id = lax.axis_index("fsdp")
    local = grads[0]
    total_blocks, slab_rows, side = local.shape
    share = total_blocks // groups
    half = share // 2
    up = [(i, (i + 1) % groups) for i in range(groups)]
    down = [(i, (i - 1) % groups) for i in range(groups)]

    owner = lax.dynamic_slice_in_dim(owner_table[:, 0], group_id * share, share)
    slot, place, empty = routing(owner, owners)
    own_count = jnp.sum((owner == owner_id).astype(jnp.int32))
    live = (jnp.arange(MOST, dtype=jnp.int32) < own_count).astype(jnp.int32)

    def part(source, ahead, low):
        start = (group_id + ahead) % groups * share + low
        return lax.dynamic_slice_in_dim(source, start, half, 0)

    send_up1, send_down1 = part(local, 2, 0), part(local, 2, half)
    up1 = lax.ppermute(send_up1, "rep", up)
    down1 = lax.ppermute(send_down1, "rep", down)
    later, _, _ = lax.optimization_barrier((local, send_up1, send_down1))
    up2 = lax.ppermute(part(later, 1, half), "rep", up)
    down2 = lax.ppermute(part(later, 3, 0), "rep", down)
    up3 = lax.ppermute(part(local, 1, 0) + up1, "rep", up)
    down3 = lax.ppermute(part(local, 3, half) + down1, "rep", down)
    front = part(local, 0, 0).astype(jnp.float32) + down2.astype(jnp.float32)
    back = part(local, 0, half).astype(jnp.float32) + up2.astype(jnp.float32)

    outgoing = place_blocks(place, empty, front, up3, back, down3)
    outgoing = outgoing.reshape(owners, MOST, slab_rows, side)
    arrived = lax.all_to_all(outgoing, "fsdp", split_axis=0, concat_axis=0, tiled=True)
    results, left_new, right_new, done = precondition(
        live, arrived, left_stats, right_stats, left_roots, right_roots, outgoing
    )
    returned = lax.all_to_all(results, "fsdp", split_axis=0, concat_axis=0, tiled=True)
    left_out, right_out = update_stats(live, arrived, left_stats, right_stats, done)
    preconditioned = assemble(slot, owner, returned)
    return (
        preconditioned,
        left_out,
        right_out,
        left_new.reshape(1, 1, side, side),
        right_new.reshape(1, 1, side, side),
    )


def solution(mesh):
    in_specs = (
        P("rep", None, "fsdp", None),
        P(),
        P("rep", "fsdp", None, None, None),
        P("rep", "fsdp", None, None, None),
        P("rep", "fsdp", None, None, None),
        P("rep", "fsdp", None, None, None),
    )
    out_specs = (
        P("rep", "fsdp", None),
        P("rep", "fsdp", None, None, None),
        P("rep", "fsdp", None, None, None),
        P("rep", "fsdp", None, None),
        P("rep", "fsdp", None, None),
    )
    return jax.shard_map(
        on_device, mesh=mesh, in_specs=in_specs, out_specs=out_specs, check_vma=False
    )
```

```python
import functools

import jax
import jax.numpy as jnp
from jax import lax
from jax.experimental import pallas as pl
from jax.experimental.pallas import tpu as pltpu
from jax.sharding import PartitionSpec as P

DECAY_RATE = 0.9
ROOT_RIDGE = 1e-06
GRAFT_EPS = 1e-12
NORM_EPS = 1e-12
MOST = 3

ROOT_POLY = (
    25.0 / 16.0,
    -5.0 / 16.0 - 3125.0 / 4096.0,
    3125.0 / 4096.0,
    -1250.0 / 4096.0,
    250.0 / 4096.0,
    -25.0 / 4096.0,
    1.0 / 4096.0,
)

VMEM_LIMIT = 40 * 1024 * 1024
VMEM_MOST = 52 * 1024 * 1024
VMEM_SMALL = 16 * 1024 * 1024
VMEM = pltpu.VMEM
HBM = pltpu.HBM
SMEM = pltpu.SMEM


def mul(left, right, dims=((1,), (0,))):
    return lax.dot_general(left, right, (dims, ((), ())), preferred_element_type=jnp.float32)


def blend(live, prev, gram):
    return jnp.where(live, DECAY_RATE * prev + (1.0 - DECAY_RATE) * gram, prev)


ROWS = 64
COLS = 128


def tiles(side):
    return [
        (slice(row, row + ROWS), slice(col, col + COLS))
        for row in range(0, side, ROWS)
        for col in range(0, side, COLS)
    ]


def plus_diag(tile, rows, cols, value):
    if rows.start // COLS != cols.start // COLS:
        return tile
    row_ids = lax.broadcasted_iota(jnp.int32, tile.shape, 0) + rows.start
    col_ids = lax.broadcasted_iota(jnp.int32, tile.shape, 1) + cols.start
    return tile + jnp.where(row_ids == col_ids, value, 0.0).astype(tile.dtype)


def total(parts):
    return jnp.sum(functools.reduce(lambda x, y: x + y, parts), keepdims=True)


def cost(matmuls, side, nbytes):
    return pl.CostEstimate(flops=matmuls * 2 * side**3, bytes_accessed=nbytes, transcendentals=0)


def place_kernel(after, place_ref, empty_ref, front_ref, up_ref, back_ref, down_ref, *rest):
    out_ref, sums, zeros, sem = rest[after], *rest[-3:]
    half = front_ref.shape[0]
    zeros[...] = jnp.zeros_like(zeros)

    def blank(place, carry):
        @pl.when(empty_ref[place] > 0)
        def _():
            pltpu.make_async_copy(zeros, out_ref.at[place], sem).start()

        return carry

    def put(block):
        pltpu.make_async_copy(sums.at[block], out_ref.at[place_ref[block]], sem).start()

    def add(j, carry):
        sums[j] = (front_ref[j] + up_ref[j].astype(jnp.float32)).astype(jnp.bfloat16)
        put(j)
        sums[half + j] = (back_ref[j] + down_ref[j].astype(jnp.float32)).astype(jnp.bfloat16)
        put(half + j)
        return carry

    lax.fori_loop(0, half, add, 0, unroll=4)
    lax.fori_loop(0, out_ref.shape[0], blank, 0, unroll=4)
    pltpu.make_async_copy(out_ref, out_ref, sem).wait()


def place_blocks(place, empty, front, up, back, down, *after, room=None):
    half, rows, cols = front.shape
    scalars = pl.BlockSpec(memory_space=SMEM)
    return pl.pallas_call(
        functools.partial(place_kernel, len(after)),
        out_shape=[
            jax.ShapeDtypeStruct((empty.shape[0], rows, cols), jnp.bfloat16),
            *([jax.ShapeDtypeStruct(room, jnp.bfloat16)] if room else []),
        ],
        in_specs=[scalars] * 2
        + [pl.BlockSpec(memory_space=VMEM)] * 4
        + [pl.BlockSpec(memory_space=pl.ANY)] * len(after),
        out_specs=[pl.BlockSpec(memory_space=HBM)] * (2 if room else 1),
        scratch_shapes=[
            VMEM((2 * half, rows, cols), jnp.bfloat16),
            VMEM((rows, cols), jnp.bfloat16),
            pltpu.SemaphoreType.DMA(()),
        ],
        compiler_params=pltpu.CompilerParams(vmem_limit_bytes=VMEM_LIMIT),
        cost_estimate=cost(0, 0, 8 * half * rows * cols * 2),
        name="place_blocks",
    )(place, empty, front, up, back, down, *after)


def add_kernel(one_ref, two_ref, three_ref, four_ref, *rest):
    first_ref, second_ref = rest[-2:]

    def add(j, carry):
        first_ref[j] = one_ref[j] + two_ref[j]
        second_ref[j] = three_ref[j] + four_ref[j]
        return carry

    lax.fori_loop(0, first_ref.shape[0], add, 0, unroll=8)


def add_pairs(one, two, three, four, *after):
    near = pl.BlockSpec(memory_space=VMEM)
    shape = jax.ShapeDtypeStruct(one.shape, one.dtype)
    return pl.pallas_call(
        add_kernel,
        out_shape=[shape, shape],
        in_specs=[near] * 4 + [pl.BlockSpec(memory_space=pl.ANY)] * len(after),
        out_specs=[near, near],
        compiler_params=pltpu.CompilerParams(vmem_limit_bytes=VMEM_SMALL),
        cost_estimate=cost(800, 512, 2 * one.size),
        name="add_pairs",
    )(one, two, three, four, *after)


def precondition_kernel(
    live_ref, arrived_a, arrived_b, left_stats, right_stats, left_roots, right_roots, _, out, left_new, right_new,
    done_ref, stats, roots, results, wide, prod, raws, low, square, term, in_sems, out_sems,
):
    side = stats.shape[-1]
    entries = side * side
    f32, bf16 = jnp.float32, jnp.bfloat16
    c0, c1, c2, c3, c4, c5, c6 = ROOT_POLY
    grid = tiles(side)
    fetch = {}

    def get(name, source, target):
        fetch[name] = pltpu.make_async_copy(source, target, in_sems.at[len(fetch)])
        fetch[name].start()

    for slot in range(1, MOST):
        get("r%d" % slot, right_roots.at[0, 0, slot], roots.at[2 * slot - 1])
        get("l%d" % slot, left_roots.at[0, 0, slot], roots.at[2 * slot - 2])
    get("left", left_stats.at[0, 0, 0], stats.at[0])
    get("right", right_stats.at[0, 0, 0], stats.at[1])

    def block_of(slot):
        halves = [half[:, slot].reshape(side, side // 2) for half in (arrived_a, arrived_b)]
        return jnp.concatenate(halves, axis=1)

    def give(number, target):
        copy = pltpu.make_async_copy(results.at[number], target, out_sems.at[number])
        copy.start()
        return copy

    def put(number, rows, cols, tile):
        slabs = slice(rows.start // 16, rows.stop // 16)
        results[number, slabs, :, cols] = tile.reshape(ROWS // 16, 16, COLS)

    def power(tile_of):
        return total([jnp.square(tile_of(rows, cols)) for rows, cols in grid]) * (1.0 / entries)

    def graft(slot, block, raw):
        grad_power = power(lambda rows, cols: block[rows, cols].astype(f32))
        scale = jnp.sqrt(grad_power) / jnp.sqrt(power(lambda rows, cols: raw[rows, cols]) + GRAFT_EPS)
        for rows, cols in grid:
            put(slot, rows, cols, (raw[rows, cols] * scale).astype(bf16))

    block = block_of(0)
    others = [block_of(slot) for slot in range(1, MOST)]
    wide[0] = mul(block, block, ((1,), (1,)))
    wide[1] = mul(block, block, ((0,), (0,)))
    for i in range(MOST - 1):
        fetch["r%d" % (i + 1)].wait()
        raws[i] = mul(others[i], roots[2 * i + 1])
    for i in range(MOST - 1):
        for rows, cols in grid:
            square[i, rows, cols] = raws[i, rows, cols].astype(bf16)
        fetch["l%d" % (i + 1)].wait()
        raws[i] = mul(roots[2 * i], square[i])
    sent = []
    live = live_ref[0] > 0
    keep = jnp.where(live, DECAY_RATE, 1.0)
    take = jnp.where(live, 1.0 - DECAY_RATE, 0.0)
    scales = []
    for i, name in enumerate(("left", "right")):
        fetch[name].wait()
        squares = []
        for rows, cols in grid:
            tile = keep * stats[i, rows, cols] + take * wide[i, rows, cols]
            tile = plus_diag(tile, rows, cols, ROOT_RIDGE)
            low[i, rows, cols] = tile.astype(bf16)
            squares.append(tile * tile)
        frob = side * jnp.sqrt(total(squares) * (1.0 / entries) + NORM_EPS)
        scales.append(2.5 / frob)
        prod[i] = mul(low[i], low[i])
        graft(i + 1, others[i], raws.at[i])
        sent.append(give(i + 1, out.at[:, i + 1]))
    for i in range(2):
        one, two = scales[i], scales[i] * scales[i]
        for rows, cols in grid:
            tile = prod[i, rows, cols].astype(bf16)
            square[i, rows, cols] = tile
            tile = (c5 * one).astype(bf16) * low[i, rows, cols] + (c6 * two).astype(bf16) * tile
            term[i, rows, cols] = plus_diag(tile, rows, cols, c4)
        prod[i] = mul(square[i], term[i])
    for i in range(2):
        one, two = scales[i], scales[i] * scales[i]
        for rows, cols in grid:
            tile = (two * prod[i, rows, cols]).astype(bf16) + (c3 * one).astype(bf16) * low[i, rows, cols]
            term[i, rows, cols] = plus_diag(tile, rows, cols, c2)
        prod[i] = mul(square[i], term[i])
    for i in (1, 0):
        one, two = scales[i], scales[i] * scales[i]
        for rows, cols in grid:
            tile = two * prod[i, rows, cols] + (c1 * one) * low[i, rows, cols].astype(f32)
            tile = plus_diag(tile, rows, cols, c0).astype(bf16)
            term[i, rows, cols] = tile
            put(MOST + i, rows, cols, tile)
    sent += [give(MOST, left_new), give(MOST + 1, right_new)]
    prod[0] = mul(block, term[1])
    for rows, cols in grid:
        low[0, rows, cols] = prod[0, rows, cols].astype(bf16)
    prod[1] = mul(term[0], low[0])
    graft(0, block, prod.at[1])
    sent.append(give(0, out.at[:, 0]))
    for copy in sent:
        copy.wait()
    done_ref[0] = 0


def precondition(live, arrived, left_stats, right_stats, left_roots, right_roots, spent):
    owners, _, rows, width = arrived[0].shape
    side = left_stats.shape[-1]
    root = jax.ShapeDtypeStruct((owners, rows, side), jnp.bfloat16)
    far = pl.BlockSpec(memory_space=HBM)
    return pl.pallas_call(
        precondition_kernel,
        out_shape=[
            jax.ShapeDtypeStruct((owners, MOST, rows, side), jnp.bfloat16), root, root, token_shape(),
        ],
        in_specs=[pl.BlockSpec(memory_space=SMEM)] + [pl.BlockSpec(memory_space=VMEM)] * 2 + [far] * 5,
        out_specs=[far] * 3 + [pl.BlockSpec(memory_space=SMEM)],
        scratch_shapes=[
            VMEM((2, side, side), jnp.float32),
            VMEM((2 * MOST - 2, side, side), jnp.bfloat16),
            VMEM((MOST + 2, owners, rows, side), jnp.bfloat16),
            VMEM((2, side, side), jnp.float32),
            VMEM((2, side, side), jnp.float32),
            VMEM((2, side, side), jnp.float32),
            VMEM((2, side, side), jnp.bfloat16),
            VMEM((2, side, side), jnp.bfloat16),
            VMEM((2, side, side), jnp.bfloat16),
            pltpu.SemaphoreType.DMA((2 * MOST,)),
            pltpu.SemaphoreType.DMA((MOST + 2,)),
        ],
        compiler_params=pltpu.CompilerParams(vmem_limit_bytes=VMEM_MOST),
        cost_estimate=cost(14, side, 9 * side * side * 4),
        input_output_aliases={7: 0},
        name="precondition",
    )(live, *arrived, left_stats, right_stats, left_roots, right_roots, spent)


def stats_kernel(live_ref, front_ref, back_ref, lprev_ref, rprev_ref, _, left_ref, right_ref):
    side = lprev_ref.shape[-1]
    block = jnp.concatenate([front_ref[:, 0], back_ref[:, 0]], axis=-1).reshape(side, side)
    live = live_ref[pl.program_id(0)] > 0
    left_ref[0, 0, 0] = blend(live, lprev_ref[0, 0, 0], mul(block, block, ((1,), (1,))))
    right_ref[0, 0, 0] = blend(live, rprev_ref[0, 0, 0], mul(block, block, ((0,), (0,))))


def update_stats(live, arrived, left_stats, right_stats, tied):
    owners, _, rows, width = arrived[0].shape
    side = left_stats.shape[-1]
    at_slot = pl.BlockSpec((1, 1, 1, side, side), lambda s: (0, 0, s, 0, 0))
    shape = jax.ShapeDtypeStruct(left_stats.shape, jnp.float32)
    return pl.pallas_call(
        stats_kernel,
        grid=(MOST,),
        out_shape=[shape, shape],
        in_specs=[pl.BlockSpec(memory_space=SMEM)]
        + [pl.BlockSpec((owners, 1, rows, width), lambda s: (0, s, 0, 0))] * 2
        + [at_slot, at_slot, pl.BlockSpec(memory_space=SMEM)],
        out_specs=[at_slot, at_slot],
        compiler_params=pltpu.CompilerParams(vmem_limit_bytes=VMEM_MOST),
        cost_estimate=cost(2 * MOST, side, 13 * side * side * 4),
        name="update_stats",
    )(live, *arrived, left_stats, right_stats, tied)


def assemble_kernel(slot_ref, owner_ref, back_ref, out_ref, sem):
    count = out_ref.shape[0]

    def start(b, carry):
        pltpu.make_async_copy(back_ref.at[owner_ref[b], slot_ref[b]], out_ref.at[b], sem).start()
        return carry

    lax.fori_loop(0, count, start, 0, unroll=8)
    pltpu.make_async_copy(out_ref, out_ref, sem).wait()


def assemble(slot_of, owner_of, back):
    count = slot_of.shape[0]
    rows, cols = back.shape[2:]
    return pl.pallas_call(
        assemble_kernel,
        out_shape=jax.ShapeDtypeStruct((count, rows, cols), jnp.bfloat16),
        in_specs=[pl.BlockSpec(memory_space=SMEM)] * 2 + [pl.BlockSpec(memory_space=pl.ANY)],
        out_specs=pl.BlockSpec(memory_space=HBM),
        scratch_shapes=[pltpu.SemaphoreType.DMA(())],
        compiler_params=pltpu.CompilerParams(vmem_limit_bytes=VMEM_LIMIT),
        cost_estimate=cost(0, 0, 2 * count * rows * cols * 2),
        name="assemble",
    )(slot_of, owner_of, back)


def token_shape():
    return jax.ShapeDtypeStruct((1,), jnp.int32)


def routing(owner, owners):
    ids = jnp.arange(owner.shape[0], dtype=jnp.int32)
    same = owner[:, None] == owner[None, :]
    slot = jnp.sum((same & (ids[None, :] < ids[:, None])).astype(jnp.int32), axis=1)
    place = owner * MOST + slot
    taken = place[None, :] == jnp.arange(owners * MOST, dtype=jnp.int32)[:, None]
    return slot, place, 1 - jnp.sum(taken.astype(jnp.int32), axis=1)


def on_device(grads, owner_table, left_stats, right_stats, left_roots, right_roots):
    groups = lax.axis_size("rep")
    owners = lax.axis_size("fsdp")
    group_id = lax.axis_index("rep")
    owner_id = lax.axis_index("fsdp")
    local = grads[0]
    total_blocks, slab_rows, side = local.shape
    share = total_blocks // groups
    half = share // 2
    up = [(i, (i + 1) % groups) for i in range(groups)]
    down = [(i, (i - 1) % groups) for i in range(groups)]

    owner = lax.dynamic_slice_in_dim(owner_table[:, 0], group_id * share, share)
    slot, place, empty = routing(owner, owners)
    own_count = jnp.sum((owner == owner_id).astype(jnp.int32))
    live = (jnp.arange(MOST, dtype=jnp.int32) < own_count).astype(jnp.int32)

    width = side // 2

    def part(source, ahead, low, column):
        start = (group_id + ahead) % groups * share + low
        return lax.dynamic_slice(source, (start, 0, column), (half, slab_rows, width))

    def send(pair):
        return lax.ppermute(pair[0], "rep", up), lax.ppermute(pair[1], "rep", down)

    def firsts(source, column):
        return part(source, 2, 0, column), part(source, 2, half, column)

    def seconds(source, column):
        return part(source, 1, half, column), part(source, 3, 0, column)

    def mids(source, column):
        return part(source, 1, 0, column), part(source, 3, half, column)

    def own_sums(source, column, up2, down2):
        front = part(source, 0, 0, column).astype(jnp.float32) + down2.astype(jnp.float32)
        return front, part(source, 0, half, column).astype(jnp.float32) + up2.astype(jnp.float32)

    first = firsts(local, 0)
    up1, down1 = send(first)
    later, _ = lax.optimization_barrier((local, first))
    second = seconds(later, 0)
    up2, down2 = send(second)
    later, _ = lax.optimization_barrier((later, second))
    mid = mids(later, 0)
    third = mid[0] + up1, mid[1] + down1
    up3, down3 = send(third)
    later, _ = lax.optimization_barrier((later, third))
    firsts_b, seconds_b = firsts(later, width), seconds(later, width)
    sums = own_sums(local, 0, up2, down2)
    up1, down1 = send(firsts_b)
    up2, down2 = send(seconds_b)
    (outgoing_a,) = place_blocks(place, empty, sums[0], up3, sums[1], down3, *firsts_b, *seconds_b)
    mid = mids(later, width)
    third = add_pairs(mid[0], up1, mid[1], down1, outgoing_a)
    up3, down3 = send(third)
    later, _ = lax.optimization_barrier((later, third))
    sums = own_sums(later, width, up2, down2)
    outgoing_b, spent = place_blocks(
        place, empty, sums[0], up3, sums[1], down3, room=(owners, MOST, slab_rows, side)
    )
    arrived = [
        lax.all_to_all(
            outgoing.reshape(owners, MOST, slab_rows, width), "fsdp", split_axis=0, concat_axis=0, tiled=True
        )
        for outgoing in (outgoing_a, outgoing_b)
    ]
    results, left_new, right_new, done = precondition(
        live, arrived, left_stats, right_stats, left_roots, right_roots, spent
    )
    returned = lax.all_to_all(results, "fsdp", split_axis=0, concat_axis=0, tiled=True)
    left_out, right_out = update_stats(live, arrived, left_stats, right_stats, done)
    preconditioned = assemble(slot, owner, returned)
    return (
        preconditioned,
        left_out,
        right_out,
        left_new.reshape(1, 1, side, side),
        right_new.reshape(1, 1, side, side),
    )


def solution(mesh):
    in_specs = (
        P("rep", None, "fsdp", None),
        P(),
        P("rep", "fsdp", None, None, None),
        P("rep", "fsdp", None, None, None),
        P("rep", "fsdp", None, None, None),
        P("rep", "fsdp", None, None, None),
    )
    out_specs = (
        P("rep", "fsdp", None),
        P("rep", "fsdp", None, None, None),
        P("rep", "fsdp", None, None, None),
        P("rep", "fsdp", None, None),
        P("rep", "fsdp", None, None),
    )
    return jax.shard_map(
        on_device, mesh=mesh, in_specs=in_specs, out_specs=out_specs, check_vma=False
    )
```

```python
import functools

import jax
import jax.numpy as jnp
from jax import lax
from jax.experimental import pallas as pl
from jax.experimental.pallas import tpu as pltpu
from jax.sharding import PartitionSpec as P

DECAY_RATE = 0.9
ROOT_RIDGE = 1e-06
GRAFT_EPS = 1e-12
NORM_EPS = 1e-12
MOST = 3

ROOT_POLY = (
    25.0 / 16.0,
    -5.0 / 16.0 - 3125.0 / 4096.0,
    3125.0 / 4096.0,
    -1250.0 / 4096.0,
    250.0 / 4096.0,
    -25.0 / 4096.0,
    1.0 / 4096.0,
)

VMEM_LIMIT = 40 * 1024 * 1024
VMEM_MOST = 52 * 1024 * 1024
VMEM_ALL = 60 * 1024 * 1024
VMEM_SMALL = 16 * 1024 * 1024
VMEM = pltpu.VMEM
HBM = pltpu.HBM
SMEM = pltpu.SMEM


def mul(left, right, dims=((1,), (0,))):
    return lax.dot_general(left, right, (dims, ((), ())), preferred_element_type=jnp.float32)


def blend(live, prev, gram):
    return jnp.where(live, DECAY_RATE * prev + (1.0 - DECAY_RATE) * gram, prev)


ROWS = 64
COLS = 128
PARTS = 4


def tiles(side):
    return [
        (slice(row, row + ROWS), slice(col, col + COLS))
        for row in range(0, side, ROWS)
        for col in range(0, side, COLS)
    ]


def plus_diag(tile, rows, cols, value):
    if rows.start // COLS != cols.start // COLS:
        return tile
    row_ids = lax.broadcasted_iota(jnp.int32, tile.shape, 0) + rows.start
    col_ids = lax.broadcasted_iota(jnp.int32, tile.shape, 1) + cols.start
    return tile + jnp.where(row_ids == col_ids, value, 0.0).astype(tile.dtype)


def total(parts):
    return jnp.sum(functools.reduce(lambda x, y: x + y, parts), keepdims=True)


def cost(matmuls, side, nbytes):
    return pl.CostEstimate(flops=matmuls * 2 * side**3, bytes_accessed=nbytes, transcendentals=0)


def spare_kernel(_, room_ref, done_ref):
    done_ref[0] = 0


def spare_room(after, shape):
    scalars = pl.BlockSpec(memory_space=SMEM)
    return pl.pallas_call(
        spare_kernel,
        out_shape=[jax.ShapeDtypeStruct(shape, jnp.bfloat16), token_shape()],
        in_specs=[scalars],
        out_specs=[pl.BlockSpec(memory_space=pl.ANY), scalars],
        compiler_params=pltpu.CompilerParams(vmem_limit_bytes=VMEM_ALL),
        name="spare_room",
    )(after)


def place_kernel(after, place_ref, empty_ref, front_ref, up_ref, back_ref, down_ref, *rest):
    out_ref, sums, zeros, sem = rest[after], *rest[-3:]
    half = front_ref.shape[0]
    zeros[...] = jnp.zeros_like(zeros)

    def blank(place, carry):
        @pl.when(empty_ref[place] > 0)
        def _():
            pltpu.make_async_copy(zeros, out_ref.at[place], sem).start()

        return carry

    def put(block):
        pltpu.make_async_copy(sums.at[block], out_ref.at[place_ref[block]], sem).start()

    def add(j, carry):
        sums[j] = (front_ref[j] + up_ref[j].astype(jnp.float32)).astype(jnp.bfloat16)
        put(j)
        sums[half + j] = (back_ref[j] + down_ref[j].astype(jnp.float32)).astype(jnp.bfloat16)
        put(half + j)
        return carry

    lax.fori_loop(0, half, add, 0, unroll=4)
    lax.fori_loop(0, out_ref.shape[0], blank, 0, unroll=4)
    pltpu.make_async_copy(out_ref, out_ref, sem).wait()


def place_blocks(place, empty, front, up, back, down, *after):
    half, rows, cols = front.shape
    scalars = pl.BlockSpec(memory_space=SMEM)
    return pl.pallas_call(
        functools.partial(place_kernel, len(after)),
        out_shape=jax.ShapeDtypeStruct((empty.shape[0], rows, cols), jnp.bfloat16),
        in_specs=[scalars] * 2
        + [pl.BlockSpec(memory_space=VMEM)] * 4
        + [pl.BlockSpec(memory_space=pl.ANY)] * len(after),
        out_specs=pl.BlockSpec(memory_space=HBM),
        scratch_shapes=[
            VMEM((2 * half, rows, cols), jnp.bfloat16),
            VMEM((rows, cols), jnp.bfloat16),
            pltpu.SemaphoreType.DMA(()),
        ],
        compiler_params=pltpu.CompilerParams(vmem_limit_bytes=VMEM_LIMIT),
        cost_estimate=cost(0, 0, 8 * half * rows * cols * 2),
        name="place_blocks",
    )(place, empty, front, up, back, down, *after)


def add_kernel(one_ref, two_ref, three_ref, four_ref, *rest):
    first_ref, second_ref = rest[-2:]

    def add(j, carry):
        first_ref[j] = one_ref[j] + two_ref[j]
        second_ref[j] = three_ref[j] + four_ref[j]
        return carry

    lax.fori_loop(0, first_ref.shape[0], add, 0, unroll=8)


def add_pairs(one, two, three, four, *after):
    near = pl.BlockSpec(memory_space=VMEM)
    shape = jax.ShapeDtypeStruct(one.shape, one.dtype)
    return pl.pallas_call(
        add_kernel,
        out_shape=[shape, shape],
        in_specs=[near] * 4 + [pl.BlockSpec(memory_space=pl.ANY)] * len(after),
        out_specs=[near, near],
        compiler_params=pltpu.CompilerParams(vmem_limit_bytes=VMEM_SMALL),
        cost_estimate=cost(800, 512, 2 * one.size),
        name="add_pairs",
    )(one, two, three, four, *after)


def new_roots(live, stats, grams, low, square, term, prod, between):
    side = stats.shape[-1]
    f32, bf16 = jnp.float32, jnp.bfloat16
    c0, c1, c2, c3, c4, c5, c6 = ROOT_POLY
    grid = tiles(side)
    keep = jnp.where(live, DECAY_RATE, 1.0)
    take = jnp.where(live, 1.0 - DECAY_RATE, 0.0)
    scales = []
    for i in range(2):
        squares = []
        for rows, cols in grid:
            tile = keep * stats[i, rows, cols] + take * grams[i, rows, cols]
            tile = plus_diag(tile, rows, cols, ROOT_RIDGE)
            low[i, rows, cols] = tile.astype(bf16)
            squares.append(tile * tile)
        frob = side * jnp.sqrt(total(squares) * (1.0 / (side * side)) + NORM_EPS)
        scales.append(2.5 / frob)
        prod[i] = mul(low[i], low[i])
        between()
    for i in range(2):
        one, two = scales[i], scales[i] * scales[i]
        for rows, cols in grid:
            tile = prod[i, rows, cols].astype(bf16)
            square[i, rows, cols] = tile
            tile = (c5 * one).astype(bf16) * low[i, rows, cols] + (c6 * two).astype(bf16) * tile
            term[i, rows, cols] = plus_diag(tile, rows, cols, c4)
        prod[i] = mul(square[i], term[i])
    for i in range(2):
        one, two = scales[i], scales[i] * scales[i]
        for rows, cols in grid:
            tile = (two * prod[i, rows, cols]).astype(bf16) + (c3 * one).astype(bf16) * low[i, rows, cols]
            term[i, rows, cols] = plus_diag(tile, rows, cols, c2)
        prod[i] = mul(square[i], term[i])
    for i in (1, 0):
        one, two = scales[i], scales[i] * scales[i]
        for rows, cols in grid:
            tile = two * prod[i, rows, cols] + (c1 * one) * low[i, rows, cols].astype(f32)
            term[i, rows, cols] = plus_diag(tile, rows, cols, c0).astype(bf16)


def precondition_kernel(
    live_ref, arrived_a, arrived_b, left_stats, right_stats, left_roots, right_roots, _, out,
    done_ref, stats, roots, results, wide, prod, raws, low, square, term, in_sems, out_sems,
):
    side = stats.shape[-1]
    entries = side * side
    f32, bf16 = jnp.float32, jnp.bfloat16
    grid = tiles(side)
    fetch = {}

    def get(name, source, target):
        fetch[name] = pltpu.make_async_copy(source, target, in_sems.at[len(fetch)])
        fetch[name].start()

    for slot in range(1, MOST):
        get("r%d" % slot, right_roots.at[0, 0, slot], roots.at[2 * slot - 1])
        get("l%d" % slot, left_roots.at[0, 0, slot], roots.at[2 * slot - 2])
    get("left", left_stats.at[0, 0, 0], stats.at[0])
    get("right", right_stats.at[0, 0, 0], stats.at[1])

    def block_of(slot):
        halves = [half[:, slot].reshape(side, side // 2) for half in (arrived_a, arrived_b)]
        return jnp.concatenate(halves, axis=1)

    def give(slot, low=0, high=arrived_a.shape[0], part=0):
        slabs = pl.ds(low, high - low)
        copy = pltpu.make_async_copy(results.at[slot, slabs], out.at[slabs, slot], out_sems.at[slot + part])
        copy.start()
        sent.append(copy)

    def put(number, rows, cols, tile):
        slabs = slice(rows.start // 16, rows.stop // 16)
        results[number, slabs, :, cols] = tile.reshape(ROWS // 16, 16, COLS)

    def power(tile_of):
        return total([jnp.square(tile_of(rows, cols)) for rows, cols in grid]) * (1.0 / entries)

    def graft(slot, block, raw, parts=1):
        grad_power = power(lambda rows, cols: block[rows, cols].astype(f32))
        scale = jnp.sqrt(grad_power) / jnp.sqrt(power(lambda rows, cols: raw[rows, cols]) + GRAFT_EPS)
        share = results.shape[1] // parts
        for part in range(parts):
            for rows, cols in grid:
                if rows.start // 16 // share == part:
                    put(slot, rows, cols, (raw[rows, cols] * scale).astype(bf16))
            give(slot, part * share, (part + 1) * share, MOST * (part > 0) + max(part - 1, 0))

    block = block_of(0)
    others = [block_of(slot) for slot in range(1, MOST)]
    wide[0] = mul(block, block, ((1,), (1,)))
    wide[1] = mul(block, block, ((0,), (0,)))
    for i in range(MOST - 1):
        fetch["r%d" % (i + 1)].wait()
        raws[i] = mul(others[i], roots[2 * i + 1])
    for i in range(MOST - 1):
        for rows, cols in grid:
            square[i, rows, cols] = raws[i, rows, cols].astype(bf16)
        fetch["l%d" % (i + 1)].wait()
        raws[i] = mul(roots[2 * i], square[i])
    sent = []
    for i, name in enumerate(("left", "right")):
        fetch[name].wait()
    fill = iter(range(MOST - 1))

    def between():
        for i in fill:
            graft(i + 1, others[i], raws.at[i])
            break

    new_roots(live_ref[0] > 0, stats, wide, low, square, term, prod, between)
    prod[0] = mul(block, term[1])
    for rows, cols in grid:
        low[0, rows, cols] = prod[0, rows, cols].astype(bf16)
    prod[1] = mul(term[0], low[0])
    graft(0, block, prod.at[1], PARTS)
    for copy in sent:
        copy.wait()
    done_ref[0] = 0


def precondition(live, arrived, left_stats, right_stats, left_roots, right_roots, spare):
    owners, _, rows, width = arrived[0].shape
    side = left_stats.shape[-1]
    far = pl.BlockSpec(memory_space=HBM)
    return pl.pallas_call(
        precondition_kernel,
        out_shape=[jax.ShapeDtypeStruct((owners, MOST, rows, side), jnp.bfloat16), token_shape()],
        in_specs=[pl.BlockSpec(memory_space=SMEM)] + [pl.BlockSpec(memory_space=VMEM)] * 2 + [far] * 5,
        out_specs=[far, pl.BlockSpec(memory_space=SMEM)],
        scratch_shapes=[
            VMEM((2, side, side), jnp.float32),
            VMEM((2 * MOST - 2, side, side), jnp.bfloat16),
            VMEM((MOST, owners, rows, side), jnp.bfloat16),
            VMEM((2, side, side), jnp.float32),
            VMEM((2, side, side), jnp.float32),
            VMEM((2, side, side), jnp.float32),
            VMEM((2, side, side), jnp.bfloat16),
            VMEM((2, side, side), jnp.bfloat16),
            VMEM((2, side, side), jnp.bfloat16),
            pltpu.SemaphoreType.DMA((2 * MOST,)),
            pltpu.SemaphoreType.DMA((MOST + PARTS - 1,)),
        ],
        compiler_params=pltpu.CompilerParams(vmem_limit_bytes=VMEM_MOST),
        cost_estimate=cost(14, side, 9 * side * side * 4),
        input_output_aliases={7: 0},
        name="precondition",
    )(live, *arrived, left_stats, right_stats, left_roots, right_roots, spare)


def stats_kernel(
    live_ref, front_ref, back_ref, lprev_ref, rprev_ref, _, left_ref, right_ref, lroot_ref, rroot_ref,
    stats, grams, low, square, term, prod,
):
    side = lprev_ref.shape[-1]
    block = jnp.concatenate([front_ref[:, 0], back_ref[:, 0]], axis=-1).reshape(side, side)
    live = live_ref[pl.program_id(0)] > 0
    grams[0] = mul(block, block, ((1,), (1,)))
    grams[1] = mul(block, block, ((0,), (0,)))
    for rows, cols in tiles(side):
        left_ref[0, 0, 0, rows, cols] = blend(live, lprev_ref[0, 0, 0, rows, cols], grams[0, rows, cols])
        right_ref[0, 0, 0, rows, cols] = blend(live, rprev_ref[0, 0, 0, rows, cols], grams[1, rows, cols])

    @pl.when(pl.program_id(0) == 0)
    def _():
        stats[0] = lprev_ref[0, 0, 0]
        stats[1] = rprev_ref[0, 0, 0]
        new_roots(live, stats, grams, low, square, term, prod, lambda: None)
        lroot_ref[0, 0] = term[0]
        rroot_ref[0, 0] = term[1]


def update_stats(live, arrived, left_stats, right_stats, tied):
    owners, _, rows, width = arrived[0].shape
    side = left_stats.shape[-1]
    at_slot = pl.BlockSpec((1, 1, 1, side, side), lambda s: (0, 0, s, 0, 0))
    of_first = pl.BlockSpec((1, 1, side, side), lambda s: (0, 0, 0, 0))
    shape = jax.ShapeDtypeStruct(left_stats.shape, jnp.float32)
    root = jax.ShapeDtypeStruct((1, 1, side, side), jnp.bfloat16)
    return pl.pallas_call(
        stats_kernel,
        grid=(MOST,),
        out_shape=[shape, shape, root, root],
        in_specs=[pl.BlockSpec(memory_space=SMEM)]
        + [pl.BlockSpec((owners, 1, rows, width), lambda s: (0, s, 0, 0))] * 2
        + [at_slot, at_slot, pl.BlockSpec(memory_space=SMEM)],
        out_specs=[at_slot, at_slot, of_first, of_first],
        scratch_shapes=[
            VMEM((2, side, side), jnp.float32),
            VMEM((2, side, side), jnp.float32),
            VMEM((2, side, side), jnp.bfloat16),
            VMEM((2, side, side), jnp.bfloat16),
            VMEM((2, side, side), jnp.bfloat16),
            VMEM((2, side, side), jnp.float32),
        ],
        compiler_params=pltpu.CompilerParams(vmem_limit_bytes=VMEM_MOST),
        cost_estimate=cost(2 * MOST + 6, side, 13 * side * side * 4),
        name="update_stats",
    )(live, *arrived, left_stats, right_stats, tied)


def assemble_kernel(slot_ref, owner_ref, back_ref, out_ref, sem):
    count = out_ref.shape[0]

    def start(b, carry):
        pltpu.make_async_copy(back_ref.at[owner_ref[b], slot_ref[b]], out_ref.at[b], sem).start()
        return carry

    lax.fori_loop(0, count, start, 0, unroll=8)
    pltpu.make_async_copy(out_ref, out_ref, sem).wait()


def assemble(slot_of, owner_of, back):
    count = slot_of.shape[0]
    rows, cols = back.shape[2:]
    return pl.pallas_call(
        assemble_kernel,
        out_shape=jax.ShapeDtypeStruct((count, rows, cols), jnp.bfloat16),
        in_specs=[pl.BlockSpec(memory_space=SMEM)] * 2 + [pl.BlockSpec(memory_space=pl.ANY)],
        out_specs=pl.BlockSpec(memory_space=HBM),
        scratch_shapes=[pltpu.SemaphoreType.DMA(())],
        compiler_params=pltpu.CompilerParams(vmem_limit_bytes=VMEM_LIMIT),
        cost_estimate=cost(0, 0, 2 * count * rows * cols * 2),
        name="assemble",
    )(slot_of, owner_of, back)


def token_shape():
    return jax.ShapeDtypeStruct((1,), jnp.int32)


def routing(owner, owners):
    ids = jnp.arange(owner.shape[0], dtype=jnp.int32)
    same = owner[:, None] == owner[None, :]
    slot = jnp.sum((same & (ids[None, :] < ids[:, None])).astype(jnp.int32), axis=1)
    place = owner * MOST + slot
    taken = place[None, :] == jnp.arange(owners * MOST, dtype=jnp.int32)[:, None]
    return slot, place, 1 - jnp.sum(taken.astype(jnp.int32), axis=1)


def on_device(grads, owner_table, left_stats, right_stats, left_roots, right_roots):
    groups = lax.axis_size("rep")
    owners = lax.axis_size("fsdp")
    group_id = lax.axis_index("rep")
    owner_id = lax.axis_index("fsdp")
    local = grads[0]
    total_blocks, slab_rows, side = local.shape
    share = total_blocks // groups
    half = share // 2
    up = [(i, (i + 1) % groups) for i in range(groups)]
    down = [(i, (i - 1) % groups) for i in range(groups)]

    owner = lax.dynamic_slice(owner_table[:, 0], (group_id * share,), (share,), allow_negative_indices=False)
    slot, place, empty = routing(owner, owners)
    own_count = jnp.sum((owner == owner_id).astype(jnp.int32))
    live = (jnp.arange(MOST, dtype=jnp.int32) < own_count).astype(jnp.int32)

    width = side // 2

    def part(source, ahead, low, column):
        start = ((group_id + ahead) & (groups - 1)) * share + low
        return lax.dynamic_slice(
            source, (start, 0, column), (half, slab_rows, width), allow_negative_indices=False
        )

    def send(pair):
        return lax.ppermute(pair[0], "rep", up), lax.ppermute(pair[1], "rep", down)

    def firsts(source, column):
        return part(source, 2, 0, column), part(source, 2, half, column)

    def seconds(source, column):
        return part(source, 1, half, column), part(source, 3, 0, column)

    def mids(source, column):
        return part(source, 1, 0, column), part(source, 3, half, column)

    def own_sums(source, column, up2, down2):
        front = part(source, 0, 0, column).astype(jnp.float32) + down2.astype(jnp.float32)
        return front, part(source, 0, half, column).astype(jnp.float32) + up2.astype(jnp.float32)

    first = firsts(local, 0)
    up1, down1 = send(first)
    later, _ = lax.optimization_barrier((local, first))
    second = seconds(later, 0)
    up2, down2 = send(second)
    later, _ = lax.optimization_barrier((later, second))
    mid = mids(later, 0)
    third = mid[0] + up1, mid[1] + down1
    up3, down3 = send(third)
    later, _ = lax.optimization_barrier((later, third))
    firsts_b, seconds_b = firsts(later, width), seconds(later, width)
    sums = own_sums(local, 0, up2, down2)
    up1, down1 = send(firsts_b)
    up2, down2 = send(seconds_b)
    spare, made = spare_room(empty, (owners, MOST, slab_rows, side))
    outgoing_a = place_blocks(place, empty, sums[0], up3, sums[1], down3, *firsts_b, *seconds_b, made)
    mid = mids(later, width)
    third = add_pairs(mid[0], up1, mid[1], down1, outgoing_a)
    up3, down3 = send(third)
    later, _ = lax.optimization_barrier((later, third))
    sums = own_sums(later, width, up2, down2)
    outgoing_b = place_blocks(place, empty, sums[0], up3, sums[1], down3)
    arrived = [
        lax.all_to_all(
            outgoing.reshape(owners, MOST, slab_rows, width), "fsdp", split_axis=0, concat_axis=0, tiled=True
        )
        for outgoing in (outgoing_a, outgoing_b)
    ]
    results, done = precondition(
        live, arrived, left_stats, right_stats, left_roots, right_roots, spare
    )
    returned = lax.all_to_all(results, "fsdp", split_axis=0, concat_axis=0, tiled=True)
    left_out, right_out, left_new, right_new = update_stats(live, arrived, left_stats, right_stats, done)
    preconditioned = assemble(slot, owner, returned)
    return (
        preconditioned,
        left_out,
        right_out,
        left_new,
        right_new,
    )


def solution(mesh):
    in_specs = (
        P("rep", None, "fsdp", None),
        P(),
        P("rep", "fsdp", None, None, None),
        P("rep", "fsdp", None, None, None),
        P("rep", "fsdp", None, None, None),
        P("rep", "fsdp", None, None, None),
    )
    out_specs = (
        P("rep", "fsdp", None),
        P("rep", "fsdp", None, None, None),
        P("rep", "fsdp", None, None, None),
        P("rep", "fsdp", None, None),
        P("rep", "fsdp", None, None),
    )
    return jax.shard_map(
        on_device, mesh=mesh, in_specs=in_specs, out_specs=out_specs, check_vma=False
    )
```

```python
import functools

import jax
import jax.numpy as jnp
from jax import lax
from jax.experimental import pallas as pl
from jax.experimental.pallas import tpu as pltpu
from jax.sharding import PartitionSpec as P

DECAY_RATE = 0.9
ROOT_RIDGE = 1e-06
GRAFT_EPS = 1e-12
NORM_EPS = 1e-12
MOST = 3

ROOT_POLY = (
    25.0 / 16.0,
    -5.0 / 16.0 - 3125.0 / 4096.0,
    3125.0 / 4096.0,
    -1250.0 / 4096.0,
    250.0 / 4096.0,
    -25.0 / 4096.0,
    1.0 / 4096.0,
)

VMEM_LIMIT = 40 * 1024 * 1024
VMEM_MOST = 52 * 1024 * 1024
VMEM_ALL = 60 * 1024 * 1024
VMEM_SMALL = 16 * 1024 * 1024
VMEM = pltpu.VMEM
HBM = pltpu.HBM
SMEM = pltpu.SMEM


def mul(left, right, dims=((1,), (0,))):
    return lax.dot_general(left, right, (dims, ((), ())), preferred_element_type=jnp.float32)


def blend(live, prev, gram):
    return jnp.where(live, DECAY_RATE * prev + (1.0 - DECAY_RATE) * gram, prev)


PIECE = 256
ROWS = 64
COLS = 128
PARTS = 4


def tiles(side):
    return [
        (slice(row, row + ROWS), slice(col, col + COLS))
        for row in range(0, side, ROWS)
        for col in range(0, side, COLS)
    ]


def product(left, right, use):
    side = left.shape[0]
    for row in range(0, side, PIECE):
        for col in range(0, side, PIECE):
            piece = mul(left[row : row + PIECE, :], right[:, col : col + PIECE])
            for r in range(0, PIECE, ROWS):
                for c in range(0, PIECE, COLS):
                    rows, cols = slice(row + r, row + r + ROWS), slice(col + c, col + c + COLS)
                    use(piece[r : r + ROWS, c : c + COLS], rows, cols)


def plus_diag(tile, rows, cols, value):
    if rows.start // COLS != cols.start // COLS:
        return tile
    row_ids = lax.broadcasted_iota(jnp.int32, tile.shape, 0) + rows.start
    col_ids = lax.broadcasted_iota(jnp.int32, tile.shape, 1) + cols.start
    return tile + jnp.where(row_ids == col_ids, value, 0.0).astype(tile.dtype)


def total(parts):
    return jnp.sum(functools.reduce(lambda x, y: x + y, parts), keepdims=True)


def cost(matmuls, side, nbytes):
    return pl.CostEstimate(flops=matmuls * 2 * side**3, bytes_accessed=nbytes, transcendentals=0)


def spare_kernel(_, room_ref, done_ref):
    done_ref[0] = 0


def spare_room(after, shape):
    scalars = pl.BlockSpec(memory_space=SMEM)
    return pl.pallas_call(
        spare_kernel,
        out_shape=[jax.ShapeDtypeStruct(shape, jnp.bfloat16), token_shape()],
        in_specs=[scalars],
        out_specs=[pl.BlockSpec(memory_space=pl.ANY), scalars],
        compiler_params=pltpu.CompilerParams(vmem_limit_bytes=VMEM_ALL),
        name="spare_room",
    )(after)


def place_kernel(after, place_ref, empty_ref, front_ref, up_ref, back_ref, down_ref, *rest):
    out_ref, sums, zeros, sem = rest[after], *rest[-3:]
    half = front_ref.shape[0]
    zeros[...] = jnp.zeros_like(zeros)

    def blank(place, carry):
        @pl.when(empty_ref[place] > 0)
        def _():
            pltpu.make_async_copy(zeros, out_ref.at[place], sem).start()

        return carry

    def put(block):
        pltpu.make_async_copy(sums.at[block], out_ref.at[place_ref[block]], sem).start()

    def add(j, carry):
        sums[j] = (front_ref[j] + up_ref[j].astype(jnp.float32)).astype(jnp.bfloat16)
        put(j)
        sums[half + j] = (back_ref[j] + down_ref[j].astype(jnp.float32)).astype(jnp.bfloat16)
        put(half + j)
        return carry

    lax.fori_loop(0, half, add, 0, unroll=4)
    lax.fori_loop(0, out_ref.shape[0], blank, 0, unroll=4)
    pltpu.make_async_copy(out_ref, out_ref, sem).wait()


def place_blocks(place, empty, front, up, back, down, *after):
    half, rows, cols = front.shape
    scalars = pl.BlockSpec(memory_space=SMEM)
    return pl.pallas_call(
        functools.partial(place_kernel, len(after)),
        out_shape=jax.ShapeDtypeStruct((empty.shape[0], rows, cols), jnp.bfloat16),
        in_specs=[scalars] * 2
        + [pl.BlockSpec(memory_space=VMEM)] * 4
        + [pl.BlockSpec(memory_space=pl.ANY)] * len(after),
        out_specs=pl.BlockSpec(memory_space=HBM),
        scratch_shapes=[
            VMEM((2 * half, rows, cols), jnp.bfloat16),
            VMEM((rows, cols), jnp.bfloat16),
            pltpu.SemaphoreType.DMA(()),
        ],
        compiler_params=pltpu.CompilerParams(vmem_limit_bytes=VMEM_LIMIT),
        cost_estimate=cost(0, 0, 8 * half * rows * cols * 2),
        name="place_blocks",
    )(place, empty, front, up, back, down, *after)


def add_kernel(one_ref, two_ref, three_ref, four_ref, *rest):
    first_ref, second_ref = rest[-2:]

    def add(j, carry):
        first_ref[j] = one_ref[j] + two_ref[j]
        second_ref[j] = three_ref[j] + four_ref[j]
        return carry

    lax.fori_loop(0, first_ref.shape[0], add, 0, unroll=8)


def add_pairs(one, two, three, four, *after):
    near = pl.BlockSpec(memory_space=VMEM)
    shape = jax.ShapeDtypeStruct(one.shape, one.dtype)
    return pl.pallas_call(
        add_kernel,
        out_shape=[shape, shape],
        in_specs=[near] * 4 + [pl.BlockSpec(memory_space=pl.ANY)] * len(after),
        out_specs=[near, near],
        compiler_params=pltpu.CompilerParams(vmem_limit_bytes=VMEM_SMALL),
        cost_estimate=cost(800, 512, 2 * one.size),
        name="add_pairs",
    )(one, two, three, four, *after)


def new_roots(live, stats, grams, low, square, inner, outer, between):
    side = stats.shape[-1]
    f32, bf16 = jnp.float32, jnp.bfloat16
    c0, c1, c2, c3, c4, c5, c6 = ROOT_POLY
    keep = jnp.where(live, DECAY_RATE, 1.0)
    take = jnp.where(live, 1.0 - DECAY_RATE, 0.0)
    scales = []
    for i in range(2):
        squares = []
        for rows, cols in tiles(side):
            tile = keep * stats[i, rows, cols] + take * grams[i, rows, cols]
            tile = plus_diag(tile, rows, cols, ROOT_RIDGE)
            low[i, rows, cols] = tile.astype(bf16)
            squares.append(tile * tile)
        frob = side * jnp.sqrt(total(squares) * (1.0 / (side * side)) + NORM_EPS)
        scales.append(2.5 / frob)

    for i in range(2):
        near, far = (c5 * scales[i]).astype(bf16), (c6 * scales[i] * scales[i]).astype(bf16)

        def first(tile, rows, cols):
            tile = tile.astype(bf16)
            square[i, rows, cols] = tile
            inner[i, rows, cols] = plus_diag(near * low[i, rows, cols] + far * tile, rows, cols, c4)

        product(low[i], low[i], first)
        between()
    for i in range(2):
        near, far = (c3 * scales[i]).astype(bf16), scales[i] * scales[i]

        def second(tile, rows, cols):
            tile = (far * tile).astype(bf16) + near * low[i, rows, cols]
            outer[i, rows, cols] = plus_diag(tile, rows, cols, c2)

        product(square[i], inner[i], second)
    for i in (1, 0):
        near, far = c1 * scales[i], scales[i] * scales[i]

        def third(tile, rows, cols):
            tile = far * tile + near * low[i, rows, cols].astype(f32)
            inner[i, rows, cols] = plus_diag(tile, rows, cols, c0).astype(bf16)

        product(square[i], outer[i], third)


def precondition_kernel(
    live_ref, arrived_a, arrived_b, left_stats, right_stats, left_roots, right_roots, _, out,
    done_ref, halves, stats, roots, results, grams, raws, applied, low, square, inner, outer, in_sems, out_sems,
):
    side = stats.shape[-1]
    entries = side * side
    f32, bf16 = jnp.float32, jnp.bfloat16
    grid = tiles(side)
    fetch = {}

    def get(name, source, target):
        fetch[name] = pltpu.make_async_copy(source, target, in_sems.at[len(fetch)])
        fetch[name].start()

    get("a0", arrived_a.at[:, 0], halves.at[0])
    for slot in range(1, MOST):
        get("a%d" % slot, arrived_a.at[:, slot], halves.at[slot])
        get("r%d" % slot, right_roots.at[0, 0, slot], roots.at[2 * slot - 1])
    for slot in range(1, MOST):
        get("l%d" % slot, left_roots.at[0, 0, slot], roots.at[2 * slot - 2])
    get("left", left_stats.at[0, 0, 0], stats.at[0])
    get("right", right_stats.at[0, 0, 0], stats.at[1])

    def block_of(slot):
        fetch["a%d" % slot].wait()
        front, back = halves[slot], arrived_b[:, slot]
        return jnp.concatenate([half.reshape(side, side // 2) for half in (front, back)], axis=1)

    def give(slot, low=0, high=arrived_a.shape[0], part=0):
        slabs = pl.ds(low, high - low)
        copy = pltpu.make_async_copy(results.at[slot, slabs], out.at[slabs, slot], out_sems.at[slot + part])
        copy.start()
        sent.append(copy)

    def put(number, rows, cols, tile):
        slabs = slice(rows.start // 16, rows.stop // 16)
        results[number, slabs, :, cols] = tile.reshape(ROWS // 16, 16, COLS)

    def power(tile_of):
        return total([jnp.square(tile_of(rows, cols)) for rows, cols in grid]) * (1.0 / entries)

    def graft(slot, out_power, parts=1):
        grad_power = power(lambda rows, cols: blocks[slot][rows, cols].astype(f32))
        scale = jnp.sqrt(grad_power) / jnp.sqrt(out_power + GRAFT_EPS)
        share = results.shape[1] // parts
        for part in range(parts):
            for rows, cols in grid:
                if rows.start // 16 // share == part:
                    put(slot, rows, cols, (raws[slot, rows, cols] * scale).astype(bf16))
            give(slot, part * share, (part + 1) * share, MOST * (part > 0) + max(part - 1, 0))

    def apply_right(slot, root):
        def use(tile, rows, cols):
            applied[slot, rows, cols] = tile.astype(bf16)

        product(blocks[slot], root, use)

    def apply_left(slot, root):
        squares = []

        def use(tile, rows, cols):
            raws[slot, rows, cols] = tile
            squares.append(tile * tile)

        product(root, applied[slot], use)
        return total(squares) * (1.0 / entries)

    blocks = [block_of(0)]
    grams[0] = mul(blocks[0], blocks[0], ((1,), (1,)))
    grams[1] = mul(blocks[0], blocks[0], ((0,), (0,)))
    for slot in range(1, MOST):
        blocks.append(block_of(slot))
        fetch["r%d" % slot].wait()
    for slot in range(1, MOST):
        apply_right(slot, roots[2 * slot - 1])
    for slot in range(1, MOST):
        fetch["l%d" % slot].wait()
    powers = [apply_left(slot, roots[2 * slot - 2]) for slot in range(1, MOST)]
    sent = []
    fetch["left"].wait()
    fetch["right"].wait()
    fill = iter(range(1, MOST))

    def between():
        for slot in fill:
            graft(slot, powers[slot - 1])
            break

    new_roots(live_ref[0] > 0, stats, grams, low, square, inner, outer, between)
    apply_right(0, inner[1])
    graft(0, apply_left(0, inner[0]), PARTS)
    for copy in sent:
        copy.wait()
    done_ref[0] = 0


def precondition(live, arrived, left_stats, right_stats, left_roots, right_roots, spare):
    owners, _, rows, width = arrived[0].shape
    side = left_stats.shape[-1]
    far = pl.BlockSpec(memory_space=HBM)
    return pl.pallas_call(
        precondition_kernel,
        out_shape=[jax.ShapeDtypeStruct((owners, MOST, rows, side), jnp.bfloat16), token_shape()],
        in_specs=[pl.BlockSpec(memory_space=SMEM), far, pl.BlockSpec(memory_space=VMEM)] + [far] * 5,
        out_specs=[far, pl.BlockSpec(memory_space=SMEM)],
        scratch_shapes=[
            VMEM((MOST, owners, rows, width), jnp.bfloat16),
            VMEM((2, side, side), jnp.float32),
            VMEM((2 * MOST - 2, side, side), jnp.bfloat16),
            VMEM((MOST, owners, rows, side), jnp.bfloat16),
            VMEM((2, side, side), jnp.float32),
            VMEM((MOST, side, side), jnp.float32),
            VMEM((MOST, side, side), jnp.bfloat16),
            VMEM((2, side, side), jnp.bfloat16),
            VMEM((2, side, side), jnp.bfloat16),
            VMEM((2, side, side), jnp.bfloat16),
            VMEM((2, side, side), jnp.bfloat16),
            pltpu.SemaphoreType.DMA((3 * MOST,)),
            pltpu.SemaphoreType.DMA((MOST + PARTS - 1,)),
        ],
        compiler_params=pltpu.CompilerParams(vmem_limit_bytes=VMEM_MOST),
        cost_estimate=cost(14, side, 9 * side * side * 4),
        input_output_aliases={7: 0},
        name="precondition",
    )(live, *arrived, left_stats, right_stats, left_roots, right_roots, spare)


def stats_kernel(
    live_ref, front_ref, back_ref, lprev_ref, rprev_ref, _, left_ref, right_ref, lroot_ref, rroot_ref,
    stats, grams, low, square, inner, outer,
):
    side = lprev_ref.shape[-1]
    block = jnp.concatenate([front_ref[:, 0], back_ref[:, 0]], axis=-1).reshape(side, side)
    live = live_ref[pl.program_id(0)] > 0
    grams[0] = mul(block, block, ((1,), (1,)))
    grams[1] = mul(block, block, ((0,), (0,)))
    for rows, cols in tiles(side):
        left_ref[0, 0, 0, rows, cols] = blend(live, lprev_ref[0, 0, 0, rows, cols], grams[0, rows, cols])
        right_ref[0, 0, 0, rows, cols] = blend(live, rprev_ref[0, 0, 0, rows, cols], grams[1, rows, cols])

    @pl.when(pl.program_id(0) == 0)
    def _():
        stats[0] = lprev_ref[0, 0, 0]
        stats[1] = rprev_ref[0, 0, 0]
        new_roots(live, stats, grams, low, square, inner, outer, lambda: None)
        lroot_ref[0, 0] = inner[0]
        rroot_ref[0, 0] = inner[1]


def update_stats(live, arrived, left_stats, right_stats, tied):
    owners, _, rows, width = arrived[0].shape
    side = left_stats.shape[-1]
    at_slot = pl.BlockSpec((1, 1, 1, side, side), lambda s: (0, 0, s, 0, 0))
    of_first = pl.BlockSpec((1, 1, side, side), lambda s: (0, 0, 0, 0))
    shape = jax.ShapeDtypeStruct(left_stats.shape, jnp.float32)
    root = jax.ShapeDtypeStruct((1, 1, side, side), jnp.bfloat16)
    return pl.pallas_call(
        stats_kernel,
        grid=(MOST,),
        out_shape=[shape, shape, root, root],
        in_specs=[pl.BlockSpec(memory_space=SMEM)]
        + [pl.BlockSpec((owners, 1, rows, width), lambda s: (0, s, 0, 0))] * 2
        + [at_slot, at_slot, pl.BlockSpec(memory_space=SMEM)],
        out_specs=[at_slot, at_slot, of_first, of_first],
        scratch_shapes=[
            VMEM((2, side, side), jnp.float32),
            VMEM((2, side, side), jnp.float32),
            VMEM((2, side, side), jnp.bfloat16),
            VMEM((2, side, side), jnp.bfloat16),
            VMEM((2, side, side), jnp.bfloat16),
            VMEM((2, side, side), jnp.bfloat16),
        ],
        compiler_params=pltpu.CompilerParams(vmem_limit_bytes=VMEM_MOST),
        cost_estimate=cost(2 * MOST + 6, side, 13 * side * side * 4),
        name="update_stats",
    )(live, *arrived, left_stats, right_stats, tied)


def assemble_kernel(slot_ref, owner_ref, back_ref, out_ref, sem):
    count = out_ref.shape[0]

    def start(b, carry):
        pltpu.make_async_copy(back_ref.at[owner_ref[b], slot_ref[b]], out_ref.at[b], sem).start()
        return carry

    lax.fori_loop(0, count, start, 0, unroll=8)
    pltpu.make_async_copy(out_ref, out_ref, sem).wait()


def assemble(slot_of, owner_of, back):
    count = slot_of.shape[0]
    rows, cols = back.shape[2:]
    return pl.pallas_call(
        assemble_kernel,
        out_shape=jax.ShapeDtypeStruct((count, rows, cols), jnp.bfloat16),
        in_specs=[pl.BlockSpec(memory_space=SMEM)] * 2 + [pl.BlockSpec(memory_space=pl.ANY)],
        out_specs=pl.BlockSpec(memory_space=HBM),
        scratch_shapes=[pltpu.SemaphoreType.DMA(())],
        compiler_params=pltpu.CompilerParams(vmem_limit_bytes=VMEM_LIMIT),
        cost_estimate=cost(0, 0, 2 * count * rows * cols * 2),
        name="assemble",
    )(slot_of, owner_of, back)


def token_shape():
    return jax.ShapeDtypeStruct((1,), jnp.int32)


def routing(owner, owners):
    ids = jnp.arange(owner.shape[0], dtype=jnp.int32)
    same = owner[:, None] == owner[None, :]
    slot = jnp.sum((same & (ids[None, :] < ids[:, None])).astype(jnp.int32), axis=1)
    place = owner * MOST + slot
    taken = place[None, :] == jnp.arange(owners * MOST, dtype=jnp.int32)[:, None]
    return slot, place, 1 - jnp.sum(taken.astype(jnp.int32), axis=1)


def on_device(grads, owner_table, left_stats, right_stats, left_roots, right_roots):
    groups = lax.axis_size("rep")
    owners = lax.axis_size("fsdp")
    group_id = lax.axis_index("rep")
    owner_id = lax.axis_index("fsdp")
    local = grads[0]
    total_blocks, slab_rows, side = local.shape
    share = total_blocks // groups
    half = share // 2
    up = [(i, (i + 1) % groups) for i in range(groups)]
    down = [(i, (i - 1) % groups) for i in range(groups)]

    width = side // 2

    def part(source, ahead, low, column):
        start = ((group_id + ahead) & (groups - 1)) * share + low
        return lax.dynamic_slice(
            source, (start, 0, column), (half, slab_rows, width), allow_negative_indices=False
        )

    def send(pair):
        return lax.ppermute(pair[0], "rep", up), lax.ppermute(pair[1], "rep", down)

    def firsts(source, column):
        return part(source, 2, 0, column), part(source, 2, half, column)

    def seconds(source, column):
        return part(source, 1, half, column), part(source, 3, 0, column)

    def mids(source, column):
        return part(source, 1, 0, column), part(source, 3, half, column)

    def own_sums(source, column, up2, down2):
        front = part(source, 0, 0, column).astype(jnp.float32) + down2.astype(jnp.float32)
        return front, part(source, 0, half, column).astype(jnp.float32) + up2.astype(jnp.float32)

    first = firsts(local, 0)
    up1, down1 = send(first)
    later, _ = lax.optimization_barrier((local, first))
    second = seconds(later, 0)
    up2, down2 = send(second)
    later, _ = lax.optimization_barrier((later, second))
    mid = mids(later, 0)
    third = mid[0] + up1, mid[1] + down1
    up3, down3 = send(third)
    later, table, _ = lax.optimization_barrier((later, owner_table, third))
    owner = lax.dynamic_slice(table[:, 0], (group_id * share,), (share,), allow_negative_indices=False)
    slot, place, empty = routing(owner, owners)
    own_count = jnp.sum((owner == owner_id).astype(jnp.int32))
    live = (jnp.arange(MOST, dtype=jnp.int32) < own_count).astype(jnp.int32)
    firsts_b, seconds_b = firsts(later, width), seconds(later, width)
    sums = own_sums(local, 0, up2, down2)
    up1, down1 = send(firsts_b)
    up2, down2 = send(seconds_b)
    outgoing_a = place_blocks(place, empty, sums[0], up3, sums[1], down3)
    spare, made = spare_room(empty, (owners, MOST, slab_rows, side))
    mid = mids(later, width)
    third = add_pairs(mid[0], up1, mid[1], down1, outgoing_a)
    up3, down3 = send(third)
    later, _ = lax.optimization_barrier((later, third))
    sums = own_sums(later, width, up2, down2)
    outgoing_b = place_blocks(place, empty, sums[0], up3, sums[1], down3, made)
    arrived = [
        lax.all_to_all(
            outgoing.reshape(owners, MOST, slab_rows, width), "fsdp", split_axis=0, concat_axis=0, tiled=True
        )
        for outgoing in (outgoing_a, outgoing_b)
    ]
    results, done = precondition(
        live, arrived, left_stats, right_stats, left_roots, right_roots, spare
    )
    returned = lax.all_to_all(results, "fsdp", split_axis=0, concat_axis=0, tiled=True)
    left_out, right_out, left_new, right_new = update_stats(live, arrived, left_stats, right_stats, done)
    preconditioned = assemble(slot, owner, returned)
    return (
        preconditioned,
        left_out,
        right_out,
        left_new,
        right_new,
    )


def solution(mesh):
    in_specs = (
        P("rep", None, "fsdp", None),
        P(),
        P("rep", "fsdp", None, None, None),
        P("rep", "fsdp", None, None, None),
        P("rep", "fsdp", None, None, None),
        P("rep", "fsdp", None, None, None),
    )
    out_specs = (
        P("rep", "fsdp", None),
        P("rep", "fsdp", None, None, None),
        P("rep", "fsdp", None, None, None),
        P("rep", "fsdp", None, None),
        P("rep", "fsdp", None, None),
    )
    return jax.shard_map(
        on_device, mesh=mesh, in_specs=in_specs, out_specs=out_specs, check_vma=False
    )
```

```python
import functools

import jax
import jax.numpy as jnp
from jax import lax
from jax.experimental import pallas as pl
from jax.experimental.pallas import tpu as pltpu
from jax.sharding import PartitionSpec as P

DECAY_RATE = 0.9
ROOT_RIDGE = 1e-06
GRAFT_EPS = 1e-12
NORM_EPS = 1e-12
MOST = 3
SPLIT = 2

ROOT_POLY = (
    25.0 / 16.0,
    -5.0 / 16.0 - 3125.0 / 4096.0,
    3125.0 / 4096.0,
    -1250.0 / 4096.0,
    250.0 / 4096.0,
    -25.0 / 4096.0,
    1.0 / 4096.0,
)

VMEM_LIMIT = 40 * 1024 * 1024
VMEM_MOST = 52 * 1024 * 1024
VMEM_ALL = 60 * 1024 * 1024
VMEM_SMALL = 16 * 1024 * 1024
VMEM = pltpu.VMEM
HBM = pltpu.HBM
SMEM = pltpu.SMEM


def mul(left, right, dims=((1,), (0,))):
    return lax.dot_general(left, right, (dims, ((), ())), preferred_element_type=jnp.float32)


def blend(live, prev, gram):
    return jnp.where(live, DECAY_RATE * prev + (1.0 - DECAY_RATE) * gram, prev)


PIECE = 256
ROWS = 64
COLS = 128
PARTS = 4


def tiles(side):
    return [
        (slice(row, row + ROWS), slice(col, col + COLS))
        for row in range(0, side, ROWS)
        for col in range(0, side, COLS)
    ]


def product(left, right, use):
    side = left.shape[0]
    for row in range(0, side, PIECE):
        for col in range(0, side, PIECE):
            piece = mul(left[row : row + PIECE, :], right[:, col : col + PIECE])
            for r in range(0, PIECE, ROWS):
                for c in range(0, PIECE, COLS):
                    rows, cols = slice(row + r, row + r + ROWS), slice(col + c, col + c + COLS)
                    use(piece[r : r + ROWS, c : c + COLS], rows, cols)


def plus_diag(tile, rows, cols, value):
    if rows.start // COLS != cols.start // COLS:
        return tile
    row_ids = lax.broadcasted_iota(jnp.int32, tile.shape, 0) + rows.start
    col_ids = lax.broadcasted_iota(jnp.int32, tile.shape, 1) + cols.start
    return tile + jnp.where(row_ids == col_ids, value, 0.0).astype(tile.dtype)


def total(parts):
    return jnp.sum(functools.reduce(lambda x, y: x + y, parts), keepdims=True)


def cost(matmuls, side, nbytes):
    return pl.CostEstimate(flops=matmuls * 2 * side**3, bytes_accessed=nbytes, transcendentals=0)


def spare_room(shape):
    return pl.pallas_call(
        lambda room: None,
        out_shape=jax.ShapeDtypeStruct(shape, jnp.bfloat16),
        out_specs=pl.BlockSpec(memory_space=pl.ANY),
        compiler_params=pltpu.CompilerParams(vmem_limit_bytes=VMEM_ALL),
        name="spare_room",
    )()


def place_kernel(place_ref, empty_ref, *rest):
    (own_front, straight_front, last_front, own_back, straight_back, last_back), rest = rest[:6], rest[6:]
    out_ref, sums, zeros, sem = rest
    half = own_front.shape[0]
    zeros[...] = jnp.zeros_like(zeros)

    def blank(place, carry):
        @pl.when(empty_ref[place] > 0)
        def _():
            pltpu.make_async_copy(zeros, out_ref.at[place], sem).start()

        return carry

    def add(j, carry):
        for block, own, straight, last in (
            (j, own_front, straight_front, last_front),
            (half + j, own_back, straight_back, last_back),
        ):
            three = own[j], straight[straight.shape[0] - half + j], last[j]
            sums[block] = sum(term.astype(jnp.float32) for term in three).astype(jnp.bfloat16)
            pltpu.make_async_copy(sums.at[block], out_ref.at[place_ref[block]], sem).start()
        return carry

    lax.fori_loop(0, half, add, 0, unroll=4)
    lax.fori_loop(0, out_ref.shape[0], blank, 0, unroll=4)
    pltpu.make_async_copy(out_ref, out_ref, sem).wait()


def place_blocks(place, empty, front, back, weight=0):
    half, rows, cols = front[0].shape
    scalars = pl.BlockSpec(memory_space=SMEM)
    return pl.pallas_call(
        place_kernel,
        out_shape=jax.ShapeDtypeStruct((empty.shape[0], rows, cols), jnp.bfloat16),
        in_specs=[scalars] * 2 + [pl.BlockSpec(memory_space=VMEM)] * 6,
        out_specs=pl.BlockSpec(memory_space=HBM),
        scratch_shapes=[
            VMEM((2 * half, rows, cols), jnp.bfloat16),
            VMEM((rows, cols), jnp.bfloat16),
            pltpu.SemaphoreType.DMA(()),
        ],
        compiler_params=pltpu.CompilerParams(vmem_limit_bytes=VMEM_LIMIT),
        cost_estimate=cost(weight, 512, 8 * half * rows * cols * 2),
        name="place_blocks",
    )(place, empty, *front, *back)


def add_kernel(one_ref, two_ref, three_ref, four_ref, *rest):
    first_ref, second_ref = rest[-2:]

    def add(j, carry):
        first_ref[j] = one_ref[j] + two_ref[j]
        second_ref[j] = three_ref[j] + four_ref[j]
        return carry

    lax.fori_loop(0, first_ref.shape[0], add, 0, unroll=8)


def add_pairs(one, two, three, four, *after):
    near = pl.BlockSpec(memory_space=VMEM)
    shape = jax.ShapeDtypeStruct(one.shape, one.dtype)
    return pl.pallas_call(
        add_kernel,
        out_shape=[shape, shape],
        in_specs=[near] * 4 + [pl.BlockSpec(memory_space=pl.ANY)] * len(after),
        out_specs=[near, near],
        compiler_params=pltpu.CompilerParams(vmem_limit_bytes=VMEM_SMALL),
        cost_estimate=cost(800, 512, 2 * one.size),
        name="add_pairs",
    )(one, two, three, four, *after)


def new_roots(live, stats, grams, low, square, inner, outer, between):
    side = stats.shape[-1]
    f32, bf16 = jnp.float32, jnp.bfloat16
    c0, c1, c2, c3, c4, c5, c6 = ROOT_POLY
    keep = jnp.where(live, DECAY_RATE, 1.0)
    take = jnp.where(live, 1.0 - DECAY_RATE, 0.0)
    scales = []
    for i in range(2):
        squares = []
        for rows, cols in tiles(side):
            tile = keep * stats[i, rows, cols] + take * grams[i, rows, cols]
            tile = plus_diag(tile, rows, cols, ROOT_RIDGE)
            low[i, rows, cols] = tile.astype(bf16)
            squares.append(tile * tile)
        frob = side * jnp.sqrt(total(squares) * (1.0 / (side * side)) + NORM_EPS)
        scales.append(2.5 / frob)

    for i in range(2):
        near, far = (c5 * scales[i]).astype(bf16), (c6 * scales[i] * scales[i]).astype(bf16)

        def first(tile, rows, cols):
            tile = tile.astype(bf16)
            square[i, rows, cols] = tile
            inner[i, rows, cols] = plus_diag(near * low[i, rows, cols] + far * tile, rows, cols, c4)

        product(low[i], low[i], first)
        between()
    for i in range(2):
        near, far = (c3 * scales[i]).astype(bf16), scales[i] * scales[i]

        def second(tile, rows, cols):
            tile = (far * tile).astype(bf16) + near * low[i, rows, cols]
            outer[i, rows, cols] = plus_diag(tile, rows, cols, c2)

        product(square[i], inner[i], second)
    for i in (1, 0):
        near, far = c1 * scales[i], scales[i] * scales[i]

        def third(tile, rows, cols):
            tile = far * tile + near * low[i, rows, cols].astype(f32)
            inner[i, rows, cols] = plus_diag(tile, rows, cols, c0).astype(bf16)

        product(square[i], outer[i], third)


def precondition_kernel(
    live_ref, arrived_a, arrived_b, left_stats, right_stats, left_roots, right_roots, _, out,
    halves, stats, roots, results, grams, raws, applied, low, square, inner, outer, in_sems, out_sems,
):
    side = stats.shape[-1]
    entries = side * side
    f32, bf16 = jnp.float32, jnp.bfloat16
    grid = tiles(side)
    fetch = {}

    def get(name, source, target):
        fetch[name] = pltpu.make_async_copy(source, target, in_sems.at[len(fetch)])
        fetch[name].start()

    get("a0", arrived_a.at[:, 0], halves.at[0])
    for slot in range(1, MOST):
        get("a%d" % slot, arrived_a.at[:, slot], halves.at[slot])
        get("r%d" % slot, right_roots.at[0, 0, slot], roots.at[2 * slot - 1])
    for slot in range(1, MOST):
        get("l%d" % slot, left_roots.at[0, 0, slot], roots.at[2 * slot - 2])
    get("left", left_stats.at[0, 0, 0], stats.at[0])
    get("right", right_stats.at[0, 0, 0], stats.at[1])

    def block_of(slot):
        fetch["a%d" % slot].wait()
        front, back = halves[slot], arrived_b[:, slot]
        return jnp.concatenate([half.reshape(side, -1) for half in (front, back)], axis=1)

    def give(slot, low=0, high=arrived_a.shape[0], part=0):
        slabs = pl.ds(low, high - low)
        copy = pltpu.make_async_copy(results.at[slot, slabs], out.at[slabs, slot], out_sems.at[slot + part])
        copy.start()
        sent.append(copy)

    def put(number, rows, cols, tile):
        slabs = slice(rows.start // 16, rows.stop // 16)
        results[number, slabs, :, cols] = tile.reshape(ROWS // 16, 16, COLS)

    def power(tile_of):
        return total([jnp.square(tile_of(rows, cols)) for rows, cols in grid]) * (1.0 / entries)

    def graft(slot, out_power, parts=1):
        grad_power = power(lambda rows, cols: blocks[slot][rows, cols].astype(f32))
        scale = jnp.sqrt(grad_power) / jnp.sqrt(out_power + GRAFT_EPS)
        share = results.shape[1] // parts
        for part in range(parts):
            for rows, cols in grid:
                if rows.start // 16 // share == part:
                    put(slot, rows, cols, (raws[slot, rows, cols] * scale).astype(bf16))
            give(slot, part * share, (part + 1) * share, MOST * (part > 0) + max(part - 1, 0))

    def apply_right(slot, root):
        def use(tile, rows, cols):
            applied[slot, rows, cols] = tile.astype(bf16)

        product(blocks[slot], root, use)

    def apply_left(slot, root):
        squares = []

        def use(tile, rows, cols):
            raws[slot, rows, cols] = tile
            squares.append(tile * tile)

        product(root, applied[slot], use)
        return total(squares) * (1.0 / entries)

    blocks = [block_of(0)]
    grams[0] = mul(blocks[0], blocks[0], ((1,), (1,)))
    grams[1] = mul(blocks[0], blocks[0], ((0,), (0,)))
    for slot in range(1, MOST):
        blocks.append(block_of(slot))
        fetch["r%d" % slot].wait()
    for slot in range(1, MOST):
        apply_right(slot, roots[2 * slot - 1])
    for slot in range(1, MOST):
        fetch["l%d" % slot].wait()
    powers = [apply_left(slot, roots[2 * slot - 2]) for slot in range(1, MOST)]
    sent = []
    fetch["left"].wait()
    fetch["right"].wait()
    fill = iter(range(1, MOST))

    def between():
        for slot in fill:
            graft(slot, powers[slot - 1])
            break

    new_roots(live_ref[0] > 0, stats, grams, low, square, inner, outer, between)
    apply_right(0, inner[1])
    graft(0, apply_left(0, inner[0]), PARTS)
    for copy in sent:
        copy.wait()


def precondition(live, arrived, left_stats, right_stats, left_roots, right_roots, spare):
    owners, _, rows, width = arrived[0].shape
    side = left_stats.shape[-1]
    far = pl.BlockSpec(memory_space=HBM)
    return pl.pallas_call(
        precondition_kernel,
        out_shape=jax.ShapeDtypeStruct((owners, MOST, rows, side), jnp.bfloat16),
        in_specs=[pl.BlockSpec(memory_space=SMEM), far, pl.BlockSpec(memory_space=VMEM)] + [far] * 5,
        out_specs=far,
        scratch_shapes=[
            VMEM((MOST, owners, rows, width), jnp.bfloat16),
            VMEM((2, side, side), jnp.float32),
            VMEM((2 * MOST - 2, side, side), jnp.bfloat16),
            VMEM((MOST, owners, rows, side), jnp.bfloat16),
            VMEM((2, side, side), jnp.float32),
            VMEM((MOST, side, side), jnp.float32),
            VMEM((MOST, side, side), jnp.bfloat16),
            VMEM((2, side, side), jnp.bfloat16),
            VMEM((2, side, side), jnp.bfloat16),
            VMEM((2, side, side), jnp.bfloat16),
            VMEM((2, side, side), jnp.bfloat16),
            pltpu.SemaphoreType.DMA((3 * MOST,)),
            pltpu.SemaphoreType.DMA((MOST + PARTS - 1,)),
        ],
        compiler_params=pltpu.CompilerParams(vmem_limit_bytes=VMEM_MOST),
        cost_estimate=cost(14, side, 9 * side * side * 4),
        input_output_aliases={7: 0},
        name="precondition",
    )(live, *arrived, left_stats, right_stats, left_roots, right_roots, spare)


def stats_kernel(
    live_ref, front_ref, back_ref, lprev_ref, rprev_ref, left_ref, right_ref, lroot_ref, rroot_ref,
    stats, grams, low, square, inner, outer,
):
    side = lprev_ref.shape[-1]
    block = jnp.concatenate([front_ref[:, 0], back_ref[:, 0]], axis=-1).reshape(side, side)
    live = live_ref[pl.program_id(0)] > 0
    grams[0] = mul(block, block, ((1,), (1,)))
    grams[1] = mul(block, block, ((0,), (0,)))
    for rows, cols in tiles(side):
        left_ref[0, 0, 0, rows, cols] = blend(live, lprev_ref[0, 0, 0, rows, cols], grams[0, rows, cols])
        right_ref[0, 0, 0, rows, cols] = blend(live, rprev_ref[0, 0, 0, rows, cols], grams[1, rows, cols])

    @pl.when(pl.program_id(0) == 0)
    def _():
        stats[0] = lprev_ref[0, 0, 0]
        stats[1] = rprev_ref[0, 0, 0]
        new_roots(live, stats, grams, low, square, inner, outer, lambda: None)
        lroot_ref[0, 0] = inner[0]
        rroot_ref[0, 0] = inner[1]


def update_stats(live, arrived, left_stats, right_stats):
    owners, _, rows, _ = arrived[0].shape
    side = left_stats.shape[-1]
    at_slot = pl.BlockSpec((1, 1, 1, side, side), lambda s: (0, 0, s, 0, 0))
    of_first = pl.BlockSpec((1, 1, side, side), lambda s: (0, 0, 0, 0))
    shape = jax.ShapeDtypeStruct(left_stats.shape, jnp.float32)
    root = jax.ShapeDtypeStruct((1, 1, side, side), jnp.bfloat16)
    return pl.pallas_call(
        stats_kernel,
        grid=(MOST,),
        out_shape=[shape, shape, root, root],
        in_specs=[pl.BlockSpec(memory_space=SMEM)]
        + [pl.BlockSpec((owners, 1, rows, half.shape[3]), lambda s: (0, s, 0, 0)) for half in arrived]
        + [at_slot, at_slot],
        out_specs=[at_slot, at_slot, of_first, of_first],
        scratch_shapes=[
            VMEM((2, side, side), jnp.float32),
            VMEM((2, side, side), jnp.float32),
            VMEM((2, side, side), jnp.bfloat16),
            VMEM((2, side, side), jnp.bfloat16),
            VMEM((2, side, side), jnp.bfloat16),
            VMEM((2, side, side), jnp.bfloat16),
        ],
        compiler_params=pltpu.CompilerParams(vmem_limit_bytes=VMEM_MOST),
        cost_estimate=cost(2 * MOST + 6, side, 13 * side * side * 4),
        name="update_stats",
    )(live, *arrived, left_stats, right_stats)


def assemble_kernel(place_ref, back_ref, out_ref, sem):
    count = out_ref.shape[0]

    def start(b, carry):
        pltpu.make_async_copy(back_ref.at[place_ref[b]], out_ref.at[b], sem).start()
        return carry

    lax.fori_loop(0, count, start, 0, unroll=8)
    pltpu.make_async_copy(out_ref, out_ref, sem).wait()


def assemble(place, back):
    count = place.shape[0]
    rows, cols = back.shape[1:]
    return pl.pallas_call(
        assemble_kernel,
        out_shape=jax.ShapeDtypeStruct((count, rows, cols), jnp.bfloat16),
        in_specs=[pl.BlockSpec(memory_space=SMEM), pl.BlockSpec(memory_space=pl.ANY)],
        out_specs=pl.BlockSpec(memory_space=HBM),
        scratch_shapes=[pltpu.SemaphoreType.DMA(())],
        compiler_params=pltpu.CompilerParams(vmem_limit_bytes=VMEM_LIMIT),
        cost_estimate=cost(0, 0, 2 * count * rows * cols * 2),
        name="assemble",
    )(place, back)


def routing(owner, owners):
    ids = jnp.arange(owner.shape[0], dtype=jnp.int32)
    same = owner[:, None] == owner[None, :]
    slot = jnp.sum((same & (ids[None, :] < ids[:, None])).astype(jnp.int32), axis=1)
    place = owner * MOST + slot
    taken = place[None, :] == jnp.arange(owners * MOST, dtype=jnp.int32)[:, None]
    return place, 1 - jnp.sum(taken.astype(jnp.int32), axis=1)


def on_device(grads, owner_table, left_stats, right_stats, left_roots, right_roots):
    groups = lax.axis_size("rep")
    owners = lax.axis_size("fsdp")
    group_id = lax.axis_index("rep")
    owner_id = lax.axis_index("fsdp")
    local = grads[0]
    total_blocks, slab_rows, side = local.shape
    share = total_blocks // groups
    half = share // 2
    up = [(i, (i + 1) % groups) for i in range(groups)]
    down = [(i, (i - 1) % groups) for i in range(groups)]

    owner = lax.dynamic_slice(owner_table[:, 0], (group_id * share,), (share,), allow_negative_indices=False)
    place, empty = routing(owner, owners)
    own_count = jnp.sum((owner == owner_id).astype(jnp.int32))
    live = (jnp.arange(MOST, dtype=jnp.int32) < own_count).astype(jnp.int32)
    cut = side // SPLIT
    parts = ((0, cut), (cut, side - cut))

    def part(source, ahead, low, columns):
        start = ((group_id + ahead) & (groups - 1)) * share + low
        return lax.dynamic_slice(
            source, (start, 0, columns[0]), (half, slab_rows, columns[1]), allow_negative_indices=False
        )

    def send(pair):
        return lax.ppermute(pair[0], "rep", up), lax.ppermute(pair[1], "rep", down)

    def firsts(source, columns):
        return part(source, 2, 0, columns), part(source, 2, half, columns)

    def seconds(source, columns):
        return part(source, 1, half, columns), part(source, 3, 0, columns)

    def mids(source, columns):
        return part(source, 1, 0, columns), part(source, 3, half, columns)

    def owns(source, columns):
        return part(source, 0, 0, columns), part(source, 0, half, columns)

    first = firsts(local, parts[0])
    up1, down1 = send(first)
    later, _ = lax.optimization_barrier((local, first))
    second = seconds(later, parts[0])
    up2, down2 = send(second)
    later, _ = lax.optimization_barrier((later, second))
    own, mid = owns(later, parts[0]), mids(later, parts[0])
    third = mid[0] + up1, mid[1] + down1
    up3, down3 = send(third)
    later, _ = lax.optimization_barrier((later, third))
    pairs = zip(firsts(later, parts[1]), seconds(later, parts[1]))
    both = tuple(jnp.concatenate(pair) for pair in pairs)
    up12, down12 = send(both)
    outgoing_a = place_blocks(place, empty, (own[0], down2, up3), (own[1], up2, down3), 30)
    own, mid = owns(later, parts[1]), mids(later, parts[1])
    third = add_pairs(mid[0], up12, mid[1], down12, outgoing_a)
    up3, down3 = send(third)
    outgoing_b = place_blocks(place, empty, (own[0], down12, up3), (own[1], up12, down3))
    spare = spare_room((owners, MOST, slab_rows, side))
    arrived = [
        lax.all_to_all(
            outgoing.reshape(owners, MOST, slab_rows, -1), "fsdp", split_axis=0, concat_axis=0, tiled=True
        )
        for outgoing in (outgoing_a, outgoing_b)
    ]
    results = precondition(
        live, arrived, left_stats, right_stats, left_roots, right_roots, spare
    )
    returned = lax.all_to_all(results, "fsdp", split_axis=0, concat_axis=0, tiled=True)
    left_out, right_out, left_new, right_new = update_stats(live, arrived, left_stats, right_stats)
    preconditioned = assemble(place, returned.reshape(owners * MOST, slab_rows, side))
    return (
        preconditioned,
        left_out,
        right_out,
        left_new,
        right_new,
    )


def solution(mesh):
    in_specs = (
        P("rep", None, "fsdp", None),
        P(),
        P("rep", "fsdp", None, None, None),
        P("rep", "fsdp", None, None, None),
        P("rep", "fsdp", None, None, None),
        P("rep", "fsdp", None, None, None),
    )
    out_specs = (
        P("rep", "fsdp", None),
        P("rep", "fsdp", None, None, None),
        P("rep", "fsdp", None, None, None),
        P("rep", "fsdp", None, None),
        P("rep", "fsdp", None, None),
    )
    return jax.shard_map(
        on_device, mesh=mesh, in_specs=in_specs, out_specs=out_specs, check_vma=False
    )
```

```python
import functools

import jax
import jax.numpy as jnp
from jax import lax
from jax.experimental import pallas as pl
from jax.experimental.pallas import tpu as pltpu
from jax.sharding import PartitionSpec as P

DECAY_RATE = 0.9
ROOT_RIDGE = 1e-06
GRAFT_EPS = 1e-12
NORM_EPS = 1e-12
MOST = 3
SPLIT = 2

ROOT_POLY = (
    25.0 / 16.0,
    -5.0 / 16.0 - 3125.0 / 4096.0,
    3125.0 / 4096.0,
    -1250.0 / 4096.0,
    250.0 / 4096.0,
    -25.0 / 4096.0,
    1.0 / 4096.0,
)

VMEM_LIMIT = 40 * 1024 * 1024
VMEM_MOST = 52 * 1024 * 1024
VMEM_ALL = 60 * 1024 * 1024
VMEM_SMALL = 16 * 1024 * 1024
VMEM = pltpu.VMEM
HBM = pltpu.HBM
SMEM = pltpu.SMEM


def mul(left, right, dims=((1,), (0,))):
    return lax.dot_general(left, right, (dims, ((), ())), preferred_element_type=jnp.float32)


def blend(live, prev, gram):
    return jnp.where(live, DECAY_RATE * prev + (1.0 - DECAY_RATE) * gram, prev)


PIECE = 256
ROWS = 64
COLS = 128
PARTS = 4


def tiles(side):
    return [
        (slice(row, row + ROWS), slice(col, col + COLS))
        for row in range(0, side, ROWS)
        for col in range(0, side, COLS)
    ]


def product(left, right, use):
    side = left.shape[0]
    for row in range(0, side, PIECE):
        for col in range(0, side, PIECE):
            piece = mul(left[row : row + PIECE, :], right[:, col : col + PIECE])
            for r in range(0, PIECE, ROWS):
                for c in range(0, PIECE, COLS):
                    rows, cols = slice(row + r, row + r + ROWS), slice(col + c, col + c + COLS)
                    use(piece[r : r + ROWS, c : c + COLS], rows, cols)


def plus_diag(tile, rows, cols, value):
    if rows.start // COLS != cols.start // COLS:
        return tile
    row_ids = lax.broadcasted_iota(jnp.int32, tile.shape, 0) + rows.start
    col_ids = lax.broadcasted_iota(jnp.int32, tile.shape, 1) + cols.start
    return tile + jnp.where(row_ids == col_ids, value, 0.0).astype(tile.dtype)


def total(parts):
    return jnp.sum(functools.reduce(lambda x, y: x + y, parts), keepdims=True)


def cost(matmuls, side, nbytes):
    return pl.CostEstimate(flops=matmuls * 2 * side**3, bytes_accessed=nbytes, transcendentals=0)


def spare_room(shape):
    return pl.pallas_call(
        lambda room: None,
        out_shape=jax.ShapeDtypeStruct(shape, jnp.bfloat16),
        out_specs=pl.BlockSpec(memory_space=pl.ANY),
        compiler_params=pltpu.CompilerParams(vmem_limit_bytes=VMEM_ALL),
        name="spare_room",
    )()


def place_kernel(place_ref, empty_ref, *rest):
    (own_front, straight_front, last_front, own_back, straight_back, last_back), rest = rest[:6], rest[6:]
    out_ref, sums, zeros, sem = rest
    half = own_front.shape[0]
    zeros[...] = jnp.zeros_like(zeros)

    def blank(place, carry):
        @pl.when(empty_ref[place] > 0)
        def _():
            pltpu.make_async_copy(zeros, out_ref.at[place], sem).start()

        return carry

    def add(j, carry):
        for block, own, straight, last in (
            (j, own_front, straight_front, last_front),
            (half + j, own_back, straight_back, last_back),
        ):
            three = own[j], straight[straight.shape[0] - half + j], last[j]
            sums[block] = sum(term.astype(jnp.float32) for term in three).astype(jnp.bfloat16)
            pltpu.make_async_copy(sums.at[block], out_ref.at[place_ref[block]], sem).start()
        return carry

    lax.fori_loop(0, half, add, 0, unroll=4)
    lax.fori_loop(0, out_ref.shape[0], blank, 0, unroll=4)
    pltpu.make_async_copy(out_ref, out_ref, sem).wait()


def place_blocks(place, empty, front, back, weight=0):
    half, rows, cols = front[0].shape
    scalars = pl.BlockSpec(memory_space=SMEM)
    return pl.pallas_call(
        place_kernel,
        out_shape=jax.ShapeDtypeStruct((empty.shape[0], rows, cols), jnp.bfloat16),
        in_specs=[scalars] * 2 + [pl.BlockSpec(memory_space=VMEM)] * 6,
        out_specs=pl.BlockSpec(memory_space=HBM),
        scratch_shapes=[
            VMEM((2 * half, rows, cols), jnp.bfloat16),
            VMEM((rows, cols), jnp.bfloat16),
            pltpu.SemaphoreType.DMA(()),
        ],
        compiler_params=pltpu.CompilerParams(vmem_limit_bytes=VMEM_LIMIT),
        cost_estimate=cost(weight, 512, 8 * half * rows * cols * 2),
        name="place_blocks",
    )(place, empty, *front, *back)


def add_kernel(one_ref, two_ref, three_ref, four_ref, *rest):
    first_ref, second_ref = rest[-2:]

    def add(j, carry):
        first_ref[j] = one_ref[j] + two_ref[j]
        second_ref[j] = three_ref[j] + four_ref[j]
        return carry

    lax.fori_loop(0, first_ref.shape[0], add, 0, unroll=8)


def add_pairs(one, two, three, four, *after):
    near = pl.BlockSpec(memory_space=VMEM)
    shape = jax.ShapeDtypeStruct(one.shape, one.dtype)
    return pl.pallas_call(
        add_kernel,
        out_shape=[shape, shape],
        in_specs=[near] * 4 + [pl.BlockSpec(memory_space=pl.ANY)] * len(after),
        out_specs=[near, near],
        compiler_params=pltpu.CompilerParams(vmem_limit_bytes=VMEM_SMALL),
        cost_estimate=cost(800, 512, 2 * one.size),
        name="add_pairs",
    )(one, two, three, four, *after)


def new_roots(live, stats, grams, low, square, inner, outer, between):
    side = stats.shape[-1]
    f32, bf16 = jnp.float32, jnp.bfloat16
    c0, c1, c2, c3, c4, c5, c6 = ROOT_POLY
    keep = jnp.where(live, DECAY_RATE, 1.0)
    take = jnp.where(live, 1.0 - DECAY_RATE, 0.0)
    scales = []
    for i in range(2):
        squares = []
        for rows, cols in tiles(side):
            tile = keep * stats[i, rows, cols] + take * grams[i, rows, cols]
            tile = plus_diag(tile, rows, cols, ROOT_RIDGE)
            low[i, rows, cols] = tile.astype(bf16)
            squares.append(tile * tile)
        frob = side * jnp.sqrt(total(squares) * (1.0 / (side * side)) + NORM_EPS)
        scales.append(2.5 / frob)

    for i in range(2):
        near, far = (c5 * scales[i]).astype(bf16), (c6 * scales[i] * scales[i]).astype(bf16)

        def first(tile, rows, cols):
            tile = tile.astype(bf16)
            square[i, rows, cols] = tile
            inner[i, rows, cols] = plus_diag(near * low[i, rows, cols] + far * tile, rows, cols, c4)

        product(low[i], low[i], first)
        between()
    for i in range(2):
        near, far = (c3 * scales[i]).astype(bf16), scales[i] * scales[i]

        def second(tile, rows, cols):
            tile = (far * tile).astype(bf16) + near * low[i, rows, cols]
            outer[i, rows, cols] = plus_diag(tile, rows, cols, c2)

        product(square[i], inner[i], second)
    for i in (1, 0):
        near, far = c1 * scales[i], scales[i] * scales[i]

        def third(tile, rows, cols):
            tile = far * tile + near * low[i, rows, cols].astype(f32)
            inner[i, rows, cols] = plus_diag(tile, rows, cols, c0).astype(bf16)

        product(square[i], outer[i], third)


def precondition_kernel(
    live_ref, arrived_a, arrived_b, left_stats, right_stats, left_roots, right_roots, _, out,
    halves, stats, roots, results, grams, raws, applied, low, square, inner, outer, in_sems, out_sems,
):
    side = stats.shape[-1]
    entries = side * side
    f32, bf16 = jnp.float32, jnp.bfloat16
    grid = tiles(side)
    fetch = {}

    def get(name, source, target):
        fetch[name] = pltpu.make_async_copy(source, target, in_sems.at[len(fetch)])
        fetch[name].start()

    get("a0", arrived_a.at[:, 0], halves.at[0])
    for slot in range(1, MOST):
        get("a%d" % slot, arrived_a.at[:, slot], halves.at[slot])
        get("r%d" % slot, right_roots.at[0, 0, slot], roots.at[2 * slot - 1])
    for slot in range(1, MOST):
        get("l%d" % slot, left_roots.at[0, 0, slot], roots.at[2 * slot - 2])
    get("left", left_stats.at[0, 0, 0], stats.at[0])
    get("right", right_stats.at[0, 0, 0], stats.at[1])

    def block_of(slot):
        fetch["a%d" % slot].wait()
        front, back = halves[slot], arrived_b[:, slot]
        return jnp.concatenate([half.reshape(side, -1) for half in (front, back)], axis=1)

    def give(slot, low=0, high=arrived_a.shape[0], part=0):
        slabs = pl.ds(low, high - low)
        copy = pltpu.make_async_copy(results.at[slot, slabs], out.at[slabs, slot], out_sems.at[slot + part])
        copy.start()
        sent.append(copy)

    def put(number, rows, cols, tile):
        slabs = slice(rows.start // 16, rows.stop // 16)
        results[number, slabs, :, cols] = tile.reshape(ROWS // 16, 16, COLS)

    def power(tile_of):
        return total([jnp.square(tile_of(rows, cols)) for rows, cols in grid]) * (1.0 / entries)

    def graft(slot, out_power, parts=1):
        grad_power = power(lambda rows, cols: blocks[slot][rows, cols].astype(f32))
        scale = jnp.sqrt(grad_power) / jnp.sqrt(out_power + GRAFT_EPS)
        share = results.shape[1] // parts
        for part in range(parts):
            for rows, cols in grid:
                if rows.start // 16 // share == part:
                    put(slot, rows, cols, (raws[slot, rows, cols] * scale).astype(bf16))
            give(slot, part * share, (part + 1) * share, MOST * (part > 0) + max(part - 1, 0))

    def apply_right(slot, root):
        def use(tile, rows, cols):
            applied[slot, rows, cols] = tile.astype(bf16)

        product(blocks[slot], root, use)

    def apply_left(slot, root):
        squares = []

        def use(tile, rows, cols):
            raws[slot, rows, cols] = tile
            squares.append(tile * tile)

        product(root, applied[slot], use)
        return total(squares) * (1.0 / entries)

    blocks = [block_of(0)]
    grams[0] = mul(blocks[0], blocks[0], ((1,), (1,)))
    grams[1] = mul(blocks[0], blocks[0], ((0,), (0,)))
    for slot in range(1, MOST):
        blocks.append(block_of(slot))
        fetch["r%d" % slot].wait()
    for slot in range(1, MOST):
        apply_right(slot, roots[2 * slot - 1])
    for slot in range(1, MOST):
        fetch["l%d" % slot].wait()
    powers = [apply_left(slot, roots[2 * slot - 2]) for slot in range(1, MOST)]
    sent = []
    fetch["left"].wait()
    fetch["right"].wait()
    fill = iter(range(1, MOST))

    def between():
        for slot in fill:
            graft(slot, powers[slot - 1])
            break

    new_roots(live_ref[0] > 0, stats, grams, low, square, inner, outer, between)
    apply_right(0, inner[1])
    graft(0, apply_left(0, inner[0]), PARTS)
    for copy in sent:
        copy.wait()


def precondition(live, arrived, left_stats, right_stats, left_roots, right_roots, spare):
    owners, _, rows, width = arrived[0].shape
    side = left_stats.shape[-1]
    far = pl.BlockSpec(memory_space=HBM)
    return pl.pallas_call(
        precondition_kernel,
        out_shape=jax.ShapeDtypeStruct((owners, MOST, rows, side), jnp.bfloat16),
        in_specs=[pl.BlockSpec(memory_space=SMEM), far, pl.BlockSpec(memory_space=VMEM)] + [far] * 5,
        out_specs=far,
        scratch_shapes=[
            VMEM((MOST, owners, rows, width), jnp.bfloat16),
            VMEM((2, side, side), jnp.float32),
            VMEM((2 * MOST - 2, side, side), jnp.bfloat16),
            VMEM((MOST, owners, rows, side), jnp.bfloat16),
            VMEM((2, side, side), jnp.float32),
            VMEM((MOST, side, side), jnp.float32),
            VMEM((MOST, side, side), jnp.bfloat16),
            VMEM((2, side, side), jnp.bfloat16),
            VMEM((2, side, side), jnp.bfloat16),
            VMEM((2, side, side), jnp.bfloat16),
            VMEM((2, side, side), jnp.bfloat16),
            pltpu.SemaphoreType.DMA((3 * MOST,)),
            pltpu.SemaphoreType.DMA((MOST + PARTS - 1,)),
        ],
        compiler_params=pltpu.CompilerParams(vmem_limit_bytes=VMEM_MOST),
        cost_estimate=cost(14, side, 9 * side * side * 4),
        input_output_aliases={7: 0},
        name="precondition",
    )(live, *arrived, left_stats, right_stats, left_roots, right_roots, spare)


def stats_kernel(
    live_ref, front_ref, back_ref, lprev_ref, rprev_ref, left_ref, right_ref, lroot_ref, rroot_ref,
    stats, grams, low, square, inner, outer,
):
    side = lprev_ref.shape[-1]
    block = jnp.concatenate([front_ref[:, 0], back_ref[:, 0]], axis=-1).reshape(side, side)
    live = live_ref[pl.program_id(0)] > 0
    grams[0] = mul(block, block, ((1,), (1,)))
    grams[1] = mul(block, block, ((0,), (0,)))
    for rows, cols in tiles(side):
        left_ref[0, 0, 0, rows, cols] = blend(live, lprev_ref[0, 0, 0, rows, cols], grams[0, rows, cols])
        right_ref[0, 0, 0, rows, cols] = blend(live, rprev_ref[0, 0, 0, rows, cols], grams[1, rows, cols])

    @pl.when(pl.program_id(0) == 0)
    def _():
        stats[0] = lprev_ref[0, 0, 0]
        stats[1] = rprev_ref[0, 0, 0]
        new_roots(live, stats, grams, low, square, inner, outer, lambda: None)
        lroot_ref[0, 0] = inner[0]
        rroot_ref[0, 0] = inner[1]


def update_stats(live, arrived, left_stats, right_stats):
    owners, _, rows, _ = arrived[0].shape
    side = left_stats.shape[-1]
    at_slot = pl.BlockSpec((1, 1, 1, side, side), lambda s: (0, 0, s, 0, 0))
    of_first = pl.BlockSpec((1, 1, side, side), lambda s: (0, 0, 0, 0))
    shape = jax.ShapeDtypeStruct(left_stats.shape, jnp.float32)
    root = jax.ShapeDtypeStruct((1, 1, side, side), jnp.bfloat16)
    return pl.pallas_call(
        stats_kernel,
        grid=(MOST,),
        out_shape=[shape, shape, root, root],
        in_specs=[pl.BlockSpec(memory_space=SMEM)]
        + [pl.BlockSpec((owners, 1, rows, half.shape[3]), lambda s: (0, s, 0, 0)) for half in arrived]
        + [at_slot, at_slot],
        out_specs=[at_slot, at_slot, of_first, of_first],
        scratch_shapes=[
            VMEM((2, side, side), jnp.float32),
            VMEM((2, side, side), jnp.float32),
            VMEM((2, side, side), jnp.bfloat16),
            VMEM((2, side, side), jnp.bfloat16),
            VMEM((2, side, side), jnp.bfloat16),
            VMEM((2, side, side), jnp.bfloat16),
        ],
        compiler_params=pltpu.CompilerParams(vmem_limit_bytes=VMEM_MOST),
        cost_estimate=cost(2 * MOST + 6, side, 13 * side * side * 4),
        name="update_stats",
    )(live, *arrived, left_stats, right_stats)


def assemble_kernel(place_ref, back_ref, out_ref, sem):
    count = out_ref.shape[0]

    def start(b, carry):
        pltpu.make_async_copy(back_ref.at[place_ref[b]], out_ref.at[b], sem).start()
        return carry

    lax.fori_loop(0, count, start, 0, unroll=8)
    pltpu.make_async_copy(out_ref, out_ref, sem).wait()


def assemble(place, back):
    count = place.shape[0]
    rows, cols = back.shape[1:]
    return pl.pallas_call(
        assemble_kernel,
        out_shape=jax.ShapeDtypeStruct((count, rows, cols), jnp.bfloat16),
        in_specs=[pl.BlockSpec(memory_space=SMEM), pl.BlockSpec(memory_space=pl.ANY)],
        out_specs=pl.BlockSpec(memory_space=HBM),
        scratch_shapes=[pltpu.SemaphoreType.DMA(())],
        compiler_params=pltpu.CompilerParams(vmem_limit_bytes=VMEM_LIMIT),
        cost_estimate=cost(0, 0, 2 * count * rows * cols * 2),
        name="assemble",
    )(place, back)


def routing(owner, owners):
    ids = jnp.arange(owner.shape[0], dtype=jnp.int32)
    same = owner[:, None] == owner[None, :]
    slot = jnp.sum((same & (ids[None, :] < ids[:, None])).astype(jnp.int32), axis=1)
    place = owner * MOST + slot
    taken = place[None, :] == jnp.arange(owners * MOST, dtype=jnp.int32)[:, None]
    return place, 1 - jnp.sum(taken.astype(jnp.int32), axis=1)


def on_device(grads, owner_table, left_stats, right_stats, left_roots, right_roots):
    groups = lax.axis_size("rep")
    owners = lax.axis_size("fsdp")
    group_id = lax.axis_index("rep")
    owner_id = lax.axis_index("fsdp")
    local = grads[0]
    total_blocks, slab_rows, side = local.shape
    share = total_blocks // groups
    half = share // 2
    up = [(i, (i + 1) % groups) for i in range(groups)]
    down = [(i, (i - 1) % groups) for i in range(groups)]

    owner = lax.dynamic_slice(owner_table[:, 0], (group_id * share,), (share,), allow_negative_indices=False)
    place, empty = routing(owner, owners)
    own_count = jnp.sum((owner == owner_id).astype(jnp.int32))
    live = (jnp.arange(MOST, dtype=jnp.int32) < own_count).astype(jnp.int32)
    cut = side // SPLIT
    parts = ((0, cut), (cut, side - cut))

    def part(source, ahead, low, columns):
        start = ((group_id + ahead) & (groups - 1)) * share + low
        return lax.dynamic_slice(
            source, (start, 0, columns[0]), (half, slab_rows, columns[1]), allow_negative_indices=False
        )

    def send(pair):
        return lax.ppermute(pair[0], "rep", up), lax.ppermute(pair[1], "rep", down)

    def firsts(source, columns):
        return part(source, 2, 0, columns), part(source, 2, half, columns)

    def seconds(source, columns):
        return part(source, 1, half, columns), part(source, 3, 0, columns)

    def mids(source, columns):
        return part(source, 1, 0, columns), part(source, 3, half, columns)

    def owns(source, columns):
        return part(source, 0, 0, columns), part(source, 0, half, columns)

    first = firsts(local, parts[0])
    up1, down1 = send(first)
    later, _ = lax.optimization_barrier((local, first))
    second = seconds(later, parts[0])
    up2, down2 = send(second)
    later, _ = lax.optimization_barrier((later, second))
    own, mid = lax.optimization_barrier((owns(later, parts[0]), mids(later, parts[0])))
    third = mid[0] + up1, mid[1] + down1
    up3, down3 = send(third)
    later, _ = lax.optimization_barrier((later, third))
    pairs = zip(firsts(later, parts[1]), seconds(later, parts[1]))
    both = tuple(jnp.concatenate(pair) for pair in pairs)
    up12, down12 = send(both)
    outgoing_a = place_blocks(place, empty, (own[0], down2, up3), (own[1], up2, down3), 30)
    own, mid = owns(later, parts[1]), mids(later, parts[1])
    third = add_pairs(mid[0], up12, mid[1], down12, outgoing_a)
    up3, down3 = send(third)
    outgoing_b = place_blocks(place, empty, (own[0], down12, up3), (own[1], up12, down3))
    spare = spare_room((owners, MOST, slab_rows, side))
    arrived = [
        lax.all_to_all(
            outgoing.reshape(owners, MOST, slab_rows, -1), "fsdp", split_axis=0, concat_axis=0, tiled=True
        )
        for outgoing in (outgoing_a, outgoing_b)
    ]
    results = precondition(
        live, arrived, left_stats, right_stats, left_roots, right_roots, spare
    )
    returned = lax.all_to_all(results, "fsdp", split_axis=0, concat_axis=0, tiled=True)
    left_out, right_out, left_new, right_new = update_stats(live, arrived, left_stats, right_stats)
    preconditioned = assemble(place, returned.reshape(owners * MOST, slab_rows, side))
    return (
        preconditioned,
        left_out,
        right_out,
        left_new,
        right_new,
    )


def solution(mesh):
    in_specs = (
        P("rep", None, "fsdp", None),
        P(),
        P("rep", "fsdp", None, None, None),
        P("rep", "fsdp", None, None, None),
        P("rep", "fsdp", None, None, None),
        P("rep", "fsdp", None, None, None),
    )
    out_specs = (
        P("rep", "fsdp", None),
        P("rep", "fsdp", None, None, None),
        P("rep", "fsdp", None, None, None),
        P("rep", "fsdp", None, None),
        P("rep", "fsdp", None, None),
    )
    return jax.shard_map(
        on_device, mesh=mesh, in_specs=in_specs, out_specs=out_specs, check_vma=False
    )
```

```python
import functools

import jax
import jax.numpy as jnp
from jax import lax
from jax.experimental import pallas as pl
from jax.experimental.pallas import tpu as pltpu
from jax.sharding import PartitionSpec as P

DECAY_RATE = 0.9
ROOT_RIDGE = 1e-06
GRAFT_EPS = 1e-12
NORM_EPS = 1e-12
MOST = 3
SPLIT = 2

ROOT_POLY = (
    25.0 / 16.0,
    -5.0 / 16.0 - 3125.0 / 4096.0,
    3125.0 / 4096.0,
    -1250.0 / 4096.0,
    250.0 / 4096.0,
    -25.0 / 4096.0,
    1.0 / 4096.0,
)

VMEM_LIMIT = 40 * 1024 * 1024
VMEM_MOST = 52 * 1024 * 1024
VMEM_ALL = 60 * 1024 * 1024
VMEM_SMALL = 16 * 1024 * 1024
VMEM = pltpu.VMEM
HBM = pltpu.HBM
SMEM = pltpu.SMEM


def mul(left, right, dims=((1,), (0,))):
    return lax.dot_general(left, right, (dims, ((), ())), preferred_element_type=jnp.float32)


def blend(live, prev, gram):
    return jnp.where(live, DECAY_RATE * prev + (1.0 - DECAY_RATE) * gram, prev)


PIECE = 256
ROWS = 64
COLS = 128
PARTS = 4


def tiles(side):
    return [
        (slice(row, row + ROWS), slice(col, col + COLS))
        for row in range(0, side, ROWS)
        for col in range(0, side, COLS)
    ]


def product(left, right, use):
    side = left.shape[0]
    for row in range(0, side, PIECE):
        for col in range(0, side, PIECE):
            piece = mul(left[row : row + PIECE, :], right[:, col : col + PIECE])
            for r in range(0, PIECE, ROWS):
                for c in range(0, PIECE, COLS):
                    rows, cols = slice(row + r, row + r + ROWS), slice(col + c, col + c + COLS)
                    use(piece[r : r + ROWS, c : c + COLS], rows, cols)


def plus_diag(tile, rows, cols, value):
    if rows.start // COLS != cols.start // COLS:
        return tile
    row_ids = lax.broadcasted_iota(jnp.int32, tile.shape, 0) + rows.start
    col_ids = lax.broadcasted_iota(jnp.int32, tile.shape, 1) + cols.start
    return tile + jnp.where(row_ids == col_ids, value, 0.0).astype(tile.dtype)


def total(parts):
    return jnp.sum(functools.reduce(lambda x, y: x + y, parts), keepdims=True)


def cost(matmuls, side, nbytes):
    return pl.CostEstimate(flops=matmuls * 2 * side**3, bytes_accessed=nbytes, transcendentals=0)


def spare_room(shape):
    return pl.pallas_call(
        lambda room: None,
        out_shape=jax.ShapeDtypeStruct(shape, jnp.bfloat16),
        out_specs=pl.BlockSpec(memory_space=pl.ANY),
        compiler_params=pltpu.CompilerParams(vmem_limit_bytes=VMEM_ALL),
        name="spare_room",
    )()


def place_kernel(place_ref, empty_ref, *rest):
    (own_front, straight_front, last_front, own_back, straight_back, last_back), rest = rest[:6], rest[6:]
    out_ref, sums, zeros, sem = rest
    half = own_front.shape[0]
    zeros[...] = jnp.zeros_like(zeros)

    def blank(number, carry):
        pltpu.make_async_copy(zeros, out_ref.at[empty_ref[number]], sem).start()
        return carry

    lax.fori_loop(0, empty_ref.shape[0], blank, 0, unroll=8)

    def add(j, carry):
        for block, own, straight, last in (
            (j, own_front, straight_front, last_front),
            (half + j, own_back, straight_back, last_back),
        ):
            three = own[j], straight[straight.shape[0] - half + j], last[j]
            sums[block] = sum(term.astype(jnp.float32) for term in three).astype(jnp.bfloat16)
            pltpu.make_async_copy(sums.at[block], out_ref.at[place_ref[block]], sem).start()
        return carry

    lax.fori_loop(0, half, add, 0, unroll=4)
    pltpu.make_async_copy(out_ref, out_ref, sem).wait()


def place_blocks(place, empty, front, back, weight=0):
    half, rows, cols = front[0].shape
    scalars = pl.BlockSpec(memory_space=SMEM)
    return pl.pallas_call(
        place_kernel,
        out_shape=jax.ShapeDtypeStruct((2 * half + empty.shape[0], rows, cols), jnp.bfloat16),
        in_specs=[scalars] * 2 + [pl.BlockSpec(memory_space=VMEM)] * 6,
        out_specs=pl.BlockSpec(memory_space=HBM),
        scratch_shapes=[
            VMEM((2 * half, rows, cols), jnp.bfloat16),
            VMEM((rows, cols), jnp.bfloat16),
            pltpu.SemaphoreType.DMA(()),
        ],
        compiler_params=pltpu.CompilerParams(vmem_limit_bytes=VMEM_LIMIT),
        cost_estimate=cost(weight, 512, 8 * half * rows * cols * 2),
        name="place_blocks",
    )(place, empty, *front, *back)


def add_kernel(one_ref, two_ref, three_ref, four_ref, *rest):
    first_ref, second_ref = rest[-2:]

    def add(j, carry):
        first_ref[j] = one_ref[j] + two_ref[j]
        second_ref[j] = three_ref[j] + four_ref[j]
        return carry

    lax.fori_loop(0, first_ref.shape[0], add, 0, unroll=8)


def add_pairs(one, two, three, four, *after):
    near = pl.BlockSpec(memory_space=VMEM)
    shape = jax.ShapeDtypeStruct(one.shape, one.dtype)
    return pl.pallas_call(
        add_kernel,
        out_shape=[shape, shape],
        in_specs=[near] * 4 + [pl.BlockSpec(memory_space=pl.ANY)] * len(after),
        out_specs=[near, near],
        compiler_params=pltpu.CompilerParams(vmem_limit_bytes=VMEM_SMALL),
        cost_estimate=cost(800, 512, 2 * one.size),
        name="add_pairs",
    )(one, two, three, four, *after)


def new_roots(live, stats, grams, low, square, inner, outer, between):
    side = stats.shape[-1]
    f32, bf16 = jnp.float32, jnp.bfloat16
    c0, c1, c2, c3, c4, c5, c6 = ROOT_POLY
    keep = jnp.where(live, DECAY_RATE, 1.0)
    take = jnp.where(live, 1.0 - DECAY_RATE, 0.0)
    scales = []
    for i in range(2):
        squares = []
        for rows, cols in tiles(side):
            tile = keep * stats[i, rows, cols] + take * grams[i, rows, cols]
            tile = plus_diag(tile, rows, cols, ROOT_RIDGE)
            low[i, rows, cols] = tile.astype(bf16)
            squares.append(tile * tile)
        frob = side * jnp.sqrt(total(squares) * (1.0 / (side * side)) + NORM_EPS)
        scales.append(2.5 / frob)

    for i in range(2):
        near, far = (c5 * scales[i]).astype(bf16), (c6 * scales[i] * scales[i]).astype(bf16)

        def first(tile, rows, cols):
            tile = tile.astype(bf16)
            square[i, rows, cols] = tile
            inner[i, rows, cols] = plus_diag(near * low[i, rows, cols] + far * tile, rows, cols, c4)

        product(low[i], low[i], first)
        between()
    for i in range(2):
        near, far = (c3 * scales[i]).astype(bf16), scales[i] * scales[i]

        def second(tile, rows, cols):
            tile = (far * tile).astype(bf16) + near * low[i, rows, cols]
            outer[i, rows, cols] = plus_diag(tile, rows, cols, c2)

        product(square[i], inner[i], second)
    for i in (1, 0):
        near, far = c1 * scales[i], scales[i] * scales[i]

        def third(tile, rows, cols):
            tile = far * tile + near * low[i, rows, cols].astype(f32)
            inner[i, rows, cols] = plus_diag(tile, rows, cols, c0).astype(bf16)

        product(square[i], outer[i], third)


def precondition_kernel(
    live_ref, arrived_a, arrived_b, left_stats, right_stats, left_roots, right_roots, _, out,
    halves, stats, roots, results, grams, raws, applied, low, square, inner, outer, in_sems, out_sems,
):
    side = stats.shape[-1]
    entries = side * side
    f32, bf16 = jnp.float32, jnp.bfloat16
    grid = tiles(side)
    fetch = {}

    def get(name, source, target):
        fetch[name] = pltpu.make_async_copy(source, target, in_sems.at[len(fetch)])
        fetch[name].start()

    get("a0", arrived_a.at[:, 0], halves.at[0])
    for slot in range(1, MOST):
        get("a%d" % slot, arrived_a.at[:, slot], halves.at[slot])
        get("r%d" % slot, right_roots.at[0, 0, slot], roots.at[2 * slot - 1])
    for slot in range(1, MOST):
        get("l%d" % slot, left_roots.at[0, 0, slot], roots.at[2 * slot - 2])
    get("left", left_stats.at[0, 0, 0], stats.at[0])
    get("right", right_stats.at[0, 0, 0], stats.at[1])

    def block_of(slot):
        fetch["a%d" % slot].wait()
        front, back = halves[slot], arrived_b[:, slot]
        return jnp.concatenate([half.reshape(side, -1) for half in (front, back)], axis=1)

    def give(slot, low=0, high=arrived_a.shape[0], part=0):
        slabs = pl.ds(low, high - low)
        copy = pltpu.make_async_copy(results.at[slot, slabs], out.at[slabs, slot], out_sems.at[slot + part])
        copy.start()
        sent.append(copy)

    def put(number, rows, cols, tile):
        slabs = slice(rows.start // 16, rows.stop // 16)
        results[number, slabs, :, cols] = tile.reshape(ROWS // 16, 16, COLS)

    def power(tile_of):
        return total([jnp.square(tile_of(rows, cols)) for rows, cols in grid]) * (1.0 / entries)

    def graft(slot, out_power, parts=1):
        grad_power = power(lambda rows, cols: blocks[slot][rows, cols].astype(f32))
        scale = jnp.sqrt(grad_power) / jnp.sqrt(out_power + GRAFT_EPS)
        share = results.shape[1] // parts
        for part in range(parts):
            for rows, cols in grid:
                if rows.start // 16 // share == part:
                    put(slot, rows, cols, (raws[slot, rows, cols] * scale).astype(bf16))
            give(slot, part * share, (part + 1) * share, MOST * (part > 0) + max(part - 1, 0))

    def apply_right(slot, root):
        def use(tile, rows, cols):
            applied[slot, rows, cols] = tile.astype(bf16)

        product(blocks[slot], root, use)

    def apply_left(slot, root):
        squares = []

        def use(tile, rows, cols):
            raws[slot, rows, cols] = tile
            squares.append(tile * tile)

        product(root, applied[slot], use)
        return total(squares) * (1.0 / entries)

    blocks = [block_of(0)]
    grams[0] = mul(blocks[0], blocks[0], ((1,), (1,)))
    grams[1] = mul(blocks[0], blocks[0], ((0,), (0,)))
    for slot in range(1, MOST):
        blocks.append(block_of(slot))
        fetch["r%d" % slot].wait()
    for slot in range(1, MOST):
        apply_right(slot, roots[2 * slot - 1])
    for slot in range(1, MOST):
        fetch["l%d" % slot].wait()
    powers = [apply_left(slot, roots[2 * slot - 2]) for slot in range(1, MOST)]
    sent = []
    fetch["left"].wait()
    fetch["right"].wait()
    fill = iter(range(1, MOST))

    def between():
        for slot in fill:
            graft(slot, powers[slot - 1])
            break

    new_roots(live_ref[0] > 0, stats, grams, low, square, inner, outer, between)
    apply_right(0, inner[1])
    graft(0, apply_left(0, inner[0]), PARTS)
    for copy in sent:
        copy.wait()


def precondition(live, arrived, left_stats, right_stats, left_roots, right_roots, spare):
    owners, _, rows, width = arrived[0].shape
    side = left_stats.shape[-1]
    far = pl.BlockSpec(memory_space=HBM)
    return pl.pallas_call(
        precondition_kernel,
        out_shape=jax.ShapeDtypeStruct((owners, MOST, rows, side), jnp.bfloat16),
        in_specs=[pl.BlockSpec(memory_space=SMEM), far, pl.BlockSpec(memory_space=VMEM)] + [far] * 5,
        out_specs=far,
        scratch_shapes=[
            VMEM((MOST, owners, rows, width), jnp.bfloat16),
            VMEM((2, side, side), jnp.float32),
            VMEM((2 * MOST - 2, side, side), jnp.bfloat16),
            VMEM((MOST, owners, rows, side), jnp.bfloat16),
            VMEM((2, side, side), jnp.float32),
            VMEM((MOST, side, side), jnp.float32),
            VMEM((MOST, side, side), jnp.bfloat16),
            VMEM((2, side, side), jnp.bfloat16),
            VMEM((2, side, side), jnp.bfloat16),
            VMEM((2, side, side), jnp.bfloat16),
            VMEM((2, side, side), jnp.bfloat16),
            pltpu.SemaphoreType.DMA((3 * MOST,)),
            pltpu.SemaphoreType.DMA((MOST + PARTS - 1,)),
        ],
        compiler_params=pltpu.CompilerParams(vmem_limit_bytes=VMEM_MOST),
        cost_estimate=cost(14, side, 9 * side * side * 4),
        input_output_aliases={7: 0},
        name="precondition",
    )(live, *arrived, left_stats, right_stats, left_roots, right_roots, spare)


def stats_kernel(
    live_ref, front_ref, back_ref, lprev_ref, rprev_ref, left_ref, right_ref, lroot_ref, rroot_ref,
    stats, grams, low, square, inner, outer,
):
    side = lprev_ref.shape[-1]
    block = jnp.concatenate([front_ref[:, 0], back_ref[:, 0]], axis=-1).reshape(side, side)
    live = live_ref[pl.program_id(0)] > 0
    grams[0] = mul(block, block, ((1,), (1,)))
    grams[1] = mul(block, block, ((0,), (0,)))
    for rows, cols in tiles(side):
        left_ref[0, 0, 0, rows, cols] = blend(live, lprev_ref[0, 0, 0, rows, cols], grams[0, rows, cols])
        right_ref[0, 0, 0, rows, cols] = blend(live, rprev_ref[0, 0, 0, rows, cols], grams[1, rows, cols])

    @pl.when(pl.program_id(0) == 0)
    def _():
        stats[0] = lprev_ref[0, 0, 0]
        stats[1] = rprev_ref[0, 0, 0]
        new_roots(live, stats, grams, low, square, inner, outer, lambda: None)
        lroot_ref[0, 0] = inner[0]
        rroot_ref[0, 0] = inner[1]


def update_stats(live, arrived, left_stats, right_stats):
    owners, _, rows, _ = arrived[0].shape
    side = left_stats.shape[-1]
    at_slot = pl.BlockSpec((1, 1, 1, side, side), lambda s: (0, 0, s, 0, 0))
    of_first = pl.BlockSpec((1, 1, side, side), lambda s: (0, 0, 0, 0))
    shape = jax.ShapeDtypeStruct(left_stats.shape, jnp.float32)
    root = jax.ShapeDtypeStruct((1, 1, side, side), jnp.bfloat16)
    return pl.pallas_call(
        stats_kernel,
        grid=(MOST,),
        out_shape=[shape, shape, root, root],
        in_specs=[pl.BlockSpec(memory_space=SMEM)]
        + [pl.BlockSpec((owners, 1, rows, half.shape[3]), lambda s: (0, s, 0, 0)) for half in arrived]
        + [at_slot, at_slot],
        out_specs=[at_slot, at_slot, of_first, of_first],
        scratch_shapes=[
            VMEM((2, side, side), jnp.float32),
            VMEM((2, side, side), jnp.float32),
            VMEM((2, side, side), jnp.bfloat16),
            VMEM((2, side, side), jnp.bfloat16),
            VMEM((2, side, side), jnp.bfloat16),
            VMEM((2, side, side), jnp.bfloat16),
        ],
        compiler_params=pltpu.CompilerParams(vmem_limit_bytes=VMEM_MOST),
        cost_estimate=cost(2 * MOST + 6, side, 13 * side * side * 4),
        name="update_stats",
    )(live, *arrived, left_stats, right_stats)


def assemble_kernel(place_ref, back_ref, out_ref, sem):
    count = out_ref.shape[0]

    def start(b, carry):
        pltpu.make_async_copy(back_ref.at[place_ref[b]], out_ref.at[b], sem).start()
        return carry

    lax.fori_loop(0, count, start, 0, unroll=8)
    pltpu.make_async_copy(out_ref, out_ref, sem).wait()


def assemble(place, back):
    count = place.shape[0]
    rows, cols = back.shape[1:]
    return pl.pallas_call(
        assemble_kernel,
        out_shape=jax.ShapeDtypeStruct((count, rows, cols), jnp.bfloat16),
        in_specs=[pl.BlockSpec(memory_space=SMEM), pl.BlockSpec(memory_space=pl.ANY)],
        out_specs=pl.BlockSpec(memory_space=HBM),
        scratch_shapes=[pltpu.SemaphoreType.DMA(())],
        compiler_params=pltpu.CompilerParams(vmem_limit_bytes=VMEM_LIMIT),
        cost_estimate=cost(0, 0, 2 * count * rows * cols * 2),
        name="assemble",
    )(place, back)


def routing(owner, owners):
    ids = jnp.arange(owner.shape[0], dtype=jnp.int32)
    same = owner[:, None] == owner[None, :]
    slot = jnp.sum((same & (ids[None, :] < ids[:, None])).astype(jnp.int32), axis=1)
    place = owner * MOST + slot
    taken = place[None, :] == jnp.arange(owners * MOST, dtype=jnp.int32)[:, None]
    spots = jnp.arange(owners * MOST, dtype=jnp.int32)
    free = 1 - jnp.sum(taken.astype(jnp.int32), axis=1)
    before = jnp.sum(jnp.where(spots[None, :] < spots[:, None], free[None, :], 0), axis=1)
    numbers = jnp.arange(owners * MOST - owner.shape[0], dtype=jnp.int32)
    listed = (before[None, :] == numbers[:, None]) & (free[None, :] > 0)
    return place, jnp.sum(jnp.where(listed, spots[None, :], 0), axis=1)


def on_device(grads, owner_table, left_stats, right_stats, left_roots, right_roots):
    groups = lax.axis_size("rep")
    owners = lax.axis_size("fsdp")
    group_id = lax.axis_index("rep")
    owner_id = lax.axis_index("fsdp")
    local = grads[0]
    total_blocks, slab_rows, side = local.shape
    share = total_blocks // groups
    half = share // 2
    up = [(i, (i + 1) % groups) for i in range(groups)]
    down = [(i, (i - 1) % groups) for i in range(groups)]

    owner = lax.dynamic_slice(owner_table[:, 0], (group_id * share,), (share,), allow_negative_indices=False)
    place, empty = routing(owner, owners)
    own_count = jnp.sum((owner == owner_id).astype(jnp.int32))
    live = (jnp.arange(MOST, dtype=jnp.int32) < own_count).astype(jnp.int32)
    cut = side // SPLIT
    parts = ((0, cut), (cut, side - cut))

    def part(source, ahead, low, columns):
        start = ((group_id + ahead) & (groups - 1)) * share + low
        return lax.dynamic_slice(
            source, (start, 0, columns[0]), (half, slab_rows, columns[1]), allow_negative_indices=False
        )

    def send(pair):
        return lax.ppermute(pair[0], "rep", up), lax.ppermute(pair[1], "rep", down)

    def firsts(source, columns):
        return part(source, 2, 0, columns), part(source, 2, half, columns)

    def seconds(source, columns):
        return part(source, 1, half, columns), part(source, 3, 0, columns)

    def mids(source, columns):
        return part(source, 1, 0, columns), part(source, 3, half, columns)

    def owns(source, columns):
        return part(source, 0, 0, columns), part(source, 0, half, columns)

    first = firsts(local, parts[0])
    up1, down1 = send(first)
    later, _ = lax.optimization_barrier((local, first))
    second = seconds(later, parts[0])
    up2, down2 = send(second)
    later, _ = lax.optimization_barrier((later, second))
    own, mid = lax.optimization_barrier((owns(later, parts[0]), mids(later, parts[0])))
    third = mid[0] + up1, mid[1] + down1
    up3, down3 = send(third)
    later, _ = lax.optimization_barrier((later, third))
    pairs = zip(firsts(later, parts[1]), seconds(later, parts[1]))
    both = tuple(jnp.concatenate(pair) for pair in pairs)
    up12, down12 = send(both)
    outgoing_a = place_blocks(place, empty, (own[0], down2, up3), (own[1], up2, down3), 30)
    mid = mids(later, parts[1])
    third = add_pairs(mid[0], up12, mid[1], down12, outgoing_a)
    up3, down3 = send(third)
    later, _ = lax.optimization_barrier((later, third))
    own = owns(later, parts[1])
    outgoing_b = place_blocks(place, empty, (own[0], down12, up3), (own[1], up12, down3))
    spare = spare_room((owners, MOST, slab_rows, side))
    arrived = [
        lax.all_to_all(
            outgoing.reshape(owners, MOST, slab_rows, -1), "fsdp", split_axis=0, concat_axis=0, tiled=True
        )
        for outgoing in (outgoing_a, outgoing_b)
    ]
    results = precondition(
        live, arrived, left_stats, right_stats, left_roots, right_roots, spare
    )
    returned = lax.all_to_all(results, "fsdp", split_axis=0, concat_axis=0, tiled=True)
    left_out, right_out, left_new, right_new = update_stats(live, arrived, left_stats, right_stats)
    preconditioned = assemble(place, returned.reshape(owners * MOST, slab_rows, side))
    return (
        preconditioned,
        left_out,
        right_out,
        left_new,
        right_new,
    )


def solution(mesh):
    in_specs = (
        P("rep", None, "fsdp", None),
        P(),
        P("rep", "fsdp", None, None, None),
        P("rep", "fsdp", None, None, None),
        P("rep", "fsdp", None, None, None),
        P("rep", "fsdp", None, None, None),
    )
    out_specs = (
        P("rep", "fsdp", None),
        P("rep", "fsdp", None, None, None),
        P("rep", "fsdp", None, None, None),
        P("rep", "fsdp", None, None),
        P("rep", "fsdp", None, None),
    )
    return jax.shard_map(
        on_device, mesh=mesh, in_specs=in_specs, out_specs=out_specs, check_vma=False
    )
```

```python
import functools

import jax
import jax.numpy as jnp
from jax import lax
from jax.experimental import pallas as pl
from jax.experimental.pallas import tpu as pltpu
from jax.sharding import PartitionSpec as P

DECAY_RATE = 0.9
ROOT_RIDGE = 1e-06
GRAFT_EPS = 1e-12
NORM_EPS = 1e-12
MOST = 3
SPLIT = 2

ROOT_POLY = (
    25.0 / 16.0,
    -5.0 / 16.0 - 3125.0 / 4096.0,
    3125.0 / 4096.0,
    -1250.0 / 4096.0,
    250.0 / 4096.0,
    -25.0 / 4096.0,
    1.0 / 4096.0,
)

VMEM_LIMIT = 40 * 1024 * 1024
VMEM_MOST = 52 * 1024 * 1024
VMEM_ALL = 60 * 1024 * 1024
VMEM_SMALL = 16 * 1024 * 1024
VMEM = pltpu.VMEM
HBM = pltpu.HBM
SMEM = pltpu.SMEM


def mul(left, right, dims=((1,), (0,))):
    return lax.dot_general(left, right, (dims, ((), ())), preferred_element_type=jnp.float32)


def blend(live, prev, gram):
    return jnp.where(live, DECAY_RATE * prev + (1.0 - DECAY_RATE) * gram, prev)


PIECE = 256
ROWS = 64
COLS = 128
PARTS = 4


def tiles(side):
    return [
        (slice(row, row + ROWS), slice(col, col + COLS))
        for row in range(0, side, ROWS)
        for col in range(0, side, COLS)
    ]


def product(left, right, use):
    side = left.shape[0]
    for col in range(0, side, PIECE):
        piece = mul(left[:, :], right[:, col : col + PIECE])
        for row in range(0, side, ROWS):
            for c in range(0, PIECE, COLS):
                rows, cols = slice(row, row + ROWS), slice(col + c, col + c + COLS)
                use(piece[row : row + ROWS, c : c + COLS], rows, cols)


def plus_diag(tile, rows, cols, value):
    if rows.start // COLS != cols.start // COLS:
        return tile
    row_ids = lax.broadcasted_iota(jnp.int32, tile.shape, 0) + rows.start
    col_ids = lax.broadcasted_iota(jnp.int32, tile.shape, 1) + cols.start
    return tile + jnp.where(row_ids == col_ids, value, 0.0).astype(tile.dtype)


def total(parts):
    return jnp.sum(functools.reduce(lambda x, y: x + y, parts), keepdims=True)


def cost(matmuls, side, nbytes):
    return pl.CostEstimate(flops=matmuls * 2 * side**3, bytes_accessed=nbytes, transcendentals=0)


def spare_room(shape):
    return pl.pallas_call(
        lambda room: None,
        out_shape=jax.ShapeDtypeStruct(shape, jnp.bfloat16),
        out_specs=pl.BlockSpec(memory_space=pl.ANY),
        compiler_params=pltpu.CompilerParams(vmem_limit_bytes=VMEM_ALL),
        name="spare_room",
    )()


def place_kernel(place_ref, empty_ref, *rest):
    (own_front, straight_front, last_front, own_back, straight_back, last_back), rest = rest[:6], rest[6:]
    out_ref, sums, zeros, sem = rest
    half = own_front.shape[0]
    zeros[...] = jnp.zeros_like(zeros)

    def blank(place, carry):
        @pl.when(empty_ref[place] > 0)
        def _():
            pltpu.make_async_copy(zeros, out_ref.at[place], sem).start()

        return carry

    def add(j, carry):
        for block, own, straight, last in (
            (j, own_front, straight_front, last_front),
            (half + j, own_back, straight_back, last_back),
        ):
            three = own[j], straight[straight.shape[0] - half + j], last[j]
            sums[block] = sum(term.astype(jnp.float32) for term in three).astype(jnp.bfloat16)
            pltpu.make_async_copy(sums.at[block], out_ref.at[place_ref[block]], sem).start()
        return carry

    lax.fori_loop(0, half, add, 0, unroll=4)
    lax.fori_loop(0, out_ref.shape[0], blank, 0, unroll=4)
    pltpu.make_async_copy(out_ref, out_ref, sem).wait()


def place_blocks(place, empty, front, back, weight=0):
    half, rows, cols = front[0].shape
    scalars = pl.BlockSpec(memory_space=SMEM)
    return pl.pallas_call(
        place_kernel,
        out_shape=jax.ShapeDtypeStruct((empty.shape[0], rows, cols), jnp.bfloat16),
        in_specs=[scalars] * 2 + [pl.BlockSpec(memory_space=VMEM)] * 6,
        out_specs=pl.BlockSpec(memory_space=HBM),
        scratch_shapes=[
            VMEM((2 * half, rows, cols), jnp.bfloat16),
            VMEM((rows, cols), jnp.bfloat16),
            pltpu.SemaphoreType.DMA(()),
        ],
        compiler_params=pltpu.CompilerParams(vmem_limit_bytes=VMEM_LIMIT),
        cost_estimate=cost(weight, 512, 8 * half * rows * cols * 2),
        name="place_blocks",
    )(place, empty, *front, *back)


def add_kernel(one_ref, two_ref, three_ref, four_ref, *rest):
    first_ref, second_ref = rest[-2:]

    def add(j, carry):
        first_ref[j] = one_ref[j] + two_ref[j]
        second_ref[j] = three_ref[j] + four_ref[j]
        return carry

    lax.fori_loop(0, first_ref.shape[0], add, 0, unroll=8)


def add_pairs(one, two, three, four, *after):
    near = pl.BlockSpec(memory_space=VMEM)
    shape = jax.ShapeDtypeStruct(one.shape, one.dtype)
    return pl.pallas_call(
        add_kernel,
        out_shape=[shape, shape],
        in_specs=[near] * 4 + [pl.BlockSpec(memory_space=pl.ANY)] * len(after),
        out_specs=[near, near],
        compiler_params=pltpu.CompilerParams(vmem_limit_bytes=VMEM_SMALL),
        cost_estimate=cost(800, 512, 2 * one.size),
        name="add_pairs",
    )(one, two, three, four, *after)


def new_roots(live, stats, grams, low, square, inner, outer, between):
    side = stats.shape[-1]
    f32, bf16 = jnp.float32, jnp.bfloat16
    c0, c1, c2, c3, c4, c5, c6 = ROOT_POLY
    keep = jnp.where(live, DECAY_RATE, 1.0)
    take = jnp.where(live, 1.0 - DECAY_RATE, 0.0)
    scales = []
    for i in range(2):
        squares = []
        for rows, cols in tiles(side):
            tile = keep * stats[i, rows, cols] + take * grams[i, rows, cols]
            tile = plus_diag(tile, rows, cols, ROOT_RIDGE)
            low[i, rows, cols] = tile.astype(bf16)
            squares.append(tile * tile)
        frob = side * jnp.sqrt(total(squares) * (1.0 / (side * side)) + NORM_EPS)
        scales.append(2.5 / frob)

    for i in range(2):
        near, far = (c5 * scales[i]).astype(bf16), (c6 * scales[i] * scales[i]).astype(bf16)

        def first(tile, rows, cols):
            tile = tile.astype(bf16)
            square[i, rows, cols] = tile
            inner[i, rows, cols] = plus_diag(near * low[i, rows, cols] + far * tile, rows, cols, c4)

        product(low[i], low[i], first)
        between()
    for i in range(2):
        near, far = (c3 * scales[i]).astype(bf16), scales[i] * scales[i]

        def second(tile, rows, cols):
            tile = (far * tile).astype(bf16) + near * low[i, rows, cols]
            outer[i, rows, cols] = plus_diag(tile, rows, cols, c2)

        product(square[i], inner[i], second)
    for i in (1, 0):
        near, far = c1 * scales[i], scales[i] * scales[i]

        def third(tile, rows, cols):
            tile = far * tile + near * low[i, rows, cols].astype(f32)
            inner[i, rows, cols] = plus_diag(tile, rows, cols, c0).astype(bf16)

        product(square[i], outer[i], third)


def precondition_kernel(
    live_ref, arrived_a, arrived_b, left_stats, right_stats, left_roots, right_roots, _, out,
    halves, stats, roots, results, grams, raws, applied, low, square, inner, outer, in_sems, out_sems,
):
    side = stats.shape[-1]
    entries = side * side
    f32, bf16 = jnp.float32, jnp.bfloat16
    grid = tiles(side)
    fetch = {}

    def get(name, source, target):
        fetch[name] = pltpu.make_async_copy(source, target, in_sems.at[len(fetch)])
        fetch[name].start()

    get("a0", arrived_a.at[:, 0], halves.at[0])
    for slot in range(1, MOST):
        get("a%d" % slot, arrived_a.at[:, slot], halves.at[slot])
        get("r%d" % slot, right_roots.at[0, 0, slot], roots.at[2 * slot - 1])
    for slot in range(1, MOST):
        get("l%d" % slot, left_roots.at[0, 0, slot], roots.at[2 * slot - 2])
    get("left", left_stats.at[0, 0, 0], stats.at[0])
    get("right", right_stats.at[0, 0, 0], stats.at[1])

    def block_of(slot):
        fetch["a%d" % slot].wait()
        front, back = halves[slot], arrived_b[:, slot]
        return jnp.concatenate([half.reshape(side, -1) for half in (front, back)], axis=1)

    def give(slot, low=0, high=arrived_a.shape[0], part=0):
        slabs = pl.ds(low, high - low)
        copy = pltpu.make_async_copy(results.at[slot, slabs], out.at[slabs, slot], out_sems.at[slot + part])
        copy.start()
        sent.append(copy)

    def put(number, rows, cols, tile):
        slabs = slice(rows.start // 16, rows.stop // 16)
        results[number, slabs, :, cols] = tile.reshape(ROWS // 16, 16, COLS)

    def power(tile_of):
        return total([jnp.square(tile_of(rows, cols)) for rows, cols in grid]) * (1.0 / entries)

    def graft(slot, out_power, parts=1):
        grad_power = power(lambda rows, cols: blocks[slot][rows, cols].astype(f32))
        scale = jnp.sqrt(grad_power) / jnp.sqrt(out_power + GRAFT_EPS)
        share = results.shape[1] // parts
        for part in range(parts):
            for rows, cols in grid:
                if rows.start // 16 // share == part:
                    put(slot, rows, cols, (raws[slot, rows, cols] * scale).astype(bf16))
            give(slot, part * share, (part + 1) * share, MOST * (part > 0) + max(part - 1, 0))

    def apply_right(slot, root):
        def use(tile, rows, cols):
            applied[slot, rows, cols] = tile.astype(bf16)

        product(blocks[slot], root, use)

    def apply_left(slot, root):
        squares = []

        def use(tile, rows, cols):
            raws[slot, rows, cols] = tile
            squares.append(tile * tile)

        product(root, applied[slot], use)
        return total(squares) * (1.0 / entries)

    blocks = [block_of(0)]
    grams[0] = mul(blocks[0], blocks[0], ((1,), (1,)))
    grams[1] = mul(blocks[0], blocks[0], ((0,), (0,)))
    for slot in range(1, MOST):
        blocks.append(block_of(slot))
        fetch["r%d" % slot].wait()
    for slot in range(1, MOST):
        apply_right(slot, roots[2 * slot - 1])
    for slot in range(1, MOST):
        fetch["l%d" % slot].wait()
    powers = [apply_left(slot, roots[2 * slot - 2]) for slot in range(1, MOST)]
    sent = []
    fetch["left"].wait()
    fetch["right"].wait()
    fill = iter(range(1, MOST))

    def between():
        for slot in fill:
            graft(slot, powers[slot - 1])
            break

    new_roots(live_ref[0] > 0, stats, grams, low, square, inner, outer, between)
    apply_right(0, inner[1])
    graft(0, apply_left(0, inner[0]), PARTS)
    for copy in sent:
        copy.wait()


def precondition(live, arrived, left_stats, right_stats, left_roots, right_roots, spare):
    owners, _, rows, width = arrived[0].shape
    side = left_stats.shape[-1]
    far = pl.BlockSpec(memory_space=HBM)
    return pl.pallas_call(
        precondition_kernel,
        out_shape=jax.ShapeDtypeStruct((owners, MOST, rows, side), jnp.bfloat16),
        in_specs=[pl.BlockSpec(memory_space=SMEM), far, pl.BlockSpec(memory_space=VMEM)] + [far] * 5,
        out_specs=far,
        scratch_shapes=[
            VMEM((MOST, owners, rows, width), jnp.bfloat16),
            VMEM((2, side, side), jnp.float32),
            VMEM((2 * MOST - 2, side, side), jnp.bfloat16),
            VMEM((MOST, owners, rows, side), jnp.bfloat16),
            VMEM((2, side, side), jnp.float32),
            VMEM((MOST, side, side), jnp.float32),
            VMEM((MOST, side, side), jnp.bfloat16),
            VMEM((2, side, side), jnp.bfloat16),
            VMEM((2, side, side), jnp.bfloat16),
            VMEM((2, side, side), jnp.bfloat16),
            VMEM((2, side, side), jnp.bfloat16),
            pltpu.SemaphoreType.DMA((3 * MOST,)),
            pltpu.SemaphoreType.DMA((MOST + PARTS - 1,)),
        ],
        compiler_params=pltpu.CompilerParams(vmem_limit_bytes=VMEM_MOST),
        cost_estimate=cost(14, side, 9 * side * side * 4),
        input_output_aliases={7: 0},
        name="precondition",
    )(live, *arrived, left_stats, right_stats, left_roots, right_roots, spare)


def stats_kernel(
    live_ref, front_ref, back_ref, lprev_ref, rprev_ref, left_ref, right_ref, lroot_ref, rroot_ref,
    stats, grams, low, square, inner, outer,
):
    side = lprev_ref.shape[-1]
    block = jnp.concatenate([front_ref[:, 0], back_ref[:, 0]], axis=-1).reshape(side, side)
    live = live_ref[pl.program_id(0)] > 0
    grams[0] = mul(block, block, ((1,), (1,)))
    grams[1] = mul(block, block, ((0,), (0,)))
    for rows, cols in tiles(side):
        left_ref[0, 0, 0, rows, cols] = blend(live, lprev_ref[0, 0, 0, rows, cols], grams[0, rows, cols])
        right_ref[0, 0, 0, rows, cols] = blend(live, rprev_ref[0, 0, 0, rows, cols], grams[1, rows, cols])

    @pl.when(pl.program_id(0) == 0)
    def _():
        stats[0] = lprev_ref[0, 0, 0]
        stats[1] = rprev_ref[0, 0, 0]
        new_roots(live, stats, grams, low, square, inner, outer, lambda: None)
        lroot_ref[0, 0] = inner[0]
        rroot_ref[0, 0] = inner[1]


def update_stats(live, arrived, left_stats, right_stats):
    owners, _, rows, _ = arrived[0].shape
    side = left_stats.shape[-1]
    at_slot = pl.BlockSpec((1, 1, 1, side, side), lambda s: (0, 0, s, 0, 0))
    of_first = pl.BlockSpec((1, 1, side, side), lambda s: (0, 0, 0, 0))
    shape = jax.ShapeDtypeStruct(left_stats.shape, jnp.float32)
    root = jax.ShapeDtypeStruct((1, 1, side, side), jnp.bfloat16)
    return pl.pallas_call(
        stats_kernel,
        grid=(MOST,),
        out_shape=[shape, shape, root, root],
        in_specs=[pl.BlockSpec(memory_space=SMEM)]
        + [pl.BlockSpec((owners, 1, rows, half.shape[3]), lambda s: (0, s, 0, 0)) for half in arrived]
        + [at_slot, at_slot],
        out_specs=[at_slot, at_slot, of_first, of_first],
        scratch_shapes=[
            VMEM((2, side, side), jnp.float32),
            VMEM((2, side, side), jnp.float32),
            VMEM((2, side, side), jnp.bfloat16),
            VMEM((2, side, side), jnp.bfloat16),
            VMEM((2, side, side), jnp.bfloat16),
            VMEM((2, side, side), jnp.bfloat16),
        ],
        compiler_params=pltpu.CompilerParams(vmem_limit_bytes=VMEM_MOST),
        cost_estimate=cost(2 * MOST + 6, side, 13 * side * side * 4),
        name="update_stats",
    )(live, *arrived, left_stats, right_stats)


def assemble_kernel(place_ref, back_ref, out_ref, sem):
    count = out_ref.shape[0]

    def start(b, carry):
        pltpu.make_async_copy(back_ref.at[place_ref[b]], out_ref.at[b], sem).start()
        return carry

    lax.fori_loop(0, count, start, 0, unroll=8)
    pltpu.make_async_copy(out_ref, out_ref, sem).wait()


def assemble(place, back):
    count = place.shape[0]
    rows, cols = back.shape[1:]
    return pl.pallas_call(
        assemble_kernel,
        out_shape=jax.ShapeDtypeStruct((count, rows, cols), jnp.bfloat16),
        in_specs=[pl.BlockSpec(memory_space=SMEM), pl.BlockSpec(memory_space=pl.ANY)],
        out_specs=pl.BlockSpec(memory_space=HBM),
        scratch_shapes=[pltpu.SemaphoreType.DMA(())],
        compiler_params=pltpu.CompilerParams(vmem_limit_bytes=VMEM_LIMIT),
        cost_estimate=cost(0, 0, 2 * count * rows * cols * 2),
        name="assemble",
    )(place, back)


def routing(owner, owners):
    ids = jnp.arange(owner.shape[0], dtype=jnp.int32)
    same = owner[:, None] == owner[None, :]
    slot = jnp.sum((same & (ids[None, :] < ids[:, None])).astype(jnp.int32), axis=1)
    place = owner * MOST + slot
    taken = place[None, :] == jnp.arange(owners * MOST, dtype=jnp.int32)[:, None]
    return place, 1 - jnp.sum(taken.astype(jnp.int32), axis=1)


def on_device(grads, owner_table, left_stats, right_stats, left_roots, right_roots):
    groups = lax.axis_size("rep")
    owners = lax.axis_size("fsdp")
    group_id = lax.axis_index("rep")
    owner_id = lax.axis_index("fsdp")
    local = grads[0]
    total_blocks, slab_rows, side = local.shape
    share = total_blocks // groups
    half = share // 2
    up = [(i, (i + 1) % groups) for i in range(groups)]
    down = [(i, (i - 1) % groups) for i in range(groups)]

    owner = lax.dynamic_slice(owner_table[:, 0], (group_id * share,), (share,), allow_negative_indices=False)
    place, empty = routing(owner, owners)
    own_count = jnp.sum((owner == owner_id).astype(jnp.int32))
    live = (jnp.arange(MOST, dtype=jnp.int32) < own_count).astype(jnp.int32)
    cut = side // SPLIT
    parts = ((0, cut), (cut, side - cut))

    def part(source, ahead, low, columns):
        start = ((group_id + ahead) & (groups - 1)) * share + low
        return lax.dynamic_slice(
            source, (start, 0, columns[0]), (half, slab_rows, columns[1]), allow_negative_indices=False
        )

    def send(pair):
        return lax.ppermute(pair[0], "rep", up), lax.ppermute(pair[1], "rep", down)

    def firsts(source, columns):
        return part(source, 2, 0, columns), part(source, 2, half, columns)

    def seconds(source, columns):
        return part(source, 1, half, columns), part(source, 3, 0, columns)

    def mids(source, columns):
        return part(source, 1, 0, columns), part(source, 3, half, columns)

    def owns(source, columns):
        return part(source, 0, 0, columns), part(source, 0, half, columns)

    first = firsts(local, parts[0])
    up1, down1 = send(first)
    later, _ = lax.optimization_barrier((local, first))
    second = seconds(later, parts[0])
    up2, down2 = send(second)
    later, _ = lax.optimization_barrier((later, second))
    own, mid = lax.optimization_barrier((owns(later, parts[0]), mids(later, parts[0])))
    third = mid[0] + up1, mid[1] + down1
    up3, down3 = send(third)
    later, _ = lax.optimization_barrier((later, third))
    pairs = zip(firsts(later, parts[1]), seconds(later, parts[1]))
    both = tuple(jnp.concatenate(pair) for pair in pairs)
    up12, down12 = send(both)
    outgoing_a = place_blocks(place, empty, (own[0], down2, up3), (own[1], up2, down3), 30)
    own, mid = owns(later, parts[1]), mids(later, parts[1])
    third = add_pairs(mid[0], up12, mid[1], down12, outgoing_a)
    up3, down3 = send(third)
    outgoing_b = place_blocks(place, empty, (own[0], down12, up3), (own[1], up12, down3))
    spare = spare_room((owners, MOST, slab_rows, side))
    arrived = [
        lax.all_to_all(
            outgoing.reshape(owners, MOST, slab_rows, -1), "fsdp", split_axis=0, concat_axis=0, tiled=True
        )
        for outgoing in (outgoing_a, outgoing_b)
    ]
    results = precondition(
        live, arrived, left_stats, right_stats, left_roots, right_roots, spare
    )
    returned = lax.all_to_all(results, "fsdp", split_axis=0, concat_axis=0, tiled=True)
    left_out, right_out, left_new, right_new = update_stats(live, arrived, left_stats, right_stats)
    preconditioned = assemble(place, returned.reshape(owners * MOST, slab_rows, side))
    return (
        preconditioned,
        left_out,
        right_out,
        left_new,
        right_new,
    )


def solution(mesh):
    in_specs = (
        P("rep", None, "fsdp", None),
        P(),
        P("rep", "fsdp", None, None, None),
        P("rep", "fsdp", None, None, None),
        P("rep", "fsdp", None, None, None),
        P("rep", "fsdp", None, None, None),
    )
    out_specs = (
        P("rep", "fsdp", None),
        P("rep", "fsdp", None, None, None),
        P("rep", "fsdp", None, None, None),
        P("rep", "fsdp", None, None),
        P("rep", "fsdp", None, None),
    )
    return jax.shard_map(
        on_device, mesh=mesh, in_specs=in_specs, out_specs=out_specs, check_vma=False
    )
```

```python
import functools

import jax
import jax.numpy as jnp
from jax import lax
from jax.experimental import pallas as pl
from jax.experimental.pallas import tpu as pltpu
from jax.sharding import PartitionSpec as P

DECAY_RATE = 0.9
ROOT_RIDGE = 1e-06
GRAFT_EPS = 1e-12
NORM_EPS = 1e-12
MOST = 3
SPLIT = 2

ROOT_POLY = (
    25.0 / 16.0,
    -5.0 / 16.0 - 3125.0 / 4096.0,
    3125.0 / 4096.0,
    -1250.0 / 4096.0,
    250.0 / 4096.0,
    -25.0 / 4096.0,
    1.0 / 4096.0,
)

VMEM_LIMIT = 40 * 1024 * 1024
VMEM_MOST = 52 * 1024 * 1024
VMEM_ALL = 60 * 1024 * 1024
VMEM_SMALL = 16 * 1024 * 1024
VMEM = pltpu.VMEM
HBM = pltpu.HBM
SMEM = pltpu.SMEM


def mul(left, right, dims=((1,), (0,))):
    return lax.dot_general(left, right, (dims, ((), ())), preferred_element_type=jnp.float32)


def blend(live, prev, gram):
    return jnp.where(live, DECAY_RATE * prev + (1.0 - DECAY_RATE) * gram, prev)


PIECE = 256
ROWS = 64
COLS = 128
PARTS = 4


def tiles(side):
    return [
        (slice(row, row + ROWS), slice(col, col + COLS))
        for row in range(0, side, ROWS)
        for col in range(0, side, COLS)
    ]


def product(left, right, use):
    side = left.shape[0]
    for col in range(0, side, PIECE):
        piece = mul(left[:, :], right[:, col : col + PIECE])
        for row in range(0, side, ROWS):
            for c in range(0, PIECE, COLS):
                rows, cols = slice(row, row + ROWS), slice(col + c, col + c + COLS)
                use(piece[row : row + ROWS, c : c + COLS], rows, cols)


def plus_diag(tile, rows, cols, value):
    if rows.start // COLS != cols.start // COLS:
        return tile
    row_ids = lax.broadcasted_iota(jnp.int32, tile.shape, 0) + rows.start
    col_ids = lax.broadcasted_iota(jnp.int32, tile.shape, 1) + cols.start
    return tile + jnp.where(row_ids == col_ids, value, 0.0).astype(tile.dtype)


def total(parts):
    return jnp.sum(functools.reduce(lambda x, y: x + y, parts), keepdims=True)


def cost(matmuls, side, nbytes):
    return pl.CostEstimate(flops=matmuls * 2 * side**3, bytes_accessed=nbytes, transcendentals=0)


def spare_room(shape):
    return pl.pallas_call(
        lambda room: None,
        out_shape=jax.ShapeDtypeStruct(shape, jnp.bfloat16),
        out_specs=pl.BlockSpec(memory_space=pl.ANY),
        compiler_params=pltpu.CompilerParams(vmem_limit_bytes=VMEM_ALL),
        name="spare_room",
    )()


def place_kernel(place_ref, empty_ref, *rest):
    (own_front, straight_front, last_front, own_back, straight_back, last_back), rest = rest[:6], rest[6:]
    out_ref, sums, zeros, sem = rest
    half = own_front.shape[0]
    zeros[...] = jnp.zeros_like(zeros)

    def blank(place, carry):
        @pl.when(empty_ref[place] > 0)
        def _():
            pltpu.make_async_copy(zeros, out_ref.at[place], sem).start()

        return carry

    def add(j, carry):
        for block, own, straight, last in (
            (j, own_front, straight_front, last_front),
            (half + j, own_back, straight_back, last_back),
        ):
            three = own[j], straight[straight.shape[0] - half + j], last[j]
            sums[block] = sum(term.astype(jnp.float32) for term in three).astype(jnp.bfloat16)
            pltpu.make_async_copy(sums.at[block], out_ref.at[place_ref[block]], sem).start()
        return carry

    lax.fori_loop(0, half, add, 0, unroll=4)
    lax.fori_loop(0, out_ref.shape[0], blank, 0, unroll=4)
    pltpu.make_async_copy(out_ref, out_ref, sem).wait()


def place_blocks(place, empty, front, back, weight=0):
    half, rows, cols = front[0].shape
    scalars = pl.BlockSpec(memory_space=SMEM)
    return pl.pallas_call(
        place_kernel,
        out_shape=jax.ShapeDtypeStruct((empty.shape[0], rows, cols), jnp.bfloat16),
        in_specs=[scalars] * 2 + [pl.BlockSpec(memory_space=VMEM)] * 6,
        out_specs=pl.BlockSpec(memory_space=HBM),
        scratch_shapes=[
            VMEM((2 * half, rows, cols), jnp.bfloat16),
            VMEM((rows, cols), jnp.bfloat16),
            pltpu.SemaphoreType.DMA(()),
        ],
        compiler_params=pltpu.CompilerParams(vmem_limit_bytes=VMEM_LIMIT),
        cost_estimate=cost(weight, 512, 8 * half * rows * cols * 2),
        name="place_blocks",
    )(place, empty, *front, *back)


def add_kernel(one_ref, two_ref, three_ref, four_ref, *rest):
    first_ref, second_ref = rest[-2:]

    def add(j, carry):
        first_ref[j] = one_ref[j] + two_ref[j]
        second_ref[j] = three_ref[j] + four_ref[j]
        return carry

    lax.fori_loop(0, first_ref.shape[0], add, 0, unroll=8)


def add_pairs(one, two, three, four, *after):
    near = pl.BlockSpec(memory_space=VMEM)
    shape = jax.ShapeDtypeStruct(one.shape, one.dtype)
    return pl.pallas_call(
        add_kernel,
        out_shape=[shape, shape],
        in_specs=[near] * 4 + [pl.BlockSpec(memory_space=pl.ANY)] * len(after),
        out_specs=[near, near],
        compiler_params=pltpu.CompilerParams(vmem_limit_bytes=VMEM_SMALL),
        cost_estimate=cost(800, 512, 2 * one.size),
        name="add_pairs",
    )(one, two, three, four, *after)


def new_roots(live, stats, grams, low, square, inner, outer, between):
    side = stats.shape[-1]
    f32, bf16 = jnp.float32, jnp.bfloat16
    c0, c1, c2, c3, c4, c5, c6 = ROOT_POLY
    keep = jnp.where(live, DECAY_RATE, 1.0)
    take = jnp.where(live, 1.0 - DECAY_RATE, 0.0)
    scales = []
    for i in range(2):
        squares = []
        for rows, cols in tiles(side):
            tile = keep * stats[i, rows, cols] + take * grams[i, rows, cols]
            tile = plus_diag(tile, rows, cols, ROOT_RIDGE)
            low[i, rows, cols] = tile.astype(bf16)
            squares.append(tile * tile)
        frob = side * jnp.sqrt(total(squares) * (1.0 / (side * side)) + NORM_EPS)
        scales.append(2.5 / frob)

    for i in range(2):
        near, far = (c5 * scales[i]).astype(bf16), (c6 * scales[i] * scales[i]).astype(bf16)

        def first(tile, rows, cols):
            tile = tile.astype(bf16)
            square[i, rows, cols] = tile
            inner[i, rows, cols] = plus_diag(near * low[i, rows, cols] + far * tile, rows, cols, c4)

        product(low[i], low[i], first)
        between()
    for i in range(2):
        near, far = (c3 * scales[i]).astype(bf16), scales[i] * scales[i]

        def second(tile, rows, cols):
            tile = (far * tile).astype(bf16) + near * low[i, rows, cols]
            outer[i, rows, cols] = plus_diag(tile, rows, cols, c2)

        product(square[i], inner[i], second)
    for i in (1, 0):
        near, far = c1 * scales[i], scales[i] * scales[i]

        def third(tile, rows, cols):
            tile = far * tile + near * low[i, rows, cols].astype(f32)
            inner[i, rows, cols] = plus_diag(tile, rows, cols, c0).astype(bf16)

        product(square[i], outer[i], third)


def precondition_kernel(
    live_ref, arrived_a, arrived_b, left_stats, right_stats, left_roots, right_roots, _, out,
    halves, stats, roots, results, grams, raws, applied, low, square, inner, outer, in_sems, out_sems,
):
    side = stats.shape[-1]
    entries = side * side
    f32, bf16 = jnp.float32, jnp.bfloat16
    grid = tiles(side)
    fetch = {}

    def get(name, source, target):
        fetch[name] = pltpu.make_async_copy(source, target, in_sems.at[len(fetch)])
        fetch[name].start()

    get("a0", arrived_a.at[:, 0], halves.at[0])
    for slot in range(1, MOST):
        get("a%d" % slot, arrived_a.at[:, slot], halves.at[slot])
        get("r%d" % slot, right_roots.at[0, 0, slot], roots.at[2 * slot - 1])
    for slot in range(1, MOST):
        get("l%d" % slot, left_roots.at[0, 0, slot], roots.at[2 * slot - 2])
    get("left", left_stats.at[0, 0, 0], stats.at[0])
    get("right", right_stats.at[0, 0, 0], stats.at[1])

    def block_of(slot):
        fetch["a%d" % slot].wait()
        front, back = halves[slot], arrived_b[:, slot]
        return jnp.concatenate([half.reshape(side, -1) for half in (front, back)], axis=1)

    def give(slot, low=0, high=arrived_a.shape[0], part=0):
        slabs = pl.ds(low, high - low)
        copy = pltpu.make_async_copy(results.at[slot, slabs], out.at[slabs, slot], out_sems.at[slot + part])
        copy.start()
        sent.append(copy)

    def put(number, rows, cols, tile):
        slabs = slice(rows.start // 16, rows.stop // 16)
        results[number, slabs, :, cols] = tile.reshape(ROWS // 16, 16, COLS)

    def power(tile_of):
        return total([jnp.square(tile_of(rows, cols)) for rows, cols in grid]) * (1.0 / entries)

    def graft(slot, out_power, parts=1):
        grad_power = power(lambda rows, cols: blocks[slot][rows, cols].astype(f32))
        scale = jnp.sqrt(grad_power) / jnp.sqrt(out_power + GRAFT_EPS)
        share = results.shape[1] // parts
        for part in range(parts):
            for rows, cols in grid:
                if rows.start // 16 // share == part:
                    put(slot, rows, cols, (raws[slot, rows, cols] * scale).astype(bf16))
            give(slot, part * share, (part + 1) * share, MOST * (part > 0) + max(part - 1, 0))

    def apply_right(slot, root):
        def use(tile, rows, cols):
            applied[slot, rows, cols] = tile.astype(bf16)

        product(blocks[slot], root, use)

    def apply_left(slot, root):
        squares = []

        def use(tile, rows, cols):
            raws[slot, rows, cols] = tile
            squares.append(tile * tile)

        product(root, applied[slot], use)
        return total(squares) * (1.0 / entries)

    back = arrived_b[:, 0].reshape(side, -1)
    raws[0] = mul(back, back, ((1,), (1,)))
    blocks = [block_of(0)]
    front = halves[0].reshape(side, -1)
    grams[0] = raws[0] + mul(front, front, ((1,), (1,)))
    grams[1] = mul(blocks[0], blocks[0], ((0,), (0,)))
    for slot in range(1, MOST):
        blocks.append(block_of(slot))
        fetch["r%d" % slot].wait()
    for slot in range(1, MOST):
        apply_right(slot, roots[2 * slot - 1])
    for slot in range(1, MOST):
        fetch["l%d" % slot].wait()
    powers = [apply_left(slot, roots[2 * slot - 2]) for slot in range(1, MOST)]
    sent = []
    fetch["left"].wait()
    fetch["right"].wait()
    fill = iter(range(1, MOST))

    def between():
        for slot in fill:
            graft(slot, powers[slot - 1])
            break

    new_roots(live_ref[0] > 0, stats, grams, low, square, inner, outer, between)
    apply_right(0, inner[1])
    graft(0, apply_left(0, inner[0]), PARTS)
    for copy in sent:
        copy.wait()


def precondition(live, arrived, left_stats, right_stats, left_roots, right_roots, spare):
    owners, _, rows, width = arrived[0].shape
    side = left_stats.shape[-1]
    far = pl.BlockSpec(memory_space=HBM)
    return pl.pallas_call(
        precondition_kernel,
        out_shape=jax.ShapeDtypeStruct((owners, MOST, rows, side), jnp.bfloat16),
        in_specs=[pl.BlockSpec(memory_space=SMEM), far, pl.BlockSpec(memory_space=VMEM)] + [far] * 5,
        out_specs=far,
        scratch_shapes=[
            VMEM((MOST, owners, rows, width), jnp.bfloat16),
            VMEM((2, side, side), jnp.float32),
            VMEM((2 * MOST - 2, side, side), jnp.bfloat16),
            VMEM((MOST, owners, rows, side), jnp.bfloat16),
            VMEM((2, side, side), jnp.float32),
            VMEM((MOST, side, side), jnp.float32),
            VMEM((MOST, side, side), jnp.bfloat16),
            VMEM((2, side, side), jnp.bfloat16),
            VMEM((2, side, side), jnp.bfloat16),
            VMEM((2, side, side), jnp.bfloat16),
            VMEM((2, side, side), jnp.bfloat16),
            pltpu.SemaphoreType.DMA((3 * MOST,)),
            pltpu.SemaphoreType.DMA((MOST + PARTS - 1,)),
        ],
        compiler_params=pltpu.CompilerParams(vmem_limit_bytes=VMEM_MOST),
        cost_estimate=cost(14, side, 9 * side * side * 4),
        input_output_aliases={7: 0},
        name="precondition",
    )(live, *arrived, left_stats, right_stats, left_roots, right_roots, spare)


def stats_kernel(
    live_ref, front_ref, back_ref, lprev_ref, rprev_ref, left_ref, right_ref, lroot_ref, rroot_ref,
    stats, grams, low, square, inner, outer,
):
    side = lprev_ref.shape[-1]
    block = jnp.concatenate([front_ref[:, 0], back_ref[:, 0]], axis=-1).reshape(side, side)
    live = live_ref[pl.program_id(0)] > 0
    grams[0] = mul(block, block, ((1,), (1,)))
    grams[1] = mul(block, block, ((0,), (0,)))
    for rows, cols in tiles(side):
        left_ref[0, 0, 0, rows, cols] = blend(live, lprev_ref[0, 0, 0, rows, cols], grams[0, rows, cols])
        right_ref[0, 0, 0, rows, cols] = blend(live, rprev_ref[0, 0, 0, rows, cols], grams[1, rows, cols])

    @pl.when(pl.program_id(0) == 0)
    def _():
        stats[0] = lprev_ref[0, 0, 0]
        stats[1] = rprev_ref[0, 0, 0]
        new_roots(live, stats, grams, low, square, inner, outer, lambda: None)
        lroot_ref[0, 0] = inner[0]
        rroot_ref[0, 0] = inner[1]


def update_stats(live, arrived, left_stats, right_stats):
    owners, _, rows, _ = arrived[0].shape
    side = left_stats.shape[-1]
    at_slot = pl.BlockSpec((1, 1, 1, side, side), lambda s: (0, 0, s, 0, 0))
    of_first = pl.BlockSpec((1, 1, side, side), lambda s: (0, 0, 0, 0))
    shape = jax.ShapeDtypeStruct(left_stats.shape, jnp.float32)
    root = jax.ShapeDtypeStruct((1, 1, side, side), jnp.bfloat16)
    return pl.pallas_call(
        stats_kernel,
        grid=(MOST,),
        out_shape=[shape, shape, root, root],
        in_specs=[pl.BlockSpec(memory_space=SMEM)]
        + [pl.BlockSpec((owners, 1, rows, half.shape[3]), lambda s: (0, s, 0, 0)) for half in arrived]
        + [at_slot, at_slot],
        out_specs=[at_slot, at_slot, of_first, of_first],
        scratch_shapes=[
            VMEM((2, side, side), jnp.float32),
            VMEM((2, side, side), jnp.float32),
            VMEM((2, side, side), jnp.bfloat16),
            VMEM((2, side, side), jnp.bfloat16),
            VMEM((2, side, side), jnp.bfloat16),
            VMEM((2, side, side), jnp.bfloat16),
        ],
        compiler_params=pltpu.CompilerParams(vmem_limit_bytes=VMEM_MOST),
        cost_estimate=cost(2 * MOST + 6, side, 13 * side * side * 4),
        name="update_stats",
    )(live, *arrived, left_stats, right_stats)


def assemble_kernel(place_ref, back_ref, out_ref, sem):
    count = out_ref.shape[0]

    def start(b, carry):
        pltpu.make_async_copy(back_ref.at[place_ref[b]], out_ref.at[b], sem).start()
        return carry

    lax.fori_loop(0, count, start, 0, unroll=8)
    pltpu.make_async_copy(out_ref, out_ref, sem).wait()


def assemble(place, back):
    count = place.shape[0]
    rows, cols = back.shape[1:]
    return pl.pallas_call(
        assemble_kernel,
        out_shape=jax.ShapeDtypeStruct((count, rows, cols), jnp.bfloat16),
        in_specs=[pl.BlockSpec(memory_space=SMEM), pl.BlockSpec(memory_space=pl.ANY)],
        out_specs=pl.BlockSpec(memory_space=HBM),
        scratch_shapes=[pltpu.SemaphoreType.DMA(())],
        compiler_params=pltpu.CompilerParams(vmem_limit_bytes=VMEM_LIMIT),
        cost_estimate=cost(0, 0, 2 * count * rows * cols * 2),
        name="assemble",
    )(place, back)


def routing(owner, owners):
    ids = jnp.arange(owner.shape[0], dtype=jnp.int32)
    same = owner[:, None] == owner[None, :]
    slot = jnp.sum((same & (ids[None, :] < ids[:, None])).astype(jnp.int32), axis=1)
    place = owner * MOST + slot
    taken = place[None, :] == jnp.arange(owners * MOST, dtype=jnp.int32)[:, None]
    return place, 1 - jnp.sum(taken.astype(jnp.int32), axis=1)


def on_device(grads, owner_table, left_stats, right_stats, left_roots, right_roots):
    groups = lax.axis_size("rep")
    owners = lax.axis_size("fsdp")
    group_id = lax.axis_index("rep")
    owner_id = lax.axis_index("fsdp")
    local = grads[0]
    total_blocks, slab_rows, side = local.shape
    share = total_blocks // groups
    half = share // 2
    up = [(i, (i + 1) % groups) for i in range(groups)]
    down = [(i, (i - 1) % groups) for i in range(groups)]

    owner = lax.dynamic_slice(owner_table[:, 0], (group_id * share,), (share,), allow_negative_indices=False)
    place, empty = routing(owner, owners)
    own_count = jnp.sum((owner == owner_id).astype(jnp.int32))
    live = (jnp.arange(MOST, dtype=jnp.int32) < own_count).astype(jnp.int32)
    cut = side // SPLIT
    parts = ((0, cut), (cut, side - cut))

    def part(source, ahead, low, columns):
        start = ((group_id + ahead) & (groups - 1)) * share + low
        return lax.dynamic_slice(
            source, (start, 0, columns[0]), (half, slab_rows, columns[1]), allow_negative_indices=False
        )

    def send(pair):
        return lax.ppermute(pair[0], "rep", up), lax.ppermute(pair[1], "rep", down)

    def firsts(source, columns):
        return part(source, 2, 0, columns), part(source, 2, half, columns)

    def seconds(source, columns):
        return part(source, 1, half, columns), part(source, 3, 0, columns)

    def mids(source, columns):
        return part(source, 1, 0, columns), part(source, 3, half, columns)

    def owns(source, columns):
        return part(source, 0, 0, columns), part(source, 0, half, columns)

    first = firsts(local, parts[0])
    up1, down1 = send(first)
    later, _ = lax.optimization_barrier((local, first))
    second = seconds(later, parts[0])
    up2, down2 = send(second)
    later, _ = lax.optimization_barrier((later, second))
    own, mid = lax.optimization_barrier((owns(later, parts[0]), mids(later, parts[0])))
    third = mid[0] + up1, mid[1] + down1
    up3, down3 = send(third)
    later, _ = lax.optimization_barrier((later, third))
    pairs = zip(firsts(later, parts[1]), seconds(later, parts[1]))
    both = tuple(jnp.concatenate(pair) for pair in pairs)
    up12, down12 = send(both)
    outgoing_a = place_blocks(place, empty, (own[0], down2, up3), (own[1], up2, down3), 30)
    own, mid = owns(later, parts[1]), mids(later, parts[1])
    third = add_pairs(mid[0], up12, mid[1], down12, outgoing_a)
    up3, down3 = send(third)
    outgoing_b = place_blocks(place, empty, (own[0], down12, up3), (own[1], up12, down3))
    spare = spare_room((owners, MOST, slab_rows, side))
    arrived = [
        lax.all_to_all(
            outgoing.reshape(owners, MOST, slab_rows, -1), "fsdp", split_axis=0, concat_axis=0, tiled=True
        )
        for outgoing in (outgoing_a, outgoing_b)
    ]
    results = precondition(
        live, arrived, left_stats, right_stats, left_roots, right_roots, spare
    )
    returned = lax.all_to_all(results, "fsdp", split_axis=0, concat_axis=0, tiled=True)
    left_out, right_out, left_new, right_new = update_stats(live, arrived, left_stats, right_stats)
    preconditioned = assemble(place, returned.reshape(owners * MOST, slab_rows, side))
    return (
        preconditioned,
        left_out,
        right_out,
        left_new,
        right_new,
    )


def solution(mesh):
    in_specs = (
        P("rep", None, "fsdp", None),
        P(),
        P("rep", "fsdp", None, None, None),
        P("rep", "fsdp", None, None, None),
        P("rep", "fsdp", None, None, None),
        P("rep", "fsdp", None, None, None),
    )
    out_specs = (
        P("rep", "fsdp", None),
        P("rep", "fsdp", None, None, None),
        P("rep", "fsdp", None, None, None),
        P("rep", "fsdp", None, None),
        P("rep", "fsdp", None, None),
    )
    return jax.shard_map(
        on_device, mesh=mesh, in_specs=in_specs, out_specs=out_specs, check_vma=False
    )
```
